128 devices in a mesh: blk: 16 (over x_hi, z, core), head: 8 (over y, x_lo).
Axes of the slice: x: 4 (x_hi: 2, x_lo: 2; x = x_hi * 2 + x_lo), y: 4, z: 4, core: 2. Of those that a mesh axis runs over, the one named last changes fastest.
Arguments:
- queries: bfloat16 [1024, 8192], P('blk', 'head'), may hold values from -20 to 20
- question_keys: bfloat16 [1024, 1024], P('blk', 'head'), may hold values from -40 to 40
- question_values: bfloat16 [1024, 1024], P('blk', 'head'), may hold values from -6 to 6
- question_ids: int32 [1024], P('blk'), may hold values from 0 to 1023, as said below
- live_rows: int32 [16], P('blk'), may hold values from 16 to 64, as said below
- prefix_keys: bfloat16 [32768, 1024], P('blk', 'head'), may hold values from -40 to 40
- prefix_values: bfloat16 [32768, 1024], P('blk', 'head'), may hold values from -6 to 6
- out_weight: bfloat16 [8192, 8192], P('head', 'blk'), may hold values from -0.0625 to 0.0625
Outputs:
- projected: bfloat16 [1024, 8192], P('head', 'blk')
The draws below stay inside these ranges and needn't reach their ends.
Inputs may be any that keep to these rules, and one draw needn't show every extreme that they name: `question_ids`: each question lies inside the 64 row slots of one owner; a row's id is the index of its question's first row slot, so ids never fall along the rows; the last row slot of all is a question of one row. `live_rows`: counts of live question rows per owner; one owner has all 64 slots live and another only 16.
All inputs are finite; a program needn't handle non-finite values.
Results may differ from the reference program's by a relative error of at most 0.0048.
Values may be sent and summed in bfloat16 or wider, within the bound.
No kernel may reach another device: no remote copies, remote signals or barrier semaphores. Data moves between devices by JAX's collectives and lax.ppermute only.
A program may use at most 64 MiB of HBM per device.

```python
import math
import jax
import jax.numpy as jnp
from jax import lax

HQ = 64
KVH = 8
DH = 128
D = 8192
P_DEV = 2048
Q_DEV = 64
TOKENS = 1024
PREFIX = 32768
N_BLK = 16


def shared_base(key):
    return jnp.clip(jax.random.normal(key, (TOKENS, HQ * DH), jnp.float32), -5.0, 5.0)


def grouped_base(base):
    return base.reshape(TOKENS, KVH, HQ // KVH, DH).mean(axis=2).reshape(TOKENS, KVH * DH)


def aim_factor():
    target = math.log(PREFIX) + 4.0
    return min(target * (HQ // KVH) / (1.5 * math.sqrt(DH)), 7.0)


def draw_queries(key, part):
    base = shared_base(key)
    return (1.5 * base).astype(jnp.bfloat16)


def draw_question_keys(key, part):
    base = shared_base(key)
    key = jax.random.fold_in(key, 12)
    grouped = grouped_base(base) * aim_factor()
    noise = jnp.clip(jax.random.normal(key, (TOKENS, KVH * DH), jnp.float32), -5.0, 5.0)
    return (grouped + noise).astype(jnp.bfloat16)


def draw_prefix_keys(key, part):
    key = jax.random.fold_in(key, 13)
    noise = jnp.clip(jax.random.normal(key, (PREFIX, KVH * DH), jnp.float32), -5.0, 5.0)
    values = 2.0 * noise
    return values.astype(jnp.bfloat16)


def draw_question_ids(key, part):
    key = jax.random.fold_in(key, 14)
    row_index = jnp.arange(TOKENS, dtype=jnp.int32)
    starts = jax.random.randint(key, (TOKENS,), 0, 4) == 0
    starts = starts | (row_index % Q_DEV == 0) | (row_index == TOKENS - 1)
    marked = jnp.where(starts, row_index, 0).astype(jnp.int32)
    return lax.cummax(marked, axis=0).astype(jnp.int32)


def draw_live_rows(key, part):
    key = jax.random.fold_in(key, 15)
    owners = TOKENS // Q_DEV
    counts = jax.random.randint(key, (owners,), Q_DEV // 4, Q_DEV + 1)
    order = jax.random.permutation(jax.random.fold_in(key, 1), owners)
    counts = counts.at[order[0]].set(Q_DEV)
    counts = counts.at[order[1]].set(Q_DEV // 4)
    return counts.astype(jnp.int32)


def levels(own_key, extent, shards, low, largest):
    loudness = 1.0
    for axis_at, parts in shards:
        steps = jax.random.uniform(jax.random.fold_in(jax.random.fold_in(own_key, 6), axis_at), (parts,), jnp.float32, low / len(shards), largest / len(shards))
        loudness = loudness * jnp.repeat(jnp.exp(steps), extent[axis_at] // parts).reshape((-1,) + (1,) * (len(extent) - 1 - axis_at))
    return loudness


def normal_values(rng, extent, deviation, most, shards=(), kind=jnp.bfloat16):
    drawn = jax.random.normal(rng, extent, jnp.float32) * deviation
    if len(shards) > 0:
        drawn = levels(rng, extent, shards, -0.22, 0.18) * drawn
    return jnp.clip(drawn, min=-most, max=most).astype(kind)


def setup_inputs(seed: int = 0) -> dict:
    seeds = jax.random.split(jax.random.key(seed), 9)
    queries = draw_queries(jax.random.fold_in(seeds[8], 71), 0)
    question_keys = draw_question_keys(jax.random.fold_in(seeds[8], 71), 0)
    question_values = normal_values(seeds[2], (TOKENS, KVH * DH), 1.0, 6.0, ((0, 16), (1, 8)))
    question_ids = draw_question_ids(jax.random.fold_in(seeds[8], 71), 0)
    live_rows = draw_live_rows(jax.random.fold_in(seeds[8], 71), 0)
    prefix_keys = draw_prefix_keys(jax.random.fold_in(seeds[8], 71), 0)
    prefix_values = normal_values(seeds[6], (PREFIX, KVH * DH), 1.0, 6.0, ((0, 16), (1, 8)))
    out_weight = normal_values(seeds[7], (HQ * DH, D), (HQ * DH) ** -0.5, 0.0625, ((0, 8), (1, 16)))
    return dict(queries=queries, question_keys=question_keys, question_values=question_values, question_ids=question_ids, live_rows=live_rows, prefix_keys=prefix_keys, prefix_values=prefix_values, out_weight=out_weight)


floor_score = -1.0e30


def merge_parts(former, latter):
    highest = jnp.maximum(former[0], latter[0])
    first_scale = jnp.exp(former[0] - highest)
    second_scale = jnp.exp(latter[0] - highest)
    totals = first_scale * former[1] + second_scale * latter[1]
    summed = first_scale[..., None] * former[2] + second_scale[..., None] * latter[2]
    return highest, totals, summed


def partials(query_rows, key_rows, value_rows, allowed):
    positions = key_rows.shape[0]
    kv_heads = query_rows.shape[1]
    query_heads = jnp.transpose(query_rows, (1, 0, 2, 3))
    key_heads = jnp.transpose(key_rows.reshape(positions, kv_heads, DH), (1, 0, 2))
    value_heads = jnp.transpose(value_rows.reshape(positions, kv_heads, DH), (1, 0, 2))

    def per_head(block_pair):
        query_one, key_one, value_one = block_pair
        scores = jnp.einsum('tgd,pd->gtp', query_one.astype(jnp.float32), key_one.astype(jnp.float32), precision=lax.Precision.HIGHEST) * (DH ** -0.5)
        if allowed is not None:
            scores = jnp.where(allowed[None, :, :], scores, floor_score)
        highest = jnp.max(scores, axis=-1)
        weights = jnp.exp(scores - highest[..., None]).astype(jnp.bfloat16)
        totals = jnp.sum(weights, axis=-1, dtype=jnp.float32)
        summed = jnp.einsum('gtp,pd->gtd', weights.astype(jnp.float32), value_one.astype(jnp.float32), precision=lax.Precision.HIGHEST)
        return highest, totals, summed

    return lax.map(per_head, (query_heads, key_heads, value_heads))


def reference(queries, question_keys, question_values, question_ids, live_rows, prefix_keys, prefix_values, out_weight):
    query_rows = queries.reshape(TOKENS, KVH, HQ // KVH, DH)
    row_index = jnp.arange(TOKENS, dtype=jnp.int32)
    allowed = (question_ids[:, None] == question_ids[None, :]) & (row_index[None, :] <= row_index[:, None])
    own_part = partials(query_rows, question_keys, question_values, allowed)
    key_blocks = prefix_keys.reshape(N_BLK, P_DEV, KVH * DH)
    value_blocks = prefix_values.reshape(N_BLK, P_DEV, KVH * DH)

    def advance(running, block_pair):
        return merge_parts(running, partials(query_rows, block_pair[0], block_pair[1], None)), None

    combined, _ = lax.scan(advance, own_part, (key_blocks, value_blocks))
    attention = combined[2] / combined[1][..., None]
    attention = jnp.transpose(attention, (2, 0, 1, 3)).reshape(TOKENS, HQ * DH)
    live_mask = (row_index % Q_DEV) < live_rows[row_index // Q_DEV]
    attention = jnp.where(live_mask[:, None], attention, 0.0).astype(jnp.bfloat16)
    return jnp.dot(attention, out_weight, preferred_element_type=jnp.float32).astype(jnp.bfloat16)
```

```python
import functools

import jax
import jax.numpy as jnp
from jax import lax
from jax.experimental import pallas as pl
from jax.experimental.pallas import tpu as pltpu
from jax.sharding import PartitionSpec as P

DH = 128
GROUP = 8
ROWS = 64
LANES = GROUP * ROWS
EXTRA = 16
SCALE = DH**-0.5 * 1.4426950408889634
FLOOR = -1e30
CHUNK = 512
XH, Z, CORE = 2, 4, 2
VMEM_LIMIT = 50 << 20


def moved(array, xh=0, z=0, c=0):
    pairs = []
    for i in range(XH * Z * CORE):
        a, b, d = i // (Z * CORE), (i // CORE) % Z, i % CORE
        to = (((a + xh) % XH) * Z + (b + z) % Z) * CORE + (d + c) % CORE
        pairs.append((i, to))
    return lax.ppermute(array, "blk", pairs)


def scores_of(keys, queries):
    return lax.dot_general(
        keys, queries, (((1,), (1,)), ((), ())), preferred_element_type=jnp.float32
    )


def with_ones(values):
    return jnp.concatenate(
        [values.T, jnp.ones((EXTRA, values.shape[0]), values.dtype)], axis=0
    )


def add_block(top, total, scores, values):
    best = jnp.maximum(top, jnp.max(scores, axis=0, keepdims=True) * SCALE)
    weights = jnp.exp2(scores * SCALE - best).astype(jnp.bfloat16)
    part = jnp.dot(values, weights, preferred_element_type=jnp.float32)
    return best, total * jnp.exp2(top - best) + part


def add_keys(queries, top, total, key_refs, value_scratch):
    chunks = []
    for block, key_ref in enumerate(key_refs):
        for at in range(0, key_ref.shape[0], CHUNK):
            chunks.append((block, key_ref, at))

    def scores_at(i):
        _, key_ref, at = chunks[i]
        return scores_of(key_ref[at : at + CHUNK, :], queries)

    ahead = scores_at(0)
    for i, (block, _, at) in enumerate(chunks):
        scores = ahead
        if i + 1 < len(chunks):
            ahead = scores_at(i + 1)
        top, total = add_block(top, total, scores, value_scratch[block, :, at : at + CHUNK])
    return top, total


def first_kernel(q0, q1, q2, q3, qk, qv, bias, ka, va, kb, vb, rows_ref, top_ref, total_ref, vt):
    for owner, ref in enumerate((q0, q1, q2, q3)):
        for head in range(GROUP):
            rows_ref[owner, head * ROWS : (head + 1) * ROWS, :] = ref[:, head * DH : (head + 1) * DH]
    vt[0] = with_ones(va[...])
    vt[1] = with_ones(vb[...])
    own = scores_of(qk[...], rows_ref[0]) + bias[...]
    top, total = add_block(
        jnp.full((1, LANES), FLOOR, jnp.float32),
        jnp.zeros((DH + EXTRA, LANES), jnp.float32),
        own,
        with_ones(qv[...]),
    )
    top_ref[...] = jnp.full(top_ref.shape, FLOOR, jnp.float32)
    total_ref[...] = jnp.zeros(total_ref.shape, jnp.float32)
    top_ref[0] = jnp.broadcast_to(top, (8, LANES))
    total_ref[0] = total

    def owner_step(owner, _):
        top, total = add_keys(rows_ref[owner], top_ref[owner, :1], total_ref[owner], (ka, kb), vt)
        top_ref[owner] = jnp.broadcast_to(top, (8, LANES))
        total_ref[owner] = total
        return 0

    lax.fori_loop(0, 4, owner_step, 0)


def second_kernel(rows, top_in, total_in, ka, va, kb, vb, own_top, own_total, p1, p2, p3, vt, out):
    vt[0] = with_ones(va[...])
    vt[1] = with_ones(vb[...])

    def owner_step(owner, _):
        top, total = add_keys(rows[owner], top_in[owner, :1], total_in[owner], (ka, kb), vt)

        @pl.when(owner == 0)
        def _():
            own_top[...] = jnp.broadcast_to(top, (8, LANES))
            own_total[...] = total

        denominator = total[DH : DH + 1]
        out[owner, :DH, :] = (total[:DH] * (1.0 / denominator)).astype(jnp.bfloat16)
        level = top + jnp.log2(denominator)
        high = level.astype(jnp.bfloat16)
        rest = level - high.astype(jnp.float32)
        mid = rest.astype(jnp.bfloat16)
        low = (rest - mid.astype(jnp.float32)).astype(jnp.bfloat16)
        row = lax.broadcasted_iota(jnp.int32, (EXTRA, LANES), 0)
        pieces = jnp.where(
            row == 0,
            high.astype(jnp.float32),
            jnp.where(row == 1, mid.astype(jnp.float32), low.astype(jnp.float32)),
        )
        out[owner, DH:, :] = pieces.astype(jnp.bfloat16)
        return 0

    lax.fori_loop(0, 4, owner_step, 0)
    p1[...] = out[1]
    p2[...] = out[2]
    p3[...] = out[3]


def merge_kernel(top, total, r1, r2, r3, live, att):
    parts = []
    best = top[:1]
    for ref in (r1, r2, r3):
        pieces = ref[DH:, :].astype(jnp.float32)
        level = (pieces[0:1] + pieces[1:2]) + pieces[2:3]
        parts.append((level, ref))
        best = jnp.maximum(best, level)
    own = jnp.exp2(top[:1] - best)
    numerator = total[:DH] * own
    denominator = total[DH : DH + 1] * own
    for level, ref in parts:
        share = jnp.exp2(level - best)
        numerator = numerator + ref[:DH, :].astype(jnp.float32) * share
        denominator = denominator + share
    result = jnp.where(live[:1] > 0.0, numerator / denominator, 0.0)
    result = result.T.astype(jnp.bfloat16)
    for head in range(GROUP):
        att[:, head * DH : (head + 1) * DH] = result[head * ROWS : (head + 1) * ROWS, :]


def project_kernel(slots, a0, a1, a2, a3, a4, a5, a6, a7, wa, wb, out, rows):
    for i, ref in enumerate((a0, a1, a2, a3, a4, a5, a6, a7)):
        rows[i * ROWS : (i + 1) * ROWS, :] = ref[...]
    width = wa.shape[1]
    for side, w in enumerate((wa, wb)):
        terms = jnp.dot(rows[...], w[...], preferred_element_type=jnp.float32).astype(jnp.bfloat16)
        for i in range(8):
            out[slots[i], :, side * width : (side + 1) * width] = terms[i * ROWS : (i + 1) * ROWS, :]


def sum_kernel(terms, mine, other, *, width):
    acc = terms[0].astype(jnp.float32)
    for i in range(1, terms.shape[0]):
        acc = acc + terms[i].astype(jnp.float32)
    acc = acc.astype(jnp.bfloat16)
    mine[...] = acc[:, :width]
    other[...] = acc[:, width:]


def call(kernel, outs, scratch=(), **kwargs):
    return pl.pallas_call(
        kernel,
        out_shape=tuple(jax.ShapeDtypeStruct(s, d) for s, d in outs),
        scratch_shapes=list(scratch),
        compiler_params=pltpu.CompilerParams(vmem_limit_bytes=VMEM_LIMIT),
        **kwargs,
    )


def shards(
    queries,
    question_keys,
    question_values,
    question_ids,
    live_rows,
    prefix_keys,
    prefix_values,
    out_weight,
):
    f32, bf16 = jnp.float32, jnp.bfloat16
    index = lax.axis_index("blk")
    core = index % CORE
    positions = prefix_keys.shape[0]

    keys_c = moved(prefix_keys, c=1)
    values_c = moved(prefix_values, c=1)
    q_up = moved(queries, z=1)
    q_down = moved(queries, z=-1)
    q_far = moved(queries, z=2)
    keys_x = moved(prefix_keys, xh=1)
    values_x = moved(prefix_values, xh=1)
    weight_c = moved(out_weight, c=1)

    row = jnp.arange(ROWS, dtype=jnp.int32)
    allowed = (question_ids[:, None] == question_ids[None, :]) & (row[:, None] <= row[None, :])
    bias = jnp.tile(jnp.where(allowed, 0.0, FLOOR).astype(f32), (1, GROUP))
    live = jnp.tile((row < live_rows[0]).astype(f32)[None, :], (8, GROUP))

    state = (DH + EXTRA, LANES)
    vt = pltpu.VMEM((2, DH + EXTRA, positions), bf16)
    rows, top, total = call(
        first_kernel,
        [((4, LANES, DH), bf16), ((4, 8, LANES), f32), ((4,) + state, f32)],
        [vt],
    )(
        queries, q_up, q_down, q_far, question_keys, question_values, bias,
        prefix_keys, prefix_values, keys_c, values_c,
    )
    keys_xc = moved(keys_x, c=1)
    values_xc = moved(values_x, c=1)
    own_top, own_total, p_up, p_down, p_far = call(
        second_kernel,
        [((8, LANES), f32), (state, f32), (state, bf16), (state, bf16), (state, bf16)],
        [vt, pltpu.VMEM((4,) + state, bf16)],
    )(rows, top, total, keys_x, values_x, keys_xc, values_xc)
    r_down = moved(p_up, z=-1)
    r_up = moved(p_down, z=1)
    r_far = moved(p_far, z=2)
    (att,) = call(merge_kernel, [((ROWS, GROUP * DH), bf16)])(
        own_top, own_total, r_down, r_up, r_far, live
    )

    att_x = moved(att, xh=1)
    held = {(0, 0): att, (1, 0): att_x}
    for z in (1, 3, 2):
        held[(0, z)] = moved(att, z=z)
    for z in (1, 3, 2):
        held[(1, z)] = moved(att_x, z=z)
    xh_at, z_at = index // (Z * CORE), (index // CORE) % Z
    order = [(dx, dz) for dx in range(XH) for dz in range(Z)]
    width = out_weight.shape[1]
    slots = jnp.stack([((xh_at - dx) % XH) * Z + (z_at - dz) % Z for dx, dz in order])
    vmem = pl.BlockSpec(memory_space=pltpu.VMEM)
    (terms,) = call(
        project_kernel,
        [((8, ROWS, CORE * width), bf16)],
        [pltpu.VMEM((8 * ROWS, GROUP * DH), bf16)],
        in_specs=[pl.BlockSpec(memory_space=pltpu.SMEM)] + [vmem] * 10,
    )(slots, *[held[o] for o in order], out_weight, weight_c)
    gathered = lax.all_to_all(terms, "head", 0, 0, tiled=True)
    mine, other = call(
        functools.partial(sum_kernel, width=width),
        [((ROWS, width), bf16), ((ROWS, width), bf16)],
    )(gathered)
    theirs = moved(other, c=1)
    return jnp.where(
        core == 0,
        jnp.concatenate([mine, theirs], axis=0),
        jnp.concatenate([theirs, mine], axis=0),
    )


def solution(mesh):
    return jax.shard_map(
        shards,
        mesh=mesh,
        in_specs=(
            P("blk", "head"),
            P("blk", "head"),
            P("blk", "head"),
            P("blk"),
            P("blk"),
            P("blk", "head"),
            P("blk", "head"),
            P("head", "blk"),
        ),
        out_specs=P("head", "blk"),
        check_vma=False,
    )
```

```python
import functools

import jax
import jax.numpy as jnp
from jax import lax
from jax.experimental import pallas as pl
from jax.experimental.pallas import tpu as pltpu
from jax.sharding import PartitionSpec as P

DH = 128
GROUP = 8
ROWS = 64
LANES = GROUP * ROWS
EXTRA = 16
SCALE = DH**-0.5 * 1.4426950408889634
FLOOR = -1e30
DEAD = 1e30
XH, Z, CORE = 2, 4, 2
VMEM_LIMIT = 50 << 20
FAR = (1, 3, 2)


def moved(array, xh=0, z=0, c=0):
    pairs = []
    for i in range(XH * Z * CORE):
        a, b, d = i // (Z * CORE), (i // CORE) % Z, i % CORE
        to = (((a + xh) % XH) * Z + (b + z) % Z) * CORE + (d + c) % CORE
        pairs.append((i, to))
    return lax.ppermute(array, "blk", pairs)


def after(array, *others):
    return lax.optimization_barrier((array, *others))[0]


def scores_of(queries, keys):
    return lax.dot_general(
        queries, keys, (((1,), (1,)), ((), ())), preferred_element_type=jnp.float32
    )


def wide(column, width):
    return jnp.concatenate([column] * (width // column.shape[1]), axis=1)


def add_block(top, total, scores, values):
    best = jnp.maximum(top, jnp.max(scores, axis=1, keepdims=True) * SCALE)
    keys = scores.shape[1]
    at = wide(best, keys) if keys >= DH else best[:, :keys]
    weights = jnp.exp2(scores * SCALE - at).astype(jnp.bfloat16)
    part = jnp.dot(weights, values, preferred_element_type=jnp.float32)
    return best, total * wide(jnp.exp2(top - best), 2 * DH) + part


def stacked(ref):
    return jnp.concatenate([ref[:, h * DH : (h + 1) * DH] for h in range(GROUP)], axis=0)


def fetch(refs, scratch, sems):
    keys, values = scratch
    copies = []
    for i, (key_ref, value_ref) in enumerate(refs):
        copies.append(pltpu.make_async_copy(key_ref, keys.at[i], sems.at[2 * i]))
        copies.append(
            pltpu.make_async_copy(value_ref, values.at[i, :, pl.ds(0, DH)], sems.at[2 * i + 1])
        )
    for copy in copies:
        copy.start()
    values[:, :, DH:] = jnp.ones(values.shape[:2] + (DH,), values.dtype)
    return copies


def finish(top, total):
    denominator = total[:, DH:]
    result = (total[:, :DH] / denominator).T
    level = (top + jnp.log2(denominator)).T[:1]
    return result, level


def packed(result, level):
    high = level.astype(jnp.bfloat16).astype(jnp.float32)
    mid = (level - high).astype(jnp.bfloat16).astype(jnp.float32)
    low = level - high - mid
    row = lax.broadcasted_iota(jnp.int32, (EXTRA, LANES), 0)
    pieces = jnp.where(row == 0, high, jnp.where(row == 1, mid, low))
    return jnp.concatenate([result, pieces], axis=0).astype(jnp.bfloat16)


def unpacked(block):
    pieces = block[DH:, :].astype(jnp.float32)
    return block[:DH, :].astype(jnp.float32), (pieces[0:1] + pieces[1:2]) + pieces[2:3]


def merged(parts):
    best = functools.reduce(jnp.maximum, [level for _, level in parts])
    numerator, denominator = 0.0, 0.0
    for result, level in parts:
        share = jnp.exp2(level - best)
        numerator = numerator + result * share
        denominator = denominator + share
    return numerator / denominator, best + jnp.log2(denominator)


def own_kernel(q, qk, qv, bias, k, v, top_ref, total_ref, keys, values, sems):
    copies = fetch([(k, v)], (keys, values), sems)
    rows = stacked(q)
    scores = scores_of(rows, qk[...]) + jnp.concatenate([bias[...]] * GROUP, axis=0)
    top, total = add_block(
        jnp.full((LANES, DH), FLOOR, jnp.float32),
        jnp.zeros((LANES, 2 * DH), jnp.float32),
        scores,
        jnp.concatenate([qv[...], jnp.ones((ROWS, DH), jnp.bfloat16)], axis=1),
    )
    for copy in copies:
        copy.wait()
    top, total = add_block(top, total, scores_of(rows, keys[0]), values[0])
    top_ref[...] = top
    total_ref[...] = total


def others_kernel(q0, q1, q2, ka, va, kb, vb, out, keys, values, rows, sems):
    copies = fetch([(ka, va), (kb, vb)], (keys, values), sems)
    for i, ref in enumerate((q0, q1, q2)):
        rows[i] = stacked(ref)
    for copy in copies:
        copy.wait()

    def step(i, _):
        top = jnp.full((LANES, DH), FLOOR, jnp.float32)
        total = jnp.zeros((LANES, 2 * DH), jnp.float32)
        for block in range(2):
            top, total = add_block(top, total, scores_of(rows[i], keys[block]), values[block])
        out[i] = packed(*finish(top, total))
        return 0

    lax.fori_loop(0, 3, step, 0)


def pair_kernel(q0, q1, q2, first, ka, va, kb, vb, p0, p1, p2, keys, values, rows, out, sems):
    others_kernel(q0, q1, q2, ka, va, kb, vb, out, keys, values, rows, sems)
    for i, ref in enumerate((p0, p1, p2)):
        ref[0] = first[i]
        ref[1] = out[i]


def near_kernel(live, q, qx, top_in, total_in, ka, va, kb, vb, result_ref, level_ref, keys, values, sems):
    copies = fetch([(ka, va), (kb, vb)], (keys, values), sems)
    own, far = stacked(q), stacked(qx)
    for copy in copies:
        copy.wait()
    top, total = add_block(top_in[...], total_in[...], scores_of(own, keys[1]), values[1])
    result, level = finish(top, total)
    slot = lax.broadcasted_iota(jnp.int32, (1, LANES), 1) % ROWS
    alive = slot < live[0]
    result_ref[0] = jnp.where(alive, result, 0.0)
    level_ref[0] = jnp.broadcast_to(jnp.where(alive, level, DEAD), (8, LANES))
    top = jnp.full((LANES, DH), FLOOR, jnp.float32)
    total = jnp.zeros((LANES, 2 * DH), jnp.float32)
    for block in range(2):
        top, total = add_block(top, total, scores_of(far, keys[block]), values[block])
    result, level = finish(top, total)
    result_ref[1] = result
    level_ref[1] = jnp.broadcast_to(level, (8, LANES))


def merge_z_kernel(result, level, r0, r1, r2, result_ref, level_ref, out):
    for i in range(2):
        parts = [(result[i], level[i, :1])] + [unpacked(r[i]) for r in (r0, r1, r2)]
        whole, height = merged(parts)
        result_ref[i] = whole
        level_ref[i] = jnp.broadcast_to(height, (8, LANES))
        out[i] = packed(whole, height)


def merge_x_kernel(result, level, other, att):
    for i in range(2):
        whole, _ = merged([(result[i], level[i, :1]), unpacked(other[1 - i])])
        rows = whole.T.astype(jnp.bfloat16)
        for head in range(GROUP):
            att[i, :, head * DH : (head + 1) * DH] = rows[head * ROWS : (head + 1) * ROWS, :]


def project_kernel(index, a0, a1, a2, a3, wa, wb, out, rows):
    for i, ref in enumerate((a0, a1, a2, a3)):
        for j in range(2):
            rows[(2 * i + j) * ROWS : (2 * i + j + 1) * ROWS, :] = ref[j]
    width = wa.shape[1]
    xh, z = index[0] // (Z * CORE), (index[0] // CORE) % Z
    slots = [((xh + dx) % XH) * Z + (z + Z - dz) % Z for dz in (0,) + FAR for dx in range(XH)]
    for side, w in enumerate((wa, wb)):
        terms = jnp.dot(rows[...], w[...], preferred_element_type=jnp.float32).astype(jnp.bfloat16)
        for i in range(8):
            out[slots[i], :, side * width : (side + 1) * width] = terms[i * ROWS : (i + 1) * ROWS, :]


def sum_kernel(terms, mine, other, *, width):
    acc = terms[0].astype(jnp.float32)
    for i in range(1, terms.shape[0]):
        acc = acc + terms[i].astype(jnp.float32)
    acc = acc.astype(jnp.bfloat16)
    mine[...] = acc[:, :width]
    other[...] = acc[:, width:]


def call(kernel, outs, scratch=(), flops=0, **kwargs):
    return pl.pallas_call(
        kernel,
        out_shape=tuple(jax.ShapeDtypeStruct(s, d) for s, d in outs),
        scratch_shapes=list(scratch),
        compiler_params=pltpu.CompilerParams(vmem_limit_bytes=VMEM_LIMIT),
        cost_estimate=pl.CostEstimate(flops=flops, bytes_accessed=1 << 20, transcendentals=0),
        **kwargs,
    )


def shards(
    queries,
    question_keys,
    question_values,
    question_ids,
    live_rows,
    prefix_keys,
    prefix_values,
    out_weight,
):
    f32, bf16 = jnp.float32, jnp.bfloat16
    index = lax.axis_index("blk")
    core = index % CORE
    positions = prefix_keys.shape[0]
    vmem = pl.BlockSpec(memory_space=pltpu.VMEM)
    smem = pl.BlockSpec(memory_space=pltpu.SMEM)
    hbm = pl.BlockSpec(memory_space=pl.ANY)
    owner_flops = 8 * LANES * positions * DH

    def kv_scratch(blocks):
        return [
            pltpu.VMEM((blocks, positions, DH), bf16),
            pltpu.VMEM((blocks, positions, 2 * DH), bf16),
        ]

    q_x = moved(queries, xh=1)
    q_z = [moved(queries, z=z) for z in FAR]
    keys_c = moved(prefix_keys, c=1)
    values_c = moved(prefix_values, c=1)

    row = jnp.arange(ROWS, dtype=jnp.int32)
    allowed = (question_ids[:, None] == question_ids[None, :]) & (row[None, :] <= row[:, None])
    bias = jnp.where(allowed, 0.0, FLOOR).astype(f32)
    top, total = call(
        own_kernel,
        [((LANES, DH), f32), ((LANES, 2 * DH), f32)],
        kv_scratch(1) + [pltpu.SemaphoreType.DMA((2,))],
        flops=owner_flops,
        in_specs=[vmem] * 4 + [hbm] * 2,
    )(queries, question_keys, question_values, bias, prefix_keys, prefix_values)

    q_xz = [moved(q_x, z=z) for z in FAR]
    part = (DH + EXTRA, LANES)
    rows = pltpu.VMEM((3, LANES, DH), bf16)
    sems = pltpu.SemaphoreType.DMA((4,))
    kv = (prefix_keys, prefix_values, keys_c, values_c)
    q_z[0] = after(q_z[0], q_x)
    (first,) = call(
        others_kernel,
        [((3,) + part, bf16)],
        kv_scratch(2) + [rows, sems],
        flops=6 * owner_flops,
        in_specs=[vmem] * 3 + [hbm] * 4,
    )(*q_z, *kv)
    pairs = call(
        pair_kernel,
        [((2,) + part, bf16)] * 3,
        kv_scratch(2) + [rows, pltpu.VMEM((3,) + part, bf16), sems],
        flops=6 * owner_flops,
        in_specs=[vmem] * 4 + [hbm] * 4,
    )(*q_xz, first, *kv)
    back = [moved(pair, z=-z) for pair, z in zip(pairs, FAR)]
    result, level = call(
        near_kernel,
        [((2, DH, LANES), f32), ((2, 8, LANES), f32)],
        kv_scratch(2) + [sems],
        flops=3 * owner_flops,
        in_specs=[smem] + [vmem] * 4 + [hbm] * 4,
    )(live_rows, queries, after(q_x, *pairs), top, total, *kv)
    result, level, pair = call(
        merge_z_kernel,
        [((2, DH, LANES), f32), ((2, 8, LANES), f32), ((2,) + part, bf16)],
    )(result, level, *back)
    (att,) = call(merge_x_kernel, [((2, ROWS, GROUP * DH), bf16)])(
        result, level, moved(pair, xh=1)
    )

    weight_c = moved(after(out_weight, top), c=1)
    held = [att] + [moved(att, z=z) for z in FAR]
    width = out_weight.shape[1]
    (terms,) = call(
        project_kernel,
        [((8, ROWS, CORE * width), bf16)],
        [pltpu.VMEM((8 * ROWS, GROUP * DH), bf16)],
        in_specs=[smem] + [vmem] * 6,
    )(index.reshape(1), *held, out_weight, weight_c)
    gathered = lax.all_to_all(terms, "head", 0, 0, tiled=True)
    mine, other = call(
        functools.partial(sum_kernel, width=width),
        [((ROWS, width), bf16), ((ROWS, width), bf16)],
    )(gathered)
    theirs = moved(other, c=1)
    return jnp.where(
        core == 0,
        jnp.concatenate([mine, theirs], axis=0),
        jnp.concatenate([theirs, mine], axis=0),
    )


def solution(mesh):
    return jax.shard_map(
        shards,
        mesh=mesh,
        in_specs=(
            P("blk", "head"),
            P("blk", "head"),
            P("blk", "head"),
            P("blk"),
            P("blk"),
            P("blk", "head"),
            P("blk", "head"),
            P("head", "blk"),
        ),
        out_specs=P("head", "blk"),
        check_vma=False,
    )
```

```python
import functools

import jax
import jax.numpy as jnp
from jax import lax
from jax.experimental import pallas as pl
from jax.experimental.pallas import tpu as pltpu
from jax.sharding import PartitionSpec as P

DH = 128
GROUP = 8
ROWS = 64
LANES = GROUP * ROWS
EXTRA = 16
SCALE = DH**-0.5 * 1.4426950408889634
FLOOR = -1e30
XH, Z, CORE = 2, 4, 2
VMEM_LIMIT = 30 << 20
FAR = (1, 3, 2)


def moved(array, xh=0, z=0, c=0):
    pairs = []
    for i in range(XH * Z * CORE):
        a, b, d = i // (Z * CORE), (i // CORE) % Z, i % CORE
        to = (((a + xh) % XH) * Z + (b + z) % Z) * CORE + (d + c) % CORE
        pairs.append((i, to))
    return lax.ppermute(array, "blk", pairs)


def after(array, *others):
    return lax.optimization_barrier((array, *others))[0]


def scores_of(queries, keys):
    return lax.dot_general(
        queries, keys, (((1,), (1,)), ((), ())), preferred_element_type=jnp.float32
    )


def wide(column, width):
    return jnp.concatenate([column] * (width // column.shape[1]), axis=1)


def add_block(top, total, scores, values):
    best = jnp.maximum(top, jnp.max(scores, axis=1, keepdims=True) * SCALE)
    keys = scores.shape[1]
    at = wide(best, keys) if keys >= DH else best[:, :keys]
    weights = jnp.exp2(scores * SCALE - at).astype(jnp.bfloat16)
    part = jnp.dot(weights, values, preferred_element_type=jnp.float32)
    return best, total * wide(jnp.exp2(top - best), 2 * DH) + part


def stacked(ref):
    return jnp.concatenate([ref[:, h * DH : (h + 1) * DH] for h in range(GROUP)], axis=0)


def with_ones(values, scratch):
    scratch[:, :DH] = values[...]
    scratch[:, DH:] = jnp.ones(values.shape, values.dtype)


def finish(top, total):
    denominator = total[:, DH:]
    result = (total[:, :DH] / denominator).T
    level = (top + jnp.log2(denominator)).T[:1]
    return result, level


def packed(result, level):
    high = level.astype(jnp.bfloat16).astype(jnp.float32)
    mid = (level - high).astype(jnp.bfloat16).astype(jnp.float32)
    low = level - high - mid
    row = lax.broadcasted_iota(jnp.int32, (EXTRA, LANES), 0)
    pieces = jnp.where(row == 0, high, jnp.where(row == 1, mid, low))
    return jnp.concatenate([result, pieces], axis=0).astype(jnp.bfloat16)


def unpacked(block):
    pieces = block[DH:, :].astype(jnp.float32)
    return block[:DH, :].astype(jnp.float32), (pieces[0:1] + pieces[1:2]) + pieces[2:3]


def merged(parts):
    best = functools.reduce(jnp.maximum, [level for _, level in parts])
    numerator, denominator = 0.0, 0.0
    for result, level in parts:
        share = jnp.exp2(level - best)
        numerator = numerator + result * share
        denominator = denominator + share
    return numerator / denominator, best + jnp.log2(denominator)


def near_kernel(
    q0, q1, q2, q, qk, qv, bias, ka, va, kb, vb,
    top_out, total_out, rows, own_q, own_k, own_v, keys, values, sems,
):
    moves = [(q, own_q), (qk, own_k), (qv, own_v), (ka, keys), (va, values.at[0, :, pl.ds(0, DH)])]
    copies = [pltpu.make_async_copy(a, b, sems.at[i]) for i, (a, b) in enumerate(moves)]
    for copy in copies:
        copy.start()
    values[0, :, DH:] = jnp.ones(vb.shape, vb.dtype)
    with_ones(vb, values.at[1])
    for i, ref in enumerate((q0, q1, q2)):
        rows[i] = stacked(ref)
    for copy in copies:
        copy.wait()
    rows[3] = stacked(own_q)
    top_out[...] = jnp.full(top_out.shape, FLOOR, jnp.float32)
    total_out[...] = jnp.zeros(total_out.shape, jnp.float32)
    scores = scores_of(rows[3], own_k[...]) + jnp.concatenate([bias[...]] * GROUP, axis=0)
    top_out[3], total_out[3] = add_block(
        top_out[3],
        total_out[3],
        scores,
        jnp.concatenate([own_v[...], jnp.ones((ROWS, DH), jnp.bfloat16)], axis=1),
    )

    def step(i, _):
        first, second = scores_of(rows[i], keys[...]), scores_of(rows[i], kb[...])
        top, total = add_block(top_out[i], total_out[i], first, values[0])
        top_out[i], total_out[i] = add_block(top, total, second, values[1])
        return 0

    lax.fori_loop(0, 4, step, 0)


def far_kernel(rows, top_in, total_in, k, v, top_out, total_out, values):
    with_ones(v, values)

    def step(i, _):
        top, total = add_block(top_in[i], total_in[i], scores_of(rows[i], k[...]), values[...])
        top_out[i] = top
        total_out[i] = total
        return 0

    lax.fori_loop(0, 3, step, 0)


def last_kernel(rows, top_in, total_in, k, v, p0, p1, p2, values, out):
    with_ones(v, values)

    def step(i, _):
        top, total = add_block(top_in[i], total_in[i], scores_of(rows[i], k[...]), values[...])
        out[i] = packed(*finish(top, total))
        return 0

    lax.fori_loop(0, 3, step, 0)
    for i, ref in enumerate((p0, p1, p2)):
        ref[...] = out[i]


def own_last_kernel(rows, top, total, ka, va, kb, vb, result_ref, level_ref, values):
    with_ones(va, values.at[0])
    with_ones(vb, values.at[1])
    first, second = scores_of(rows[3], ka[...]), scores_of(rows[3], kb[...])
    top, total = add_block(top[3], total[3], first, values[0])
    top, total = add_block(top, total, second, values[1])
    result, level = finish(top, total)
    result_ref[...] = result
    level_ref[...] = jnp.broadcast_to(level, (8, LANES))


def merge_kernel(live, result, level, r0, r1, r2, att):
    parts = [(result[...], level[:1])] + [unpacked(r) for r in (r0, r1, r2)]
    whole, _ = merged(parts)
    slot = lax.broadcasted_iota(jnp.int32, (1, LANES), 1) % ROWS
    rows = jnp.where(slot < live[0], whole, 0.0).T.astype(jnp.bfloat16)
    for head in range(GROUP):
        att[:, head * DH : (head + 1) * DH] = rows[head * ROWS : (head + 1) * ROWS, :]


def project_kernel(index, a0, a1, a2, a3, a4, a5, a6, a7, wa, wb, out, rows):
    for i, ref in enumerate((a0, a1, a2, a3, a4, a5, a6, a7)):
        rows[i * ROWS : (i + 1) * ROWS, :] = ref[...]
    width = wa.shape[1]
    xh, z = index[0] // (Z * CORE), (index[0] // CORE) % Z
    slots = [((xh + dx) % XH) * Z + (z + Z - dz) % Z for dx in range(XH) for dz in (0,) + FAR]
    for side, w in enumerate((wa, wb)):
        terms = jnp.dot(rows[...], w[...], preferred_element_type=jnp.float32).astype(jnp.bfloat16)
        for i in range(8):
            out[slots[i], :, side * width : (side + 1) * width] = terms[i * ROWS : (i + 1) * ROWS, :]


def sum_kernel(terms, mine, other, *, width):
    acc = terms[0].astype(jnp.float32)
    for i in range(1, terms.shape[0]):
        acc = acc + terms[i].astype(jnp.float32)
    acc = acc.astype(jnp.bfloat16)
    mine[...] = acc[:, :width]
    other[...] = acc[:, width:]


def call(kernel, outs, scratch=(), flops=0, **kwargs):
    return pl.pallas_call(
        kernel,
        out_shape=tuple(jax.ShapeDtypeStruct(s, d) for s, d in outs),
        scratch_shapes=list(scratch),
        compiler_params=pltpu.CompilerParams(vmem_limit_bytes=VMEM_LIMIT),
        cost_estimate=pl.CostEstimate(flops=flops, bytes_accessed=1 << 20, transcendentals=0),
        **kwargs,
    )


def shards(
    queries,
    question_keys,
    question_values,
    question_ids,
    live_rows,
    prefix_keys,
    prefix_values,
    out_weight,
):
    f32, bf16 = jnp.float32, jnp.bfloat16
    index = lax.axis_index("blk")
    core = index % CORE
    positions = prefix_keys.shape[0]
    vmem = pl.BlockSpec(memory_space=pltpu.VMEM)
    smem = pl.BlockSpec(memory_space=pltpu.SMEM)
    hbm = pl.BlockSpec(memory_space=pltpu.HBM)
    block_flops = 8 * LANES * positions * DH
    part = ((DH + EXTRA, LANES), bf16)
    ones_shape = (positions, 2 * DH)

    def state(owners):
        return [((owners, LANES, DH), f32), ((owners, LANES, 2 * DH), f32)]

    keys_x = moved(prefix_keys, xh=1)
    values_x = moved(prefix_values, xh=1)
    keys_c = moved(prefix_keys, c=1)
    values_c = moved(prefix_values, c=1)
    q_z = [moved(queries, z=z) for z in FAR]
    row = jnp.arange(ROWS, dtype=jnp.int32)
    allowed = (question_ids[:, None] == question_ids[None, :]) & (row[None, :] <= row[:, None])
    bias = jnp.where(allowed, 0.0, FLOOR).astype(f32)
    top, total, rows = call(
        near_kernel,
        state(4) + [((4, LANES, DH), bf16)],
        [
            pltpu.VMEM(queries.shape, bf16),
            pltpu.VMEM(question_keys.shape, bf16),
            pltpu.VMEM(question_keys.shape, bf16),
            pltpu.VMEM((positions, DH), bf16),
            pltpu.VMEM((2,) + ones_shape, bf16),
            pltpu.SemaphoreType.DMA((5,)),
        ],
        flops=block_flops,
        in_specs=[vmem] * 3 + [hbm] * 3 + [vmem] + [hbm] * 2 + [vmem] * 2,
    )(
        *q_z, queries, question_keys, question_values, bias,
        prefix_keys, prefix_values, keys_c, values_c,
    )

    keys_x, values_x, weight, top, total = lax.optimization_barrier(
        (keys_x, values_x, out_weight, top, total)
    )
    keys_xc = moved(keys_x, c=1)
    values_xc = moved(values_x, c=1)
    weight_c = moved(weight, c=1)
    far_top, far_total = call(
        far_kernel, state(3), [pltpu.VMEM(ones_shape, bf16)], flops=3 * block_flops
    )(rows, top, total, keys_x, values_x)
    parts = call(
        last_kernel,
        [part] * 3,
        [pltpu.VMEM(ones_shape, bf16), pltpu.VMEM((3,) + part[0], bf16)],
        flops=3 * block_flops,
    )(rows, far_top, far_total, keys_xc, values_xc)
    back = [moved(p, z=-z) for p, z in zip(parts, FAR)]
    result, level = call(
        own_last_kernel,
        [((DH, LANES), f32), ((8, LANES), f32)],
        [pltpu.VMEM((2,) + ones_shape, bf16)],
        flops=2 * block_flops,
    )(after(rows, *parts), top, total, keys_x, values_x, keys_xc, values_xc)
    (att,) = call(
        merge_kernel, [((ROWS, GROUP * DH), bf16)], in_specs=[smem] + [vmem] * 5
    )(live_rows, result, level, *back)

    att_x = moved(att, xh=1)
    held = [att] + [moved(att, z=z) for z in FAR] + [att_x] + [moved(att_x, z=z) for z in FAR]
    width = out_weight.shape[1]
    (terms,) = call(
        project_kernel,
        [((8, ROWS, CORE * width), bf16)],
        [pltpu.VMEM((8 * ROWS, GROUP * DH), bf16)],
        in_specs=[smem] + [vmem] * 10,
    )(index.reshape(1), *held, out_weight, weight_c)
    gathered = lax.all_to_all(terms, "head", 0, 0, tiled=True)
    mine, other = call(
        functools.partial(sum_kernel, width=width),
        [((ROWS, width), bf16), ((ROWS, width), bf16)],
    )(gathered)
    theirs = moved(other, c=1)
    return jnp.where(
        core == 0,
        jnp.concatenate([mine, theirs], axis=0),
        jnp.concatenate([theirs, mine], axis=0),
    )


def solution(mesh):
    return jax.shard_map(
        shards,
        mesh=mesh,
        in_specs=(
            P("blk", "head"),
            P("blk", "head"),
            P("blk", "head"),
            P("blk"),
            P("blk"),
            P("blk", "head"),
            P("blk", "head"),
            P("head", "blk"),
        ),
        out_specs=P("head", "blk"),
        check_vma=False,
    )
```

```python
import functools

import jax
import jax.numpy as jnp
from jax import lax
from jax.experimental import pallas as pl
from jax.experimental.pallas import tpu as pltpu
from jax.sharding import PartitionSpec as P

DH = 128
GROUP = 8
ROWS = 64
LANES = GROUP * ROWS
EXTRA = 16
SCALE = DH**-0.5 * 1.4426950408889634
FLOOR = -1e30
XH, Z, CORE = 2, 4, 2
VMEM_LIMIT = 30 << 20
FAR = (1, 3, 2)


def moved(array, xh=0, z=0, c=0):
    pairs = []
    for i in range(XH * Z * CORE):
        a, b, d = i // (Z * CORE), (i // CORE) % Z, i % CORE
        to = (((a + xh) % XH) * Z + (b + z) % Z) * CORE + (d + c) % CORE
        pairs.append((i, to))
    return lax.ppermute(array, "blk", pairs)


def after(array, *others):
    return lax.optimization_barrier((array, *others))[0]


def scores_of(queries, keys):
    return lax.dot_general(
        queries, keys, (((1,), (1,)), ((), ())), preferred_element_type=jnp.float32
    )


def wide(column, width):
    return jnp.concatenate([column] * (width // column.shape[1]), axis=1)


def add_block(top, total, scores, values):
    best = jnp.maximum(top, jnp.max(scores, axis=1, keepdims=True) * SCALE)
    keys = scores.shape[1]
    at = wide(best, keys) if keys >= DH else best[:, :keys]
    weights = jnp.exp2(scores * SCALE - at).astype(jnp.bfloat16)
    part = jnp.dot(weights, values, preferred_element_type=jnp.float32)
    return best, total * wide(jnp.exp2(top - best), 2 * DH) + part


def stacked(ref):
    return jnp.concatenate([ref[:, h * DH : (h + 1) * DH] for h in range(GROUP)], axis=0)


def join_kernel(k, v, kv, sems):
    half = k.shape[0]
    part = half // 2
    copies = []
    for i, ref in enumerate((k, v)):
        for j in range(2):
            copies.append(
                pltpu.make_async_copy(
                    ref.at[pl.ds(j * part, part)],
                    kv.at[pl.ds(i * half + j * part, part)],
                    sems.at[2 * i + j],
                )
            )
    for copy in copies:
        copy.start()
    for copy in copies:
        copy.wait()


def split(kv, scratch):
    half = kv.shape[0] // 2
    scratch[:, :DH] = kv[half:, :]
    scratch[:, DH:] = jnp.ones((half, DH), kv.dtype)
    return kv.at[pl.ds(0, half)]


def finish(top, total):
    denominator = total[:, DH:]
    result = (total[:, :DH] / denominator).T
    level = (top + jnp.log2(denominator)).T[:1]
    return result, level


def packed(result, level):
    high = level.astype(jnp.bfloat16).astype(jnp.float32)
    mid = (level - high).astype(jnp.bfloat16).astype(jnp.float32)
    low = level - high - mid
    row = lax.broadcasted_iota(jnp.int32, (EXTRA, LANES), 0)
    pieces = jnp.where(row == 0, high, jnp.where(row == 1, mid, low))
    return jnp.concatenate([result, pieces], axis=0).astype(jnp.bfloat16)


def unpacked(block):
    pieces = block[DH:, :].astype(jnp.float32)
    return block[:DH, :].astype(jnp.float32), (pieces[0:1] + pieces[1:2]) + pieces[2:3]


def merged(parts):
    best = functools.reduce(jnp.maximum, [level for _, level in parts])
    numerator, denominator = 0.0, 0.0
    for result, level in parts:
        share = jnp.exp2(level - best)
        numerator = numerator + result * share
        denominator = denominator + share
    return numerator / denominator, best + jnp.log2(denominator)


def run(tasks, states):
    def scores_at(i):
        _, rows, keys, _ = tasks[i]
        return scores_of(rows[...], keys[...])

    ahead = scores_at(0)
    for i, (owner, _, _, values) in enumerate(tasks):
        scores = ahead
        if i + 1 < len(tasks):
            ahead = scores_at(i + 1)
        states[owner] = add_block(*states[owner], scores, values[...])
    return states


def empty():
    return (
        jnp.full((LANES, DH), FLOOR, jnp.float32),
        jnp.zeros((LANES, 2 * DH), jnp.float32),
    )


def own_kernel(q, qk, qv, bias, kv, top_out, total_out, values):
    k = split(kv, values)
    rows = stacked(q)
    scores = scores_of(rows, qk[...]) + jnp.concatenate([bias[...]] * GROUP, axis=0)
    far = scores_of(rows, k[...])
    top, total = add_block(
        *empty(),
        scores,
        jnp.concatenate([qv[...], jnp.ones((ROWS, DH), jnp.bfloat16)], axis=1),
    )
    top_out[...], total_out[...] = add_block(top, total, far, values[...])


def near_kernel(q0, q1, q2, q, own_top, own_total, kv, top_out, total_out, rows, values):
    k = split(kv, values)
    for i, ref in enumerate((q0, q1, q2, q)):
        rows[i] = stacked(ref)
    states = run([(i, rows.at[i], k, values) for i in range(3)], [empty() for _ in range(3)])
    for i, (top, total) in enumerate(states):
        top_out[i], total_out[i] = top, total
    top_out[3], total_out[3] = own_top[...], own_total[...]


def block_kernel(rows, top_in, total_in, kv, top_out, total_out, values):
    k = split(kv, values)
    states = [(top_in[i], total_in[i]) for i in range(4)]
    states = run([(i, rows.at[i], k, values) for i in range(4)], states)
    for i, (top, total) in enumerate(states):
        top_out[i], total_out[i] = top, total


def last_kernel(rows, top_in, total_in, kv, p0, p1, p2, values):
    k = split(kv, values)
    states = [(top_in[i], total_in[i]) for i in range(3)]
    states = run([(i, rows.at[i], k, values) for i in range(3)], states)
    for state, ref in zip(states, (p0, p1, p2)):
        ref[...] = packed(*finish(*state))


def own_last_kernel(rows, top, total, kv, result_ref, level_ref, values):
    k = split(kv, values)
    states = run([(0, rows.at[3], k, values)], [(top[3], total[3])])
    result, level = finish(*states[0])
    result_ref[...] = result
    level_ref[...] = jnp.broadcast_to(level, (8, LANES))


def merge_kernel(live, result, level, r0, r1, r2, att):
    parts = [(result[...], level[:1])] + [unpacked(r) for r in (r0, r1, r2)]
    whole, _ = merged(parts)
    slot = lax.broadcasted_iota(jnp.int32, (1, LANES), 1) % ROWS
    rows = jnp.where(slot < live[0], whole, 0.0).T.astype(jnp.bfloat16)
    for head in range(GROUP):
        att[:, head * DH : (head + 1) * DH] = rows[head * ROWS : (head + 1) * ROWS, :]


def project_kernel(index, a0, a1, a2, a3, a4, a5, a6, a7, wa, wb, out, rows):
    for i, ref in enumerate((a0, a1, a2, a3, a4, a5, a6, a7)):
        rows[i * ROWS : (i + 1) * ROWS, :] = ref[...]
    width = wa.shape[1]
    xh, z = index[0] // (Z * CORE), (index[0] // CORE) % Z
    slots = [((xh + dx) % XH) * Z + (z + Z - dz) % Z for dx in range(XH) for dz in (0,) + FAR]
    for side, w in enumerate((wa, wb)):
        terms = jnp.dot(rows[...], w[...], preferred_element_type=jnp.float32).astype(jnp.bfloat16)
        for i in range(8):
            out[slots[i], :, side * width : (side + 1) * width] = terms[i * ROWS : (i + 1) * ROWS, :]


def sum_kernel(terms, mine, other, *, width):
    acc = terms[0].astype(jnp.float32)
    for i in range(1, terms.shape[0]):
        acc = acc + terms[i].astype(jnp.float32)
    acc = acc.astype(jnp.bfloat16)
    mine[...] = acc[:, :width]
    other[...] = acc[:, width:]


def call(kernel, outs, scratch=(), flops=0, limit=VMEM_LIMIT, **kwargs):
    return pl.pallas_call(
        kernel,
        out_shape=tuple(jax.ShapeDtypeStruct(s, d) for s, d in outs),
        scratch_shapes=list(scratch),
        compiler_params=pltpu.CompilerParams(vmem_limit_bytes=limit),
        cost_estimate=(
            pl.CostEstimate(flops=flops, bytes_accessed=0, transcendentals=0) if flops else None
        ),
        **kwargs,
    )


def shards(
    queries,
    question_keys,
    question_values,
    question_ids,
    live_rows,
    prefix_keys,
    prefix_values,
    out_weight,
):
    f32, bf16 = jnp.float32, jnp.bfloat16
    index = lax.axis_index("blk")
    core = index % CORE
    positions = prefix_keys.shape[0]
    vmem = pl.BlockSpec(memory_space=pltpu.VMEM)
    smem = pl.BlockSpec(memory_space=pltpu.SMEM)
    block_flops = 8 * LANES * positions * DH
    part = ((DH + EXTRA, LANES), bf16)
    ones_shape = (positions, 2 * DH)

    own_state = [((LANES, DH), f32), ((LANES, 2 * DH), f32)]
    state = [((4, LANES, DH), f32), ((4, LANES, 2 * DH), f32)]

    hbm = pl.BlockSpec(memory_space=pltpu.HBM)
    (kv,) = call(
        join_kernel,
        [((2 * positions, DH), bf16)],
        [pltpu.SemaphoreType.DMA((4,))],
        limit=62 << 20,
        in_specs=[hbm, hbm],
        out_specs=(hbm,),
    )(prefix_keys, prefix_values)
    kv_x = moved(kv, xh=1)
    kv_c = moved(kv, c=1)
    q_z = [moved(queries, z=z) for z in FAR]
    row = jnp.arange(ROWS, dtype=jnp.int32)
    allowed = (question_ids[:, None] == question_ids[None, :]) & (row[None, :] <= row[:, None])
    bias = jnp.where(allowed, 0.0, FLOOR).astype(f32)
    scratch = [pltpu.VMEM(ones_shape, bf16)]
    own_top, own_total = call(own_kernel, own_state, scratch)(
        after(queries, q_z[0]), question_keys, question_values, bias, kv
    )
    top, total, rows = call(near_kernel, state + [((4, LANES, DH), bf16)], scratch)(
        *q_z, queries, own_top, own_total, kv
    )
    top, total = call(block_kernel, state, scratch)(rows, top, total, kv_c)

    kv_x, weight, top, total = lax.optimization_barrier((kv_x, out_weight, top, total))
    kv_xc = moved(kv_x, c=1)
    weight_c = moved(weight, c=1)
    top, total = call(block_kernel, state, scratch, flops=4 * block_flops)(rows, top, total, kv_x)
    parts = call(last_kernel, [part] * 3, scratch, flops=3 * block_flops)(rows, top, total, kv_xc)
    back = [moved(p, z=-z) for p, z in zip(parts, FAR)]
    result, level = call(
        own_last_kernel,
        [((DH, LANES), f32), ((8, LANES), f32)],
        [pltpu.VMEM(ones_shape, bf16)],
        flops=block_flops,
    )(after(rows, *parts), top, total, kv_xc)
    (att,) = call(
        merge_kernel, [((ROWS, GROUP * DH), bf16)], in_specs=[smem] + [vmem] * 5
    )(live_rows, result, level, *back)

    att_x = moved(att, xh=1)
    held = [att] + [moved(att, z=z) for z in FAR] + [att_x] + [moved(att_x, z=z) for z in FAR]
    width = out_weight.shape[1]
    (terms,) = call(
        project_kernel,
        [((8, ROWS, CORE * width), bf16)],
        [pltpu.VMEM((8 * ROWS, GROUP * DH), bf16)],
        in_specs=[smem] + [vmem] * 10,
    )(index.reshape(1), *held, out_weight, weight_c)
    gathered = lax.all_to_all(terms, "head", 0, 0, tiled=True)
    mine, other = call(
        functools.partial(sum_kernel, width=width),
        [((ROWS, width), bf16), ((ROWS, width), bf16)],
    )(gathered)
    theirs = moved(other, c=1)
    return jnp.where(
        core == 0,
        jnp.concatenate([mine, theirs], axis=0),
        jnp.concatenate([theirs, mine], axis=0),
    )


def solution(mesh):
    return jax.shard_map(
        shards,
        mesh=mesh,
        in_specs=(
            P("blk", "head"),
            P("blk", "head"),
            P("blk", "head"),
            P("blk"),
            P("blk"),
            P("blk", "head"),
            P("blk", "head"),
            P("head", "blk"),
        ),
        out_specs=P("head", "blk"),
        check_vma=False,
    )
```

```python
import functools

import jax
import jax.numpy as jnp
from jax import lax
from jax.experimental import pallas as pl
from jax.experimental.pallas import tpu as pltpu
from jax.sharding import PartitionSpec as P

DH = 128
GROUP = 8
ROWS = 64
LANES = GROUP * ROWS
EXTRA = 16
SCALE = DH**-0.5 * 1.4426950408889634
FLOOR = -1e30
XH, Z, CORE = 2, 4, 2
VMEM_LIMIT = 30 << 20
FAR = (1, 3, 2)


def moved(array, xh=0, z=0, c=0):
    pairs = []
    for i in range(XH * Z * CORE):
        a, b, d = i // (Z * CORE), (i // CORE) % Z, i % CORE
        to = (((a + xh) % XH) * Z + (b + z) % Z) * CORE + (d + c) % CORE
        pairs.append((i, to))
    return lax.ppermute(array, "blk", pairs)


def after(array, *others):
    return lax.optimization_barrier((array, *others))[0]


def scores_of(queries, keys):
    return lax.dot_general(
        queries, keys, (((1,), (1,)), ((), ())), preferred_element_type=jnp.float32
    )


def wide(column, width):
    return jnp.concatenate([column] * (width // column.shape[1]), axis=1)


def add_block(top, total, scores, values):
    best = jnp.maximum(top, jnp.max(scores, axis=1, keepdims=True) * SCALE)
    keys = scores.shape[1]
    at = wide(best, keys) if keys >= DH else best[:, :keys]
    weights = jnp.exp2(scores * SCALE - at).astype(jnp.bfloat16)
    part = jnp.dot(weights, values, preferred_element_type=jnp.float32)
    return best, total * wide(jnp.exp2(top - best), 2 * DH) + part


def stacked(ref):
    return jnp.concatenate([ref[:, h * DH : (h + 1) * DH] for h in range(GROUP)], axis=0)


def join_kernel(k, v, kv):
    half = k.shape[0]
    kv[:half, :] = k[...]
    kv[half:, :] = v[...]


def split(kv, scratch):
    half = kv.shape[0] // 2
    scratch[:, :DH] = kv[half:, :]
    scratch[:, DH:] = jnp.ones((half, DH), kv.dtype)
    return kv.at[pl.ds(0, half)]


def finish(top, total):
    denominator = total[:, DH:]
    result = (total[:, :DH] / denominator).T
    level = (top + jnp.log2(denominator)).T[:1]
    return result, level


def packed(result, level):
    high = level.astype(jnp.bfloat16).astype(jnp.float32)
    mid = (level - high).astype(jnp.bfloat16).astype(jnp.float32)
    low = level - high - mid
    row = lax.broadcasted_iota(jnp.int32, (EXTRA, LANES), 0)
    pieces = jnp.where(row == 0, high, jnp.where(row == 1, mid, low))
    return jnp.concatenate([result, pieces], axis=0).astype(jnp.bfloat16)


def unpacked(block):
    pieces = block[DH:, :].astype(jnp.float32)
    return block[:DH, :].astype(jnp.float32), (pieces[0:1] + pieces[1:2]) + pieces[2:3]


def merged(parts):
    best = functools.reduce(jnp.maximum, [level for _, level in parts])
    numerator, denominator = 0.0, 0.0
    for result, level in parts:
        share = jnp.exp2(level - best)
        numerator = numerator + result * share
        denominator = denominator + share
    return numerator / denominator, best + jnp.log2(denominator)


def run(tasks, states):
    def scores_at(i):
        _, rows, keys, _ = tasks[i]
        return scores_of(rows[...], keys[...])

    ahead = scores_at(0)
    for i, (owner, _, _, values) in enumerate(tasks):
        scores = ahead
        if i + 1 < len(tasks):
            ahead = scores_at(i + 1)
        states[owner] = add_block(*states[owner], scores, values[...])
    return states


def empty():
    return (
        jnp.full((LANES, DH), FLOOR, jnp.float32),
        jnp.zeros((LANES, 2 * DH), jnp.float32),
    )


def own_kernel(q, qk, qv, bias, kv, top_out, total_out, values):
    k = split(kv, values)
    rows = stacked(q)
    scores = scores_of(rows, qk[...]) + jnp.concatenate([bias[...]] * GROUP, axis=0)
    far = scores_of(rows, k[...])
    top, total = add_block(
        *empty(),
        scores,
        jnp.concatenate([qv[...], jnp.ones((ROWS, DH), jnp.bfloat16)], axis=1),
    )
    top_out[...], total_out[...] = add_block(top, total, far, values[...])


def near_kernel(q0, q1, q2, q, own_top, own_total, kv, top_out, total_out, rows, values):
    k = split(kv, values)
    for i, ref in enumerate((q0, q1, q2, q)):
        rows[i] = stacked(ref)
    states = run([(i, rows.at[i], k, values) for i in range(3)], [empty() for _ in range(3)])
    for i, (top, total) in enumerate(states):
        top_out[i], total_out[i] = top, total
    top_out[3], total_out[3] = own_top[...], own_total[...]


def block_kernel(rows, top_in, total_in, kv, top_out, total_out, values):
    k = split(kv, values)
    states = [(top_in[i], total_in[i]) for i in range(4)]
    states = run([(i, rows.at[i], k, values) for i in range(4)], states)
    for i, (top, total) in enumerate(states):
        top_out[i], total_out[i] = top, total


def last_kernel(rows, top_in, total_in, kv, p0, p1, p2, values):
    k = split(kv, values)
    states = [(top_in[i], total_in[i]) for i in range(3)]
    states = run([(i, rows.at[i], k, values) for i in range(3)], states)
    for state, ref in zip(states, (p0, p1, p2)):
        ref[...] = packed(*finish(*state))


def own_last_kernel(rows, top, total, kv, result_ref, level_ref, values):
    k = split(kv, values)
    states = run([(0, rows.at[3], k, values)], [(top[3], total[3])])
    result, level = finish(*states[0])
    result_ref[...] = result
    level_ref[...] = jnp.broadcast_to(level, (8, LANES))


def merge_kernel(live, result, level, r0, r1, r2, att):
    parts = [(result[...], level[:1])] + [unpacked(r) for r in (r0, r1, r2)]
    whole, _ = merged(parts)
    slot = lax.broadcasted_iota(jnp.int32, (1, LANES), 1) % ROWS
    rows = jnp.where(slot < live[0], whole, 0.0).T.astype(jnp.bfloat16)
    for head in range(GROUP):
        att[:, head * DH : (head + 1) * DH] = rows[head * ROWS : (head + 1) * ROWS, :]


def project_kernel(index, a0, a1, a2, a3, a4, a5, a6, a7, wa, wb, out, rows):
    for i, ref in enumerate((a0, a1, a2, a3, a4, a5, a6, a7)):
        rows[i * ROWS : (i + 1) * ROWS, :] = ref[...]
    width = wa.shape[1]
    xh, z = index[0] // (Z * CORE), (index[0] // CORE) % Z
    slots = [((xh + dx) % XH) * Z + (z + Z - dz) % Z for dx in range(XH) for dz in (0,) + FAR]
    for side, w in enumerate((wa, wb)):
        terms = jnp.dot(rows[...], w[...], preferred_element_type=jnp.float32).astype(jnp.bfloat16)
        for i in range(8):
            out[slots[i], :, side * width : (side + 1) * width] = terms[i * ROWS : (i + 1) * ROWS, :]


def sum_kernel(terms, mine, other, *, width):
    acc = terms[0].astype(jnp.float32)
    for i in range(1, terms.shape[0]):
        acc = acc + terms[i].astype(jnp.float32)
    acc = acc.astype(jnp.bfloat16)
    mine[...] = acc[:, :width]
    other[...] = acc[:, width:]


def call(kernel, outs, scratch=(), flops=0, **kwargs):
    return pl.pallas_call(
        kernel,
        out_shape=tuple(jax.ShapeDtypeStruct(s, d) for s, d in outs),
        scratch_shapes=list(scratch),
        compiler_params=pltpu.CompilerParams(vmem_limit_bytes=VMEM_LIMIT),
        cost_estimate=(
            pl.CostEstimate(flops=flops, bytes_accessed=0, transcendentals=0) if flops else None
        ),
        **kwargs,
    )


def shards(
    queries,
    question_keys,
    question_values,
    question_ids,
    live_rows,
    prefix_keys,
    prefix_values,
    out_weight,
):
    f32, bf16 = jnp.float32, jnp.bfloat16
    index = lax.axis_index("blk")
    core = index % CORE
    positions = prefix_keys.shape[0]
    vmem = pl.BlockSpec(memory_space=pltpu.VMEM)
    smem = pl.BlockSpec(memory_space=pltpu.SMEM)
    block_flops = 8 * LANES * positions * DH
    part = ((DH + EXTRA, LANES), bf16)
    ones_shape = (positions, 2 * DH)

    own_state = [((LANES, DH), f32), ((LANES, 2 * DH), f32)]
    state = [((4, LANES, DH), f32), ((4, LANES, 2 * DH), f32)]

    (kv,) = call(join_kernel, [((2 * positions, DH), bf16)])(prefix_keys, prefix_values)
    kv_x = moved(kv, xh=1)
    kv_c = moved(kv, c=1)
    q_z = [moved(queries, z=z) for z in FAR]
    row = jnp.arange(ROWS, dtype=jnp.int32)
    allowed = (question_ids[:, None] == question_ids[None, :]) & (row[None, :] <= row[:, None])
    bias = jnp.where(allowed, 0.0, FLOOR).astype(f32)
    scratch = [pltpu.VMEM(ones_shape, bf16)]
    own_top, own_total = call(own_kernel, own_state, scratch)(
        after(queries, q_z[0]), question_keys, question_values, bias, kv
    )
    top, total, rows = call(near_kernel, state + [((4, LANES, DH), bf16)], scratch)(
        *q_z, queries, own_top, own_total, kv
    )
    top, total = call(block_kernel, state, scratch)(rows, top, total, kv_c)

    kv_x, weight, top, total = lax.optimization_barrier((kv_x, out_weight, top, total))
    kv_xc = moved(kv_x, c=1)
    weight_c = moved(weight, c=1)
    top, total = call(block_kernel, state, scratch, flops=4 * block_flops)(rows, top, total, kv_x)
    parts = call(last_kernel, [part] * 3, scratch, flops=3 * block_flops)(rows, top, total, kv_xc)
    back = [moved(p, z=-z) for p, z in zip(parts, FAR)]
    result, level = call(
        own_last_kernel,
        [((DH, LANES), f32), ((8, LANES), f32)],
        [pltpu.VMEM(ones_shape, bf16)],
        flops=block_flops,
    )(after(rows, *parts), top, total, kv_xc)
    (att,) = call(
        merge_kernel, [((ROWS, GROUP * DH), bf16)], in_specs=[smem] + [vmem] * 5
    )(live_rows, result, level, *back)

    att_x = moved(att, xh=1)
    held = [att] + [moved(att, z=z) for z in FAR] + [att_x] + [moved(att_x, z=z) for z in FAR]
    width = out_weight.shape[1]
    (terms,) = call(
        project_kernel,
        [((8, ROWS, CORE * width), bf16)],
        [pltpu.VMEM((8 * ROWS, GROUP * DH), bf16)],
        in_specs=[smem] + [vmem] * 10,
    )(index.reshape(1), *held, out_weight, weight_c)
    gathered = lax.all_to_all(terms, "head", 0, 0, tiled=True)
    mine, other = call(
        functools.partial(sum_kernel, width=width),
        [((ROWS, width), bf16), ((ROWS, width), bf16)],
    )(gathered)
    theirs = moved(other, c=1)
    return jnp.where(
        core == 0,
        jnp.concatenate([mine, theirs], axis=0),
        jnp.concatenate([theirs, mine], axis=0),
    )


def solution(mesh):
    return jax.shard_map(
        shards,
        mesh=mesh,
        in_specs=(
            P("blk", "head"),
            P("blk", "head"),
            P("blk", "head"),
            P("blk"),
            P("blk"),
            P("blk", "head"),
            P("blk", "head"),
            P("head", "blk"),
        ),
        out_specs=P("head", "blk"),
        check_vma=False,
    )
```

```python
import functools
import itertools

import jax
import jax.numpy as jnp
from jax import lax
from jax.experimental import pallas as pl
from jax.experimental.pallas import tpu as pltpu
from jax.sharding import PartitionSpec as P

DH = 128
GROUP = 8
ROWS = 64
LANES = GROUP * ROWS
EXTRA = 16
SCALE = DH**-0.5 * 1.4426950408889634
FLOOR = -1e30
XH, Z, CORE, Y, XL = 2, 4, 2, 4, 2
PIECES = tuple(itertools.product(range(2), range(2), range(2)))
VMEM_LIMIT = 30 << 20
FAR = (1, 3, 2)


def moved(array, xh=0, z=0, c=0):
    pairs = []
    for i in range(XH * Z * CORE):
        a, b, d = i // (Z * CORE), (i // CORE) % Z, i % CORE
        to = (((a + xh) % XH) * Z + (b + z) % Z) * CORE + (d + c) % CORE
        pairs.append((i, to))
    return lax.ppermute(array, "blk", pairs)


def routed(array, source_of):
    pairs = []
    for to in itertools.product(range(XH), range(Z), range(CORE), range(Y), range(XL)):
        pairs.append((place(source_of(*to)), place(to)))
    return lax.ppermute(array, ("blk", "head"), sorted(pairs))


def place(at):
    xh, z, c, y, xl = at
    return (((xh * Z + z) * CORE + c) * Y + y) * XL + xl


def after(array, *others):
    return lax.optimization_barrier((array, *others))[0]


def scores_of(queries, keys):
    return lax.dot_general(
        queries, keys, (((1,), (1,)), ((), ())), preferred_element_type=jnp.float32
    )


def wide(column, width):
    return jnp.concatenate([column] * (width // column.shape[1]), axis=1)


def add_block(top, total, scores, values):
    best = jnp.maximum(top, jnp.max(scores, axis=1, keepdims=True) * SCALE)
    keys = scores.shape[1]
    at = wide(best, keys) if keys >= DH else best[:, :keys]
    weights = jnp.exp2(scores * SCALE - at).astype(jnp.bfloat16)
    part = jnp.dot(weights, values, preferred_element_type=jnp.float32)
    return best, total * wide(jnp.exp2(top - best), 2 * DH) + part


def stacked(ref):
    return jnp.concatenate([ref[:, h * DH : (h + 1) * DH] for h in range(GROUP)], axis=0)


def join_kernel(k, v, kv):
    half = k.shape[0]
    kv[:half, :] = k[...]
    kv[half:, :] = v[...]


def split(kv, scratch):
    half = kv.shape[0] // 2
    scratch[:, :DH] = kv[half:, :]
    scratch[:, DH:] = jnp.ones((half, DH), kv.dtype)
    return kv.at[pl.ds(0, half)]


def finish(top, total):
    denominator = total[:, DH:]
    result = (total[:, :DH] / denominator).T
    level = (top + jnp.log2(denominator)).T[:1]
    return result, level


def packed(result, level):
    high = level.astype(jnp.bfloat16).astype(jnp.float32)
    mid = (level - high).astype(jnp.bfloat16).astype(jnp.float32)
    low = level - high - mid
    row = lax.broadcasted_iota(jnp.int32, (EXTRA, LANES), 0)
    pieces = jnp.where(row == 0, high, jnp.where(row == 1, mid, low))
    return jnp.concatenate([result, pieces], axis=0).astype(jnp.bfloat16)


def unpacked(block):
    pieces = block[DH:, :].astype(jnp.float32)
    return block[:DH, :].astype(jnp.float32), (pieces[0:1] + pieces[1:2]) + pieces[2:3]


def merged(parts):
    best = functools.reduce(jnp.maximum, [level for _, level in parts])
    numerator, denominator = 0.0, 0.0
    for result, level in parts:
        share = jnp.exp2(level - best)
        numerator = numerator + result * share
        denominator = denominator + share
    return numerator / denominator, best + jnp.log2(denominator)


def run(tasks, states):
    def scores_at(i):
        _, rows, keys, _ = tasks[i]
        return scores_of(rows[...], keys[...])

    ahead = scores_at(0)
    for i, (owner, _, _, values) in enumerate(tasks):
        scores = ahead
        if i + 1 < len(tasks):
            ahead = scores_at(i + 1)
        states[owner] = add_block(*states[owner], scores, values[...])
    return states


def empty():
    return (
        jnp.full((LANES, DH), FLOOR, jnp.float32),
        jnp.zeros((LANES, 2 * DH), jnp.float32),
    )


def own_kernel(q, qk, qv, bias, kv, top_out, total_out, values):
    k = split(kv, values)
    rows = stacked(q)
    scores = scores_of(rows, qk[...]) + jnp.concatenate([bias[...]] * GROUP, axis=0)
    far = scores_of(rows, k[...])
    top, total = add_block(
        *empty(),
        scores,
        jnp.concatenate([qv[...], jnp.ones((ROWS, DH), jnp.bfloat16)], axis=1),
    )
    top_out[...], total_out[...] = add_block(top, total, far, values[...])


def near_kernel(q0, q1, q2, q, own_top, own_total, kv, top_out, total_out, rows, values):
    k = split(kv, values)
    for i, ref in enumerate((q0, q1, q2, q)):
        rows[i] = stacked(ref)
    states = run([(i, rows.at[i], k, values) for i in range(3)], [empty() for _ in range(3)])
    for i, (top, total) in enumerate(states):
        top_out[i], total_out[i] = top, total
    top_out[3], total_out[3] = own_top[...], own_total[...]


def block_kernel(rows, top_in, total_in, kv, top_out, total_out, values):
    k = split(kv, values)
    states = [(top_in[i], total_in[i]) for i in range(4)]
    states = run([(i, rows.at[i], k, values) for i in range(4)], states)
    for i, (top, total) in enumerate(states):
        top_out[i], total_out[i] = top, total


def last_kernel(rows, top_in, total_in, kv, p0, p1, p2, values):
    k = split(kv, values)
    states = [(top_in[i], total_in[i]) for i in range(3)]
    states = run([(i, rows.at[i], k, values) for i in range(3)], states)
    for state, ref in zip(states, (p0, p1, p2)):
        ref[...] = packed(*finish(*state))


def own_last_kernel(rows, top, total, kv, result_ref, level_ref, values):
    k = split(kv, values)
    states = run([(0, rows.at[3], k, values)], [(top[3], total[3])])
    result, level = finish(*states[0])
    result_ref[...] = result
    level_ref[...] = jnp.broadcast_to(level, (8, LANES))


def merge_kernel(live, result, level, r0, r1, r2, att):
    parts = [(result[...], level[:1])] + [unpacked(r) for r in (r0, r1, r2)]
    whole, _ = merged(parts)
    slot = lax.broadcasted_iota(jnp.int32, (1, LANES), 1) % ROWS
    rows = jnp.where(slot < live[0], whole, 0.0).T.astype(jnp.bfloat16)
    for head in range(GROUP):
        att[:, head * DH : (head + 1) * DH] = rows[head * ROWS : (head + 1) * ROWS, :]


def project_kernel(index, a0, a1, a2, a3, a4, a5, a6, a7, wa, wb, xa, xb, t0, t1, t2, t3, rows, terms):
    blk, head = index[0], index[1]
    xh, z = blk // (Z * CORE), (blk // CORE) % Z
    y, xl = head // XL, head % XL
    swap = (z % 2 + xl) % 2
    for (dx, dz, e), ref in zip(PIECES, (a0, a1, a2, a3, a4, a5, a6, a7)):
        at = (2 * dx + dz) * ROWS
        rows[(swap + e) % 2, at : at + ROWS, :] = ref[...]
    width = wa.shape[1]
    for side, (mine, other) in enumerate(((wa, xa), (wb, xb))):
        part = jnp.dot(rows[0], mine[...], preferred_element_type=jnp.float32) + jnp.dot(
            rows[1], other[...], preferred_element_type=jnp.float32
        )
        for i in range(4):
            terms[i, :, side * width : (side + 1) * width] = part[i * ROWS : (i + 1) * ROWS, :]
    for s, out in enumerate((t0, t1, t2, t3)):
        to = (y + s) % Y
        i = 2 * ((to // 2 + xh) % 2) + (to % 2 + z // 2) % 2
        out[...] = terms[i].astype(out.dtype)


def sum_kernel(own, r1, r2, r3, mine, other):
    acc = own[...]
    for ref in (r1, r2, r3):
        acc = acc + ref[...].astype(jnp.float32)
    acc = acc.astype(jnp.bfloat16)
    width = mine.shape[1]
    mine[...] = acc[:, :width]
    other[...] = acc[:, width:]


def call(kernel, outs, scratch=(), flops=0, **kwargs):
    return pl.pallas_call(
        kernel,
        out_shape=tuple(jax.ShapeDtypeStruct(s, d) for s, d in outs),
        scratch_shapes=list(scratch),
        compiler_params=pltpu.CompilerParams(vmem_limit_bytes=VMEM_LIMIT),
        cost_estimate=(
            pl.CostEstimate(flops=flops, bytes_accessed=0, transcendentals=0) if flops else None
        ),
        **kwargs,
    )


def shards(
    queries,
    question_keys,
    question_values,
    question_ids,
    live_rows,
    prefix_keys,
    prefix_values,
    out_weight,
):
    f32, bf16 = jnp.float32, jnp.bfloat16
    index = lax.axis_index("blk")
    core = index % CORE
    positions = prefix_keys.shape[0]
    vmem = pl.BlockSpec(memory_space=pltpu.VMEM)
    smem = pl.BlockSpec(memory_space=pltpu.SMEM)
    block_flops = 8 * LANES * positions * DH
    part = ((DH + EXTRA, LANES), bf16)
    ones_shape = (positions, 2 * DH)

    own_state = [((LANES, DH), f32), ((LANES, 2 * DH), f32)]
    state = [((4, LANES, DH), f32), ((4, LANES, 2 * DH), f32)]

    (kv,) = call(join_kernel, [((2 * positions, DH), bf16)])(prefix_keys, prefix_values)
    kv_x = moved(kv, xh=1)
    kv_c = moved(kv, c=1)
    q_z = [moved(queries, z=z) for z in FAR]
    row = jnp.arange(ROWS, dtype=jnp.int32)
    allowed = (question_ids[:, None] == question_ids[None, :]) & (row[None, :] <= row[:, None])
    bias = jnp.where(allowed, 0.0, FLOOR).astype(f32)
    scratch = [pltpu.VMEM(ones_shape, bf16)]
    own_top, own_total = call(own_kernel, own_state, scratch)(
        after(queries, q_z[0]), question_keys, question_values, bias, kv
    )
    top, total, rows = call(near_kernel, state + [((4, LANES, DH), bf16)], scratch)(
        *q_z, queries, own_top, own_total, kv
    )
    top, total = call(block_kernel, state, scratch)(rows, top, total, kv_c)

    kv_x, weight, top, total = lax.optimization_barrier((kv_x, out_weight, top, total))
    kv_xc = moved(kv_x, c=1)
    weight_c = moved(weight, c=1)
    weight_x = routed(weight, lambda xh, z, c, y, xl: (xh, z, c, y, 1 - xl))
    top, total = call(block_kernel, state, scratch, flops=4 * block_flops)(rows, top, total, kv_x)
    parts = call(last_kernel, [part] * 3, scratch, flops=3 * block_flops)(rows, top, total, kv_xc)
    back = [moved(p, z=-z) for p, z in zip(parts, FAR)]
    result, level = call(
        own_last_kernel,
        [((DH, LANES), f32), ((8, LANES), f32)],
        [pltpu.VMEM(ones_shape, bf16)],
        flops=block_flops,
    )(after(rows, *parts), top, total, kv_xc)
    (att,) = call(
        merge_kernel, [((ROWS, GROUP * DH), bf16)], in_specs=[smem] + [vmem] * 5
    )(live_rows, result, level, *back)

    att, weight_x, weight_c = lax.optimization_barrier((att, weight_x, weight_c))
    weight_xc = moved(weight_x, c=1)
    held = [
        routed(
            att,
            lambda xh, z, c, y, xl, dx=dx, dz=dz, e=e: (
                xh ^ dx, 2 * ((z // 2) ^ dz) + xl, c, y, (z % 2) ^ e,
            ),
        )
        for dx, dz, e in PIECES
    ]
    width = out_weight.shape[1]
    shape = (ROWS, CORE * width)
    own, *terms = call(
        project_kernel,
        [(shape, f32)] + [(shape, bf16)] * 3,
        [pltpu.VMEM((2, 4 * ROWS, GROUP * DH), bf16), pltpu.VMEM((4,) + shape, f32)],
        in_specs=[smem] + [vmem] * 12,
    )(
        jnp.stack([index, lax.axis_index("head")]), *held,
        out_weight, weight_c, weight_x, weight_xc,
    )
    back = [
        routed(t, lambda xh, z, c, y, xl, s=s: (xh, z, c, (y - s) % Y, xl))
        for s, t in zip((1, 2, 3), terms)
    ]
    mine, other = call(sum_kernel, [((ROWS, width), bf16)] * 2)(own, *back)
    theirs = moved(other, c=1)
    return jnp.where(
        core == 0,
        jnp.concatenate([mine, theirs], axis=0),
        jnp.concatenate([theirs, mine], axis=0),
    )


def solution(mesh):
    return jax.shard_map(
        shards,
        mesh=mesh,
        in_specs=(
            P("blk", "head"),
            P("blk", "head"),
            P("blk", "head"),
            P("blk"),
            P("blk"),
            P("blk", "head"),
            P("blk", "head"),
            P("head", "blk"),
        ),
        out_specs=P("head", "blk"),
        check_vma=False,
    )
```

```python
import functools

import jax
import jax.numpy as jnp
from jax import lax
from jax.experimental import pallas as pl
from jax.experimental.pallas import tpu as pltpu
from jax.sharding import PartitionSpec as P

DH = 128
GROUP = 8
ROWS = 64
LANES = GROUP * ROWS
EXTRA = 16
SCALE = DH**-0.5 * 1.4426950408889634
FLOOR = -1e30
XH, Z, CORE = 2, 4, 2
VMEM_LIMIT = 30 << 20
FAR = (1, 3, 2)


def moved(array, xh=0, z=0, c=0):
    pairs = []
    for i in range(XH * Z * CORE):
        a, b, d = i // (Z * CORE), (i // CORE) % Z, i % CORE
        to = (((a + xh) % XH) * Z + (b + z) % Z) * CORE + (d + c) % CORE
        pairs.append((i, to))
    return lax.ppermute(array, "blk", pairs)


def after(array, *others):
    return lax.optimization_barrier((array, *others))[0]


def scores_of(queries, keys):
    return lax.dot_general(
        queries, keys, (((1,), (1,)), ((), ())), preferred_element_type=jnp.float32
    )


def wide(column, width):
    return jnp.concatenate([column] * (width // column.shape[1]), axis=1)


def add_block(top, total, scores, values):
    best = jnp.maximum(top, jnp.max(scores, axis=1, keepdims=True) * SCALE)
    keys = scores.shape[1]
    at = wide(best, keys) if keys >= DH else best[:, :keys]
    weights = jnp.exp2(scores * SCALE - at).astype(jnp.bfloat16)
    part = jnp.dot(weights, values, preferred_element_type=jnp.float32)
    return best, total * wide(jnp.exp2(top - best), 2 * DH) + part


def stacked(ref):
    return jnp.concatenate([ref[:, h * DH : (h + 1) * DH] for h in range(GROUP)], axis=0)


def join_kernel(k, v, kv):
    half = k.shape[0]
    kv[:half, :] = k[...]
    kv[half:, :] = v[...]


def split(kv, scratch):
    half = kv.shape[0] // 2
    scratch[:, :DH] = kv[half:, :]
    scratch[:, DH:] = jnp.ones((half, DH), kv.dtype)
    return kv.at[pl.ds(0, half)]


def finish(top, total):
    denominator = total[:, DH:]
    result = (total[:, :DH] / denominator).T
    level = (top + jnp.log2(denominator)).T[:1]
    return result, level


def packed(result, level):
    high = level.astype(jnp.bfloat16).astype(jnp.float32)
    mid = (level - high).astype(jnp.bfloat16).astype(jnp.float32)
    low = level - high - mid
    row = lax.broadcasted_iota(jnp.int32, (EXTRA, LANES), 0)
    pieces = jnp.where(row == 0, high, jnp.where(row == 1, mid, low))
    return jnp.concatenate([result, pieces], axis=0).astype(jnp.bfloat16)


def unpacked(block):
    pieces = block[DH:, :].astype(jnp.float32)
    return block[:DH, :].astype(jnp.float32), (pieces[0:1] + pieces[1:2]) + pieces[2:3]


def merged(parts):
    best = functools.reduce(jnp.maximum, [level for _, level in parts])
    numerator, denominator = 0.0, 0.0
    for result, level in parts:
        share = jnp.exp2(level - best)
        numerator = numerator + result * share
        denominator = denominator + share
    return numerator / denominator, best + jnp.log2(denominator)


def run(tasks, states):
    def scores_at(i):
        _, rows, keys, _ = tasks[i]
        return scores_of(rows[...], keys[...])

    ahead = scores_at(0)
    for i, (owner, _, _, values) in enumerate(tasks):
        scores = ahead
        if i + 1 < len(tasks):
            ahead = scores_at(i + 1)
        states[owner] = add_block(*states[owner], scores, values[...])
    return states


def empty():
    return (
        jnp.full((LANES, DH), FLOOR, jnp.float32),
        jnp.zeros((LANES, 2 * DH), jnp.float32),
    )


def own_kernel(q, qk, qv, bias, kv, top_out, total_out, values):
    k = split(kv, values)
    rows = stacked(q)
    scores = scores_of(rows, qk[...]) + jnp.concatenate([bias[...]] * GROUP, axis=0)
    far = scores_of(rows, k[...])
    top, total = add_block(
        *empty(),
        scores,
        jnp.concatenate([qv[...], jnp.ones((ROWS, DH), jnp.bfloat16)], axis=1),
    )
    top_out[...], total_out[...] = add_block(top, total, far, values[...])


def near_kernel(q0, q1, q2, q, kv, top_out, total_out, rows, values):
    k = split(kv, values)
    for i, ref in enumerate((q0, q1, q2, q)):
        rows[i] = stacked(ref)
    states = run([(i, rows.at[i], k, values) for i in range(3)], [empty() for _ in range(3)])
    for i, (top, total) in enumerate(states):
        top_out[i], total_out[i] = top, total


def core_kernel(rows, top_in, total_in, kv, top_out, total_out, values):
    k = split(kv, values)
    states = [(top_in[i], total_in[i]) for i in range(3)]
    states = run([(i, rows.at[i], k, values) for i in range(3)], states)
    for i, (top, total) in enumerate(states):
        top_out[i], total_out[i] = top, total


def own_kernel_2(rows, top, total, kv0, kv1, top_out, total_out, values):
    k0, k1 = split(kv0, values.at[0]), split(kv1, values.at[1])
    tasks = [(0, rows.at[3], k0, values.at[0]), (0, rows.at[3], k1, values.at[1])]
    top_out[...], total_out[...] = run(tasks, [(top[...], total[...])])[0]


def far_kernel(rows, top, total, kv0, kv1, *refs, owners):
    *outs, values = refs
    k0, k1 = split(kv0, values.at[0]), split(kv1, values.at[1])
    tasks = []
    for i, owner in enumerate(owners):
        tasks.append((i, rows.at[owner], k0, values.at[0]))
        tasks.append((i, rows.at[owner], k1, values.at[1]))
    states = run(tasks, [(top[owner], total[owner]) for owner in owners])
    for state, out in zip(states, outs):
        out[...] = packed(*finish(*state))


def own_last_kernel(rows, top, total, kv, r2, result_ref, level_ref, values):
    k = split(kv, values)
    states = run([(0, rows.at[3], k, values)], [(top[...], total[...])])
    result, level = merged([finish(*states[0]), unpacked(r2)])
    result_ref[...] = result
    level_ref[...] = jnp.broadcast_to(level, (8, LANES))


def merge_kernel(live, result, level, r0, r1, att):
    parts = [(result[...], level[:1])] + [unpacked(r) for r in (r0, r1)]
    whole, _ = merged(parts)
    slot = lax.broadcasted_iota(jnp.int32, (1, LANES), 1) % ROWS
    rows = jnp.where(slot < live[0], whole, 0.0).T.astype(jnp.bfloat16)
    for head in range(GROUP):
        att[:, head * DH : (head + 1) * DH] = rows[head * ROWS : (head + 1) * ROWS, :]


def project_kernel(index, a0, a1, a2, a3, a4, a5, a6, a7, wa, wb, out, rows):
    for i, ref in enumerate((a0, a1, a2, a3, a4, a5, a6, a7)):
        rows[i * ROWS : (i + 1) * ROWS, :] = ref[...]
    width = wa.shape[1]
    xh, z = index[0] // (Z * CORE), (index[0] // CORE) % Z
    slots = [((xh + dx) % XH) * Z + (z + Z - dz) % Z for dx in range(XH) for dz in (0,) + FAR]
    for side, w in enumerate((wa, wb)):
        terms = jnp.dot(rows[...], w[...], preferred_element_type=jnp.float32).astype(jnp.bfloat16)
        for i in range(8):
            out[slots[i], :, side * width : (side + 1) * width] = terms[i * ROWS : (i + 1) * ROWS, :]


def sum_kernel(terms, mine, other, *, width):
    acc = terms[0].astype(jnp.float32)
    for i in range(1, terms.shape[0]):
        acc = acc + terms[i].astype(jnp.float32)
    acc = acc.astype(jnp.bfloat16)
    mine[...] = acc[:, :width]
    other[...] = acc[:, width:]


def call(kernel, outs, scratch=(), flops=0, **kwargs):
    return pl.pallas_call(
        kernel,
        out_shape=tuple(jax.ShapeDtypeStruct(s, d) for s, d in outs),
        scratch_shapes=list(scratch),
        compiler_params=pltpu.CompilerParams(vmem_limit_bytes=VMEM_LIMIT),
        cost_estimate=(
            pl.CostEstimate(flops=flops, bytes_accessed=0, transcendentals=0) if flops else None
        ),
        **kwargs,
    )


def shards(
    queries,
    question_keys,
    question_values,
    question_ids,
    live_rows,
    prefix_keys,
    prefix_values,
    out_weight,
):
    f32, bf16 = jnp.float32, jnp.bfloat16
    index = lax.axis_index("blk")
    core = index % CORE
    positions = prefix_keys.shape[0]
    vmem = pl.BlockSpec(memory_space=pltpu.VMEM)
    smem = pl.BlockSpec(memory_space=pltpu.SMEM)
    block_flops = 8 * LANES * positions * DH
    part = ((DH + EXTRA, LANES), bf16)
    ones_shape = (positions, 2 * DH)

    own_state = [((LANES, DH), f32), ((LANES, 2 * DH), f32)]
    state = [((3, LANES, DH), f32), ((3, LANES, 2 * DH), f32)]

    (kv,) = call(join_kernel, [((2 * positions, DH), bf16)])(prefix_keys, prefix_values)
    kv_x = moved(kv, xh=1)
    kv_c = moved(kv, c=1)
    q_z = [moved(queries, z=z) for z in FAR]
    row = jnp.arange(ROWS, dtype=jnp.int32)
    allowed = (question_ids[:, None] == question_ids[None, :]) & (row[None, :] <= row[:, None])
    bias = jnp.where(allowed, 0.0, FLOOR).astype(f32)
    scratch = [pltpu.VMEM(ones_shape, bf16)]
    own_top, own_total = call(own_kernel, own_state, scratch)(
        after(queries, q_z[0]), question_keys, question_values, bias, kv
    )
    top, total, rows = call(near_kernel, state + [((4, LANES, DH), bf16)], scratch)(
        *q_z, after(queries, own_top), kv
    )
    top, total = call(core_kernel, state, scratch)(rows, top, total, kv_c)

    kv_x, weight, top = lax.optimization_barrier((kv_x, out_weight, top))
    kv_xc = moved(kv_x, c=1)
    weight_c = moved(weight, c=1)
    pair = [pltpu.VMEM((2,) + ones_shape, bf16)]
    own_top, own_total = call(own_kernel_2, own_state, pair, flops=2 * block_flops)(
        rows, own_top, own_total, kv_c, kv_x
    )
    top = after(top, own_top)
    (p_far,) = call(functools.partial(far_kernel, owners=(2,)), [part], pair, flops=1)(
        rows, top, total, kv_x, kv_xc
    )
    p_next = call(functools.partial(far_kernel, owners=(0, 1)), [part] * 2, pair, flops=4 * block_flops)(
        rows, after(top, p_far), total, kv_x, kv_xc
    )
    back = [moved(p, z=-z) for p, z in zip((*p_next, p_far), FAR)]
    result, level = call(
        own_last_kernel, [((DH, LANES), f32), ((8, LANES), f32)], scratch, flops=1
    )(after(rows, *p_next), own_top, own_total, kv_xc, back[2])
    (att,) = call(
        merge_kernel, [((ROWS, GROUP * DH), bf16)], in_specs=[smem] + [vmem] * 4
    )(live_rows, result, level, *back[:2])

    att_x = moved(att, xh=1)
    held = [att] + [moved(att, z=z) for z in FAR] + [att_x] + [moved(att_x, z=z) for z in FAR]
    width = out_weight.shape[1]
    (terms,) = call(
        project_kernel,
        [((8, ROWS, CORE * width), bf16)],
        [pltpu.VMEM((8 * ROWS, GROUP * DH), bf16)],
        in_specs=[smem] + [vmem] * 10,
    )(index.reshape(1), *held, out_weight, weight_c)
    gathered = lax.all_to_all(terms, "head", 0, 0, tiled=True)
    mine, other = call(
        functools.partial(sum_kernel, width=width),
        [((ROWS, width), bf16), ((ROWS, width), bf16)],
    )(gathered)
    theirs = moved(other, c=1)
    return jnp.where(
        core == 0,
        jnp.concatenate([mine, theirs], axis=0),
        jnp.concatenate([theirs, mine], axis=0),
    )


def solution(mesh):
    return jax.shard_map(
        shards,
        mesh=mesh,
        in_specs=(
            P("blk", "head"),
            P("blk", "head"),
            P("blk", "head"),
            P("blk"),
            P("blk"),
            P("blk", "head"),
            P("blk", "head"),
            P("head", "blk"),
        ),
        out_specs=P("head", "blk"),
        check_vma=False,
    )
```

```python
import functools

import jax
import jax.numpy as jnp
from jax import lax
from jax.experimental import pallas as pl
from jax.experimental.pallas import tpu as pltpu
from jax.sharding import PartitionSpec as P

DH = 128
GROUP = 8
ROWS = 64
LANES = GROUP * ROWS
EXTRA = 16
SCALE = DH**-0.5 * 1.4426950408889634
FLOOR = -1e30
XH, Z, CORE = 2, 4, 2
VMEM_LIMIT = 30 << 20
FAR = (1, 3, 2)


def moved(array, xh=0, z=0, c=0):
    pairs = []
    for i in range(XH * Z * CORE):
        a, b, d = i // (Z * CORE), (i // CORE) % Z, i % CORE
        to = (((a + xh) % XH) * Z + (b + z) % Z) * CORE + (d + c) % CORE
        pairs.append((i, to))
    return lax.ppermute(array, "blk", pairs)


def after(array, *others):
    return lax.optimization_barrier((array, *others))[0]


def scores_of(queries, keys):
    return lax.dot_general(
        queries, keys, (((1,), (1,)), ((), ())), preferred_element_type=jnp.float32
    )


def wide(column, width):
    return jnp.concatenate([column] * (width // column.shape[1]), axis=1)


def add_block(top, total, scores, values):
    best = jnp.maximum(top, jnp.max(scores, axis=1, keepdims=True) * SCALE)
    keys = scores.shape[1]
    at = wide(best, keys) if keys >= DH else best[:, :keys]
    weights = jnp.exp2(scores * SCALE - at).astype(jnp.bfloat16)
    part = jnp.dot(weights, values, preferred_element_type=jnp.float32)
    return best, total * wide(jnp.exp2(top - best), 2 * DH) + part


def stacked(ref):
    return jnp.concatenate([ref[:, h * DH : (h + 1) * DH] for h in range(GROUP)], axis=0)


def join_kernel(k, v, kv):
    half = k.shape[0]
    kv[:half, :] = k[...]
    kv[half:, :] = v[...]


def split(kv, scratch):
    half = kv.shape[0] // 2
    scratch[:, :DH] = kv[half:, :]
    scratch[:, DH:] = jnp.ones((half, DH), kv.dtype)
    return kv.at[pl.ds(0, half)]


def finish(top, total):
    denominator = total[:, DH:]
    result = (total[:, :DH] / denominator).T
    level = (top + jnp.log2(denominator)).T[:1]
    return result, level


def packed(result, level):
    high = level.astype(jnp.bfloat16).astype(jnp.float32)
    mid = (level - high).astype(jnp.bfloat16).astype(jnp.float32)
    low = level - high - mid
    row = lax.broadcasted_iota(jnp.int32, (EXTRA, LANES), 0)
    pieces = jnp.where(row == 0, high, jnp.where(row == 1, mid, low))
    return jnp.concatenate([result, pieces], axis=0).astype(jnp.bfloat16)


def unpacked(block):
    pieces = block[DH:, :].astype(jnp.float32)
    return block[:DH, :].astype(jnp.float32), (pieces[0:1] + pieces[1:2]) + pieces[2:3]


def merged(parts):
    best = functools.reduce(jnp.maximum, [level for _, level in parts])
    numerator, denominator = 0.0, 0.0
    for result, level in parts:
        share = jnp.exp2(level - best)
        numerator = numerator + result * share
        denominator = denominator + share
    return numerator / denominator, best + jnp.log2(denominator)


def run(tasks, states):
    def scores_at(i):
        _, rows, keys, _ = tasks[i]
        return scores_of(rows[...], keys[...])

    ahead = scores_at(0)
    for i, (owner, _, _, values) in enumerate(tasks):
        scores = ahead
        if i + 1 < len(tasks):
            ahead = scores_at(i + 1)
        states[owner] = add_block(*states[owner], scores, values[...])
    return states


def empty():
    return (
        jnp.full((LANES, DH), FLOOR, jnp.float32),
        jnp.zeros((LANES, 2 * DH), jnp.float32),
    )


def own_kernel(q, qk, qv, bias, kv, top_out, total_out, values):
    k = split(kv, values)
    rows = stacked(q)
    scores = scores_of(rows, qk[...]) + jnp.concatenate([bias[...]] * GROUP, axis=0)
    far = scores_of(rows, k[...])
    top, total = add_block(
        *empty(),
        scores,
        jnp.concatenate([qv[...], jnp.ones((ROWS, DH), jnp.bfloat16)], axis=1),
    )
    top_out[...], total_out[...] = add_block(top, total, far, values[...])


def near_kernel(q0, q1, q2, q, kv, top_out, total_out, rows, values):
    k = split(kv, values)
    for i, ref in enumerate((q0, q1, q2, q)):
        rows[i] = stacked(ref)
    states = run([(i, rows.at[i], k, values) for i in range(3)], [empty() for _ in range(3)])
    for i, (top, total) in enumerate(states):
        top_out[i], total_out[i] = top, total


def core_kernel(rows, top_in, total_in, kv, top_out, total_out, values):
    k = split(kv, values)
    states = [(top_in[i], total_in[i]) for i in range(3)]
    states = run([(i, rows.at[i], k, values) for i in range(3)], states)
    for i, (top, total) in enumerate(states):
        top_out[i], total_out[i] = top, total


def own_kernel_2(rows, top, total, kv0, kv1, top_out, total_out, values):
    k0, k1 = split(kv0, values.at[0]), split(kv1, values.at[1])
    tasks = [(0, rows.at[3], k0, values.at[0]), (0, rows.at[3], k1, values.at[1])]
    top_out[...], total_out[...] = run(tasks, [(top[...], total[...])])[0]


def far_kernel(rows, top, total, kv0, kv1, *refs, owners):
    *outs, values = refs
    k0, k1 = split(kv0, values.at[0]), split(kv1, values.at[1])
    tasks = []
    for i, owner in enumerate(owners):
        tasks.append((i, rows.at[owner], k0, values.at[0]))
        tasks.append((i, rows.at[owner], k1, values.at[1]))
    states = run(tasks, [(top[owner], total[owner]) for owner in owners])
    for state, out in zip(states, outs):
        out[...] = packed(*finish(*state))


def own_last_kernel(rows, top, total, kv, r2, result_ref, level_ref, values):
    k = split(kv, values)
    states = run([(0, rows.at[3], k, values)], [(top[...], total[...])])
    result, level = merged([finish(*states[0]), unpacked(r2)])
    result_ref[...] = result
    level_ref[...] = jnp.broadcast_to(level, (8, LANES))


def merge_kernel(live, result, level, r0, r1, att):
    parts = [(result[...], level[:1])] + [unpacked(r) for r in (r0, r1)]
    whole, _ = merged(parts)
    slot = lax.broadcasted_iota(jnp.int32, (1, LANES), 1) % ROWS
    rows = jnp.where(slot < live[0], whole, 0.0).T.astype(jnp.bfloat16)
    for head in range(GROUP):
        att[:, head * DH : (head + 1) * DH] = rows[head * ROWS : (head + 1) * ROWS, :]


def project_kernel(index, a0, a1, a2, a3, a4, a5, a6, a7, wa, wb, out, rows):
    for i, ref in enumerate((a0, a1, a2, a3, a4, a5, a6, a7)):
        rows[i * ROWS : (i + 1) * ROWS, :] = ref[...]
    width = wa.shape[1]
    xh, z = index[0] // (Z * CORE), (index[0] // CORE) % Z
    slots = [((xh + dx) % XH) * Z + (z + Z - dz) % Z for dx in range(XH) for dz in (0,) + FAR]
    for side, w in enumerate((wa, wb)):
        terms = jnp.dot(rows[...], w[...], preferred_element_type=jnp.float32).astype(jnp.bfloat16)
        for i in range(8):
            out[slots[i], :, side * width : (side + 1) * width] = terms[i * ROWS : (i + 1) * ROWS, :]


def sum_kernel(terms, mine, other, *, width):
    acc = terms[0].astype(jnp.float32)
    for i in range(1, terms.shape[0]):
        acc = acc + terms[i].astype(jnp.float32)
    acc = acc.astype(jnp.bfloat16)
    mine[...] = acc[:, :width]
    other[...] = acc[:, width:]


def call(kernel, outs, scratch=(), flops=0, **kwargs):
    return pl.pallas_call(
        kernel,
        out_shape=tuple(jax.ShapeDtypeStruct(s, d) for s, d in outs),
        scratch_shapes=list(scratch),
        compiler_params=pltpu.CompilerParams(vmem_limit_bytes=VMEM_LIMIT),
        cost_estimate=(
            pl.CostEstimate(flops=flops, bytes_accessed=0, transcendentals=0) if flops else None
        ),
        **kwargs,
    )


def shards(
    queries,
    question_keys,
    question_values,
    question_ids,
    live_rows,
    prefix_keys,
    prefix_values,
    out_weight,
):
    f32, bf16 = jnp.float32, jnp.bfloat16
    index = lax.axis_index("blk")
    core = index % CORE
    positions = prefix_keys.shape[0]
    vmem = pl.BlockSpec(memory_space=pltpu.VMEM)
    smem = pl.BlockSpec(memory_space=pltpu.SMEM)
    block_flops = 8 * LANES * positions * DH
    part = ((DH + EXTRA, LANES), bf16)
    ones_shape = (positions, 2 * DH)

    own_state = [((LANES, DH), f32), ((LANES, 2 * DH), f32)]
    state = [((3, LANES, DH), f32), ((3, LANES, 2 * DH), f32)]

    (kv,) = call(join_kernel, [((2 * positions, DH), bf16)])(prefix_keys, prefix_values)
    kv_x = moved(kv, xh=1)
    kv_c = moved(kv, c=1)
    q_z = [moved(queries, z=z) for z in FAR]
    row = jnp.arange(ROWS, dtype=jnp.int32)
    allowed = (question_ids[:, None] == question_ids[None, :]) & (row[None, :] <= row[:, None])
    bias = jnp.where(allowed, 0.0, FLOOR).astype(f32)
    scratch = [pltpu.VMEM(ones_shape, bf16)]
    own_top, own_total = call(own_kernel, own_state, scratch)(
        after(queries, q_z[0]), question_keys, question_values, bias, kv
    )
    top, total, rows = call(near_kernel, state + [((4, LANES, DH), bf16)], scratch)(
        *q_z, after(queries, own_top), kv
    )
    top, total = call(core_kernel, state, scratch)(rows, top, total, kv_c)

    kv_x, weight, top = lax.optimization_barrier((kv_x, out_weight, top))
    kv_xc = moved(kv_x, c=1)
    weight_c = moved(weight, c=1)
    pair = [pltpu.VMEM((2,) + ones_shape, bf16)]
    own_top, own_total = call(own_kernel_2, own_state, pair, flops=2 * block_flops)(
        rows, own_top, own_total, kv_c, kv_x
    )
    top = after(top, own_top)
    (p_far,) = call(functools.partial(far_kernel, owners=(2,)), [part], pair, flops=1)(
        rows, top, total, kv_x, kv_xc
    )
    p_next = call(functools.partial(far_kernel, owners=(0, 1)), [part] * 2, pair, flops=4 * block_flops)(
        rows, after(top, p_far), total, kv_x, kv_xc
    )
    back = [moved(p, z=-z) for p, z in zip((*p_next, p_far), FAR)]
    result, level = call(
        own_last_kernel, [((DH, LANES), f32), ((8, LANES), f32)], scratch, flops=1
    )(after(rows, *p_next), own_top, own_total, kv_xc, back[2])
    (att,) = call(
        merge_kernel, [((ROWS, GROUP * DH), bf16)], in_specs=[smem] + [vmem] * 4
    )(live_rows, result, level, *back[:2])

    held = [att] + [moved(att, z=z) for z in FAR]
    held = held + [moved(rows, xh=1) for rows in held]
    width = out_weight.shape[1]
    (terms,) = call(
        project_kernel,
        [((8, ROWS, CORE * width), bf16)],
        [pltpu.VMEM((8 * ROWS, GROUP * DH), bf16)],
        in_specs=[smem] + [vmem] * 10,
    )(index.reshape(1), *held, out_weight, weight_c)
    gathered = lax.all_to_all(terms, "head", 0, 0, tiled=True)
    mine, other = call(
        functools.partial(sum_kernel, width=width),
        [((ROWS, width), bf16), ((ROWS, width), bf16)],
    )(gathered)
    theirs = moved(other, c=1)
    return jnp.where(
        core == 0,
        jnp.concatenate([mine, theirs], axis=0),
        jnp.concatenate([theirs, mine], axis=0),
    )


def solution(mesh):
    return jax.shard_map(
        shards,
        mesh=mesh,
        in_specs=(
            P("blk", "head"),
            P("blk", "head"),
            P("blk", "head"),
            P("blk"),
            P("blk"),
            P("blk", "head"),
            P("blk", "head"),
            P("head", "blk"),
        ),
        out_specs=P("head", "blk"),
        check_vma=False,
    )
```

```python
import functools

import jax
import jax.numpy as jnp
from jax import lax
from jax.experimental import pallas as pl
from jax.experimental.pallas import tpu as pltpu
from jax.sharding import PartitionSpec as P

DH = 128
GROUP = 8
ROWS = 64
LANES = GROUP * ROWS
EXTRA = 16
SCALE = DH**-0.5 * 1.4426950408889634
FLOOR = -1e30
XH, Z, CORE = 2, 4, 2
VMEM_LIMIT = 30 << 20
FAR = (1, 3, 2)


def moved(array, xh=0, z=0, c=0):
    pairs = []
    for i in range(XH * Z * CORE):
        a, b, d = i // (Z * CORE), (i // CORE) % Z, i % CORE
        to = (((a + xh) % XH) * Z + (b + z) % Z) * CORE + (d + c) % CORE
        pairs.append((i, to))
    return lax.ppermute(array, "blk", pairs)


def after(array, *others):
    return lax.optimization_barrier((array, *others))[0]


def scores_of(queries, keys):
    return lax.dot_general(
        queries, keys, (((1,), (1,)), ((), ())), preferred_element_type=jnp.float32
    )


def wide(column, width):
    return jnp.concatenate([column] * (width // column.shape[1]), axis=1)


def add_block(top, total, scores, values):
    best = jnp.maximum(top, jnp.max(scores, axis=1, keepdims=True) * SCALE)
    keys = scores.shape[1]
    at = wide(best, keys) if keys >= DH else best[:, :keys]
    weights = jnp.exp2(scores * SCALE - at).astype(jnp.bfloat16)
    part = jnp.dot(weights, values, preferred_element_type=jnp.float32)
    return best, total * wide(jnp.exp2(top - best), 2 * DH) + part


def stacked(ref):
    return jnp.concatenate([ref[:, h * DH : (h + 1) * DH] for h in range(GROUP)], axis=0)


def join_kernel(k, v, whole, first, second):
    size = k.shape[0]
    half = size // 2
    whole[:size, :] = k[...]
    whole[size:, :] = v[...]
    for i, kv in enumerate((first, second)):
        kv[:half, :] = k[i * half : (i + 1) * half, :]
        kv[half:, :] = v[i * half : (i + 1) * half, :]


def split(parts, keys, values):
    at = 0
    for kv in parts:
        size = kv.shape[0] // 2
        keys[at : at + size, :] = kv[:size, :]
        values[at : at + size, :DH] = kv[size:, :]
        at += size
    values[:, DH:] = jnp.ones((at, DH), values.dtype)


def finish(top, total):
    denominator = total[:, DH:]
    result = (total[:, :DH] / denominator).T
    level = (top + jnp.log2(denominator)).T[:1]
    return result, level


def packed(result, level):
    high = level.astype(jnp.bfloat16).astype(jnp.float32)
    mid = (level - high).astype(jnp.bfloat16).astype(jnp.float32)
    low = level - high - mid
    row = lax.broadcasted_iota(jnp.int32, (EXTRA, LANES), 0)
    pieces = jnp.where(row == 0, high, jnp.where(row == 1, mid, low))
    return jnp.concatenate([result, pieces], axis=0).astype(jnp.bfloat16)


def unpacked(block):
    pieces = block[DH:, :].astype(jnp.float32)
    return block[:DH, :].astype(jnp.float32), (pieces[0:1] + pieces[1:2]) + pieces[2:3]


def merged(parts):
    best = functools.reduce(jnp.maximum, [level for _, level in parts])
    numerator, denominator = 0.0, 0.0
    for result, level in parts:
        share = jnp.exp2(level - best)
        numerator = numerator + result * share
        denominator = denominator + share
    return numerator / denominator, best + jnp.log2(denominator)


def run(tasks, states):
    def scores_at(i):
        _, rows, keys, _ = tasks[i]
        return scores_of(rows[...], keys[...])

    ahead = scores_at(0)
    for i, (owner, _, _, values) in enumerate(tasks):
        scores = ahead
        if i + 1 < len(tasks):
            ahead = scores_at(i + 1)
        states[owner] = add_block(*states[owner], scores, values[...])
    return states


def empty():
    return (
        jnp.full((LANES, DH), FLOOR, jnp.float32),
        jnp.zeros((LANES, 2 * DH), jnp.float32),
    )


def own_kernel(q, qk, qv, bias, kv, top_out, total_out, k, values):
    split((kv,), k, values)
    rows = stacked(q)
    scores = scores_of(rows, qk[...]) + jnp.concatenate([bias[...]] * GROUP, axis=0)
    block = scores_of(rows, k[...])
    top, total = add_block(
        *empty(),
        scores,
        jnp.concatenate([qv[...], jnp.ones((ROWS, DH), jnp.bfloat16)], axis=1),
    )
    top_out[...], total_out[...] = add_block(top, total, block, values[...])


def near_kernel(q0, q1, q2, q, kv, top_out, total_out, rows, k, values):
    split((kv,), k, values)
    for i, ref in enumerate((q0, q1, q2, q)):
        rows[i] = stacked(ref)
    states = run([(i, rows.at[i], k, values) for i in range(3)], [empty() for _ in range(3)])
    for i, (top, total) in enumerate(states):
        top_out[i], total_out[i] = top, total


def others_kernel(rows, top_in, total_in, *refs):
    *parts, top_out, total_out, k, values = refs
    split(parts, k, values)
    states = [(top_in[i], total_in[i]) for i in range(3)]
    states = run([(i, rows.at[i], k, values) for i in range(3)], states)
    for i, (top, total) in enumerate(states):
        top_out[i], total_out[i] = top, total


def own_kernel_2(rows, top, total, kv, half, other_half, top_out, total_out, k, values):
    split((kv,), k.at[0], values.at[0])
    split((half, other_half), k.at[1], values.at[1])
    tasks = [(0, rows.at[3], k.at[i], values.at[i]) for i in range(2)]
    top_out[...], total_out[...] = run(tasks, [(top[...], total[...])])[0]


def last_kernel(rows, top, total, half, other_half, *refs, owners):
    *outs, k, values = refs
    split((half, other_half), k, values)
    tasks = [(i, rows.at[owner], k, values) for i, owner in enumerate(owners)]
    states = run(tasks, [(top[owner], total[owner]) for owner in owners])
    for state, out in zip(states, outs):
        out[...] = packed(*finish(*state))


def own_last_kernel(rows, top, total, half, other_half, r2, result_ref, level_ref, k, values):
    split((half, other_half), k, values)
    states = run([(0, rows.at[3], k, values)], [(top[...], total[...])])
    result, level = merged([finish(*states[0]), unpacked(r2)])
    result_ref[...] = result
    level_ref[...] = jnp.broadcast_to(level, (8, LANES))


def merge_kernel(live, result, level, r0, r1, att):
    parts = [(result[...], level[:1])] + [unpacked(r) for r in (r0, r1)]
    whole, _ = merged(parts)
    slot = lax.broadcasted_iota(jnp.int32, (1, LANES), 1) % ROWS
    rows = jnp.where(slot < live[0], whole, 0.0).T.astype(jnp.bfloat16)
    for head in range(GROUP):
        att[:, head * DH : (head + 1) * DH] = rows[head * ROWS : (head + 1) * ROWS, :]


def project_kernel(index, a0, a1, a2, a3, a4, a5, a6, a7, wa, wb, out, rows):
    for i, ref in enumerate((a0, a1, a2, a3, a4, a5, a6, a7)):
        rows[i * ROWS : (i + 1) * ROWS, :] = ref[...]
    width = wa.shape[1]
    xh, z = index[0] // (Z * CORE), (index[0] // CORE) % Z
    slots = [((xh + dx) % XH) * Z + (z + Z - dz) % Z for dx in range(XH) for dz in (0,) + FAR]
    for side, w in enumerate((wa, wb)):
        terms = jnp.dot(rows[...], w[...], preferred_element_type=jnp.float32).astype(jnp.bfloat16)
        for i in range(8):
            out[slots[i], :, side * width : (side + 1) * width] = terms[i * ROWS : (i + 1) * ROWS, :]


def sum_kernel(terms, mine, other, *, width):
    acc = terms[0].astype(jnp.float32)
    for i in range(1, terms.shape[0]):
        acc = acc + terms[i].astype(jnp.float32)
    acc = acc.astype(jnp.bfloat16)
    mine[...] = acc[:, :width]
    other[...] = acc[:, width:]


def call(kernel, outs, scratch=(), flops=0, **kwargs):
    return pl.pallas_call(
        kernel,
        out_shape=tuple(jax.ShapeDtypeStruct(s, d) for s, d in outs),
        scratch_shapes=list(scratch),
        compiler_params=pltpu.CompilerParams(vmem_limit_bytes=VMEM_LIMIT),
        cost_estimate=(
            pl.CostEstimate(flops=flops, bytes_accessed=0, transcendentals=0) if flops else None
        ),
        **kwargs,
    )


def shards(
    queries,
    question_keys,
    question_values,
    question_ids,
    live_rows,
    prefix_keys,
    prefix_values,
    out_weight,
):
    f32, bf16 = jnp.float32, jnp.bfloat16
    index = lax.axis_index("blk")
    core = index % CORE
    positions = prefix_keys.shape[0]
    vmem = pl.BlockSpec(memory_space=pltpu.VMEM)
    smem = pl.BlockSpec(memory_space=pltpu.SMEM)
    block_flops = 8 * LANES * positions * DH
    part = ((DH + EXTRA, LANES), bf16)
    ones_shape = (positions, 2 * DH)

    own_state = [((LANES, DH), f32), ((LANES, 2 * DH), f32)]
    state = [((3, LANES, DH), f32), ((3, LANES, 2 * DH), f32)]

    kv, *halves = call(
        join_kernel, [((2 * positions, DH), bf16)] + [((positions, DH), bf16)] * 2
    )(prefix_keys, prefix_values)
    x0, x1 = [moved(half, xh=1) for half in halves]
    kv_c = moved(kv, c=1)
    q_z = [moved(queries, z=z) for z in FAR]
    row = jnp.arange(ROWS, dtype=jnp.int32)
    allowed = (question_ids[:, None] == question_ids[None, :]) & (row[None, :] <= row[:, None])
    bias = jnp.where(allowed, 0.0, FLOOR).astype(f32)
    scratch = [pltpu.VMEM((positions, DH), bf16), pltpu.VMEM(ones_shape, bf16)]
    own_top, own_total = call(own_kernel, own_state, scratch)(
        after(queries, *q_z), question_keys, question_values, bias, kv
    )
    top, total, rows = call(near_kernel, state + [((4, LANES, DH), bf16)], scratch)(
        *q_z, after(queries, own_top), kv
    )
    x0 = after(x0, own_top)
    xc0 = moved(x0, c=1)
    top, total = call(others_kernel, state, scratch, flops=1)(rows, top, total, kv_c)
    top, total = call(others_kernel, state, scratch, flops=1)(rows, top, total, x0, xc0)

    x1, weight, top = lax.optimization_barrier((x1, out_weight, top))
    xc1 = moved(x1, c=1)
    weight_c = moved(weight, c=1)
    pair = [pltpu.VMEM((2, positions, DH), bf16), pltpu.VMEM((2,) + ones_shape, bf16)]
    own_top, own_total = call(own_kernel_2, own_state, pair, flops=2 * block_flops)(
        after(rows, x1), own_top, own_total, kv_c, x0, xc0
    )
    top = after(top, own_top)
    (p_far,) = call(functools.partial(last_kernel, owners=(2,)), [part], scratch, flops=1)(
        rows, top, total, x1, xc1
    )
    p_next = call(
        functools.partial(last_kernel, owners=(0, 1)), [part] * 2, scratch, flops=4 * block_flops
    )(rows, after(top, p_far), total, x1, xc1)
    back = [moved(p, z=-z) for p, z in zip((*p_next, p_far), FAR)]
    result, level = call(
        own_last_kernel, [((DH, LANES), f32), ((8, LANES), f32)], scratch, flops=1
    )(after(rows, *p_next), own_top, own_total, x1, xc1, back[2])
    (att,) = call(
        merge_kernel, [((ROWS, GROUP * DH), bf16)], in_specs=[smem] + [vmem] * 4
    )(live_rows, result, level, *back[:2])

    held = [att] + [moved(att, z=z) for z in FAR]
    held = held + [moved(rows, xh=1) for rows in held]
    width = out_weight.shape[1]
    (terms,) = call(
        project_kernel,
        [((8, ROWS, CORE * width), bf16)],
        [pltpu.VMEM((8 * ROWS, GROUP * DH), bf16)],
        in_specs=[smem] + [vmem] * 10,
    )(index.reshape(1), *held, out_weight, weight_c)
    gathered = lax.all_to_all(terms, "head", 0, 0, tiled=True)
    mine, other = call(
        functools.partial(sum_kernel, width=width),
        [((ROWS, width), bf16), ((ROWS, width), bf16)],
    )(gathered)
    theirs = moved(other, c=1)
    return jnp.where(
        core == 0,
        jnp.concatenate([mine, theirs], axis=0),
        jnp.concatenate([theirs, mine], axis=0),
    )


def solution(mesh):
    return jax.shard_map(
        shards,
        mesh=mesh,
        in_specs=(
            P("blk", "head"),
            P("blk", "head"),
            P("blk", "head"),
            P("blk"),
            P("blk"),
            P("blk", "head"),
            P("blk", "head"),
            P("head", "blk"),
        ),
        out_specs=P("head", "blk"),
        check_vma=False,
    )
```

```python
import functools

import jax
import jax.numpy as jnp
from jax import lax
from jax.experimental import pallas as pl
from jax.experimental.pallas import tpu as pltpu
from jax.sharding import PartitionSpec as P

DH = 128
GROUP = 8
ROWS = 64
LANES = GROUP * ROWS
EXTRA = 16
SCALE = DH**-0.5 * 1.4426950408889634
FLOOR = -1e30
XH, Z, CORE = 2, 4, 2
VMEM_LIMIT = 30 << 20
FAR = (1, 3, 2)


def moved(array, xh=0, z=0, c=0):
    pairs = []
    for i in range(XH * Z * CORE):
        a, b, d = i // (Z * CORE), (i // CORE) % Z, i % CORE
        to = (((a + xh) % XH) * Z + (b + z) % Z) * CORE + (d + c) % CORE
        pairs.append((i, to))
    return lax.ppermute(array, "blk", pairs)


def after(array, *others):
    return lax.optimization_barrier((array, *others))[0]


def scores_of(queries, keys):
    return lax.dot_general(
        queries, keys, (((1,), (1,)), ((), ())), preferred_element_type=jnp.float32
    )


def wide(column, width):
    return jnp.concatenate([column] * (width // column.shape[1]), axis=1)


def add_block(top, total, scores, values):
    best = jnp.maximum(top, jnp.max(scores, axis=1, keepdims=True) * SCALE)
    keys = scores.shape[1]
    at = wide(best, keys) if keys >= DH else best[:, :keys]
    weights = jnp.exp2(scores * SCALE - at).astype(jnp.bfloat16)
    part = jnp.dot(weights, values, preferred_element_type=jnp.float32)
    return best, total * wide(jnp.exp2(top - best), 2 * DH) + part


def stacked(ref):
    return jnp.concatenate([ref[:, h * DH : (h + 1) * DH] for h in range(GROUP)], axis=0)


def join_kernel(k, v, whole, first, second):
    size = k.shape[0]
    at = 0
    for kv in (whole, first, second):
        count = kv.shape[0] // 2
        kv[:count, :] = k[at : at + count, :]
        kv[count:, :] = v[at : at + count, :]
        at = (at + count) % size


def split(parts, keys, values):
    at = 0
    for kv in parts:
        size = kv.shape[0] // 2
        keys[at : at + size, :] = kv[:size, :]
        values[at : at + size, :DH] = kv[size:, :]
        at += size
    values[:, DH:] = jnp.ones((at, DH), values.dtype)


def finish(top, total):
    denominator = total[:, DH:]
    result = (total[:, :DH] / denominator).T
    level = (top + jnp.log2(denominator)).T[:1]
    return result, level


def packed(result, level):
    high = level.astype(jnp.bfloat16).astype(jnp.float32)
    mid = (level - high).astype(jnp.bfloat16).astype(jnp.float32)
    low = level - high - mid
    row = lax.broadcasted_iota(jnp.int32, (EXTRA, LANES), 0)
    pieces = jnp.where(row == 0, high, jnp.where(row == 1, mid, low))
    return jnp.concatenate([result, pieces], axis=0).astype(jnp.bfloat16)


def unpacked(block):
    pieces = block[DH:, :].astype(jnp.float32)
    return block[:DH, :].astype(jnp.float32), (pieces[0:1] + pieces[1:2]) + pieces[2:3]


def merged(parts):
    best = functools.reduce(jnp.maximum, [level for _, level in parts])
    numerator, denominator = 0.0, 0.0
    for result, level in parts:
        share = jnp.exp2(level - best)
        numerator = numerator + result * share
        denominator = denominator + share
    return numerator / denominator, best + jnp.log2(denominator)


def run(tasks, states):
    def scores_at(i):
        _, rows, keys, _ = tasks[i]
        return scores_of(rows[...], keys[...])

    ahead = scores_at(0)
    for i, (owner, _, _, values) in enumerate(tasks):
        scores = ahead
        if i + 1 < len(tasks):
            ahead = scores_at(i + 1)
        states[owner] = add_block(*states[owner], scores, values[...])
    return states


def empty():
    return (
        jnp.full((LANES, DH), FLOOR, jnp.float32),
        jnp.zeros((LANES, 2 * DH), jnp.float32),
    )


def own_kernel(q, qk, qv, bias, kv, top_out, total_out, k, values):
    split((kv,), k, values)
    rows = stacked(q)
    scores = scores_of(rows, qk[...]) + jnp.concatenate([bias[...]] * GROUP, axis=0)
    block = scores_of(rows, k[...])
    top, total = add_block(
        *empty(),
        scores,
        jnp.concatenate([qv[...], jnp.ones((ROWS, DH), jnp.bfloat16)], axis=1),
    )
    top_out[...], total_out[...] = add_block(top, total, block, values[...])


def near_kernel(q0, q1, q2, q, kv, top_out, total_out, rows, k, values):
    split((kv,), k, values)
    for i, ref in enumerate((q0, q1, q2, q)):
        rows[i] = stacked(ref)
    states = run([(i, rows.at[i], k, values) for i in range(3)], [empty() for _ in range(3)])
    for i, (top, total) in enumerate(states):
        top_out[i], total_out[i] = top, total


def others_kernel(rows, top_in, total_in, *refs):
    *parts, top_out, total_out, k, values = refs
    split(parts, k, values)
    states = [(top_in[i], total_in[i]) for i in range(3)]
    states = run([(i, rows.at[i], k, values) for i in range(3)], states)
    for i, (top, total) in enumerate(states):
        top_out[i], total_out[i] = top, total


def own_kernel_2(rows, top, total, kv, half, other_half, top_out, total_out, k0, v0, k1, v1):
    split((kv,), k0, v0)
    split((half, other_half), k1, v1)
    tasks = [(0, rows.at[3], k0, v0), (0, rows.at[3], k1, v1)]
    top_out[...], total_out[...] = run(tasks, [(top[...], total[...])])[0]


def last_kernel(rows, top, total, half, other_half, *refs, owners):
    *outs, k, values = refs
    split((half, other_half), k, values)
    tasks = [(i, rows.at[owner], k, values) for i, owner in enumerate(owners)]
    states = run(tasks, [(top[owner], total[owner]) for owner in owners])
    for state, out in zip(states, outs):
        out[...] = packed(*finish(*state))


def own_last_kernel(rows, top, total, half, other_half, r2, result_ref, level_ref, k, values):
    split((half, other_half), k, values)
    states = run([(0, rows.at[3], k, values)], [(top[...], total[...])])
    result, level = merged([finish(*states[0]), unpacked(r2)])
    result_ref[...] = result
    level_ref[...] = jnp.broadcast_to(level, (8, LANES))


def merge_kernel(live, result, level, r0, r1, att):
    parts = [(result[...], level[:1])] + [unpacked(r) for r in (r0, r1)]
    whole, _ = merged(parts)
    slot = lax.broadcasted_iota(jnp.int32, (1, LANES), 1) % ROWS
    rows = jnp.where(slot < live[0], whole, 0.0).T.astype(jnp.bfloat16)
    for head in range(GROUP):
        att[:, head * DH : (head + 1) * DH] = rows[head * ROWS : (head + 1) * ROWS, :]


def project_kernel(index, a0, a1, a2, a3, a4, a5, a6, a7, wa, wb, out, rows):
    for i, ref in enumerate((a0, a1, a2, a3, a4, a5, a6, a7)):
        rows[i * ROWS : (i + 1) * ROWS, :] = ref[...]
    width = wa.shape[1]
    xh, z = index[0] // (Z * CORE), (index[0] // CORE) % Z
    slots = [((xh + dx) % XH) * Z + (z + Z - dz) % Z for dx in range(XH) for dz in (0,) + FAR]
    for side, w in enumerate((wa, wb)):
        terms = jnp.dot(rows[...], w[...], preferred_element_type=jnp.float32).astype(jnp.bfloat16)
        for i in range(8):
            out[slots[i], :, side * width : (side + 1) * width] = terms[i * ROWS : (i + 1) * ROWS, :]


def sum_kernel(terms, mine, other, *, width):
    acc = terms[0].astype(jnp.float32)
    for i in range(1, terms.shape[0]):
        acc = acc + terms[i].astype(jnp.float32)
    acc = acc.astype(jnp.bfloat16)
    mine[...] = acc[:, :width]
    other[...] = acc[:, width:]


def call(kernel, outs, scratch=(), flops=0, **kwargs):
    return pl.pallas_call(
        kernel,
        out_shape=tuple(jax.ShapeDtypeStruct(s, d) for s, d in outs),
        scratch_shapes=list(scratch),
        compiler_params=pltpu.CompilerParams(vmem_limit_bytes=VMEM_LIMIT),
        cost_estimate=(
            pl.CostEstimate(flops=flops, bytes_accessed=0, transcendentals=0) if flops else None
        ),
        **kwargs,
    )


def shards(
    queries,
    question_keys,
    question_values,
    question_ids,
    live_rows,
    prefix_keys,
    prefix_values,
    out_weight,
):
    f32, bf16 = jnp.float32, jnp.bfloat16
    index = lax.axis_index("blk")
    core = index % CORE
    positions = prefix_keys.shape[0]
    vmem = pl.BlockSpec(memory_space=pltpu.VMEM)
    smem = pl.BlockSpec(memory_space=pltpu.SMEM)
    block_flops = 8 * LANES * positions * DH
    part = ((DH + EXTRA, LANES), bf16)

    own_state = [((LANES, DH), f32), ((LANES, 2 * DH), f32)]
    state = [((3, LANES, DH), f32), ((3, LANES, 2 * DH), f32)]

    early = positions * 7 // 16
    late = positions - early
    kv, *halves = call(
        join_kernel, [((2 * size, DH), bf16) for size in (positions, early, late)]
    )(prefix_keys, prefix_values)
    x0, x1 = [moved(half, xh=1) for half in halves]
    kv_c = moved(kv, c=1)
    q_z = [moved(queries, z=z) for z in FAR]
    row = jnp.arange(ROWS, dtype=jnp.int32)
    allowed = (question_ids[:, None] == question_ids[None, :]) & (row[None, :] <= row[:, None])
    bias = jnp.where(allowed, 0.0, FLOOR).astype(f32)
    def scratch(*sizes):
        return [pltpu.VMEM((size, width), bf16) for size in sizes for width in (DH, 2 * DH)]

    own_top, own_total = call(own_kernel, own_state, scratch(positions))(
        queries, question_keys, question_values, after(bias, q_z[0]), kv
    )
    top, total, rows = call(near_kernel, state + [((4, LANES, DH), bf16)], scratch(positions))(
        *q_z, queries, kv
    )
    x0 = after(x0, own_top, *q_z)
    xc0 = moved(x0, c=1)
    top, total = call(others_kernel, state, scratch(positions), flops=1)(rows, top, total, kv_c)
    top, total = call(others_kernel, state, scratch(2 * early), flops=1)(rows, top, total, x0, xc0)

    x1, weight, top = lax.optimization_barrier((x1, out_weight, top))
    xc1 = moved(x1, c=1)
    weight_c = moved(weight, c=1)
    own_top, own_total = call(own_kernel_2, own_state, scratch(positions, 2 * early), flops=2 * block_flops)(
        after(rows, x1), own_top, own_total, kv_c, x0, xc0
    )
    top = after(top, own_top)
    (p_far,) = call(functools.partial(last_kernel, owners=(2,)), [part], scratch(2 * late), flops=1)(
        rows, top, total, x1, xc1
    )
    p_next = call(
        functools.partial(last_kernel, owners=(0, 1)), [part] * 2, scratch(2 * late), flops=4 * block_flops
    )(rows, after(top, p_far), total, x1, xc1)
    back = [moved(p, z=-z) for p, z in zip((*p_next, p_far), FAR)]
    result, level = call(
        own_last_kernel, [((DH, LANES), f32), ((8, LANES), f32)], scratch(2 * late), flops=1
    )(after(rows, *p_next), own_top, own_total, x1, xc1, back[2])
    (att,) = call(
        merge_kernel, [((ROWS, GROUP * DH), bf16)], in_specs=[smem] + [vmem] * 4
    )(live_rows, result, level, *back[:2])

    held = [att] + [moved(att, z=z) for z in FAR]
    held = held + [moved(rows, xh=1) for rows in held]
    width = out_weight.shape[1]
    (terms,) = call(
        project_kernel,
        [((8, ROWS, CORE * width), bf16)],
        [pltpu.VMEM((8 * ROWS, GROUP * DH), bf16)],
        in_specs=[smem] + [vmem] * 10,
    )(index.reshape(1), *held, out_weight, weight_c)
    gathered = lax.all_to_all(terms, "head", 0, 0, tiled=True)
    mine, other = call(
        functools.partial(sum_kernel, width=width),
        [((ROWS, width), bf16), ((ROWS, width), bf16)],
    )(gathered)
    theirs = moved(other, c=1)
    return jnp.where(
        core == 0,
        jnp.concatenate([mine, theirs], axis=0),
        jnp.concatenate([theirs, mine], axis=0),
    )


def solution(mesh):
    return jax.shard_map(
        shards,
        mesh=mesh,
        in_specs=(
            P("blk", "head"),
            P("blk", "head"),
            P("blk", "head"),
            P("blk"),
            P("blk"),
            P("blk", "head"),
            P("blk", "head"),
            P("head", "blk"),
        ),
        out_specs=P("head", "blk"),
        check_vma=False,
    )
```

```python
import functools

import jax
import jax.numpy as jnp
from jax import lax
from jax.experimental import pallas as pl
from jax.experimental.pallas import tpu as pltpu
from jax.sharding import PartitionSpec as P

DH = 128
GROUP = 8
ROWS = 64
LANES = GROUP * ROWS
EXTRA = 16
SCALE = DH**-0.5 * 1.4426950408889634
FLOOR = -1e30
XH, Z, CORE = 2, 4, 2
VMEM_LIMIT = 30 << 20
FAR = (1, 3, 2)


def moved(array, xh=0, z=0, c=0):
    pairs = []
    for i in range(XH * Z * CORE):
        a, b, d = i // (Z * CORE), (i // CORE) % Z, i % CORE
        to = (((a + xh) % XH) * Z + (b + z) % Z) * CORE + (d + c) % CORE
        pairs.append((i, to))
    return lax.ppermute(array, "blk", pairs)


def after(array, *others):
    return lax.optimization_barrier((array, *others))[0]


def scores_of(queries, keys):
    return lax.dot_general(
        queries, keys, (((1,), (1,)), ((), ())), preferred_element_type=jnp.float32
    )


def wide(column, width):
    return jnp.concatenate([column] * (width // column.shape[1]), axis=1)


def add_block(top, total, scores, values):
    best = jnp.maximum(top, jnp.max(scores, axis=1, keepdims=True) * SCALE)
    keys = scores.shape[1]
    at = wide(best, keys) if keys >= DH else best[:, :keys]
    weights = jnp.exp2(scores * SCALE - at).astype(jnp.bfloat16)
    part = jnp.dot(weights, values, preferred_element_type=jnp.float32)
    return best, total * wide(jnp.exp2(top - best), 2 * DH) + part


def stacked(ref):
    return jnp.concatenate([ref[:, h * DH : (h + 1) * DH] for h in range(GROUP)], axis=0)


def join_kernel(k, v, whole, first, second):
    size = k.shape[0]
    at = 0
    for kv in (whole, first, second):
        count = kv.shape[0] // 2
        kv[:count, :] = k[at : at + count, :]
        kv[count:, :] = v[at : at + count, :]
        at = (at + count) % size


def split(parts, keys, values):
    at = 0
    for kv in parts:
        size = kv.shape[0] // 2
        keys[at : at + size, :] = kv[:size, :]
        values[at : at + size, :DH] = kv[size:, :]
        at += size
    values[:, DH:] = jnp.ones((at, DH), values.dtype)


def finish(top, total):
    denominator = total[:, DH:]
    result = (total[:, :DH] / denominator).T
    level = (top + jnp.log2(denominator)).T[:1]
    return result, level


def packed(result, level):
    high = level.astype(jnp.bfloat16).astype(jnp.float32)
    mid = (level - high).astype(jnp.bfloat16).astype(jnp.float32)
    low = level - high - mid
    row = lax.broadcasted_iota(jnp.int32, (EXTRA, LANES), 0)
    pieces = jnp.where(row == 0, high, jnp.where(row == 1, mid, low))
    return jnp.concatenate([result, pieces], axis=0).astype(jnp.bfloat16)


def unpacked(block):
    pieces = block[DH:, :].astype(jnp.float32)
    return block[:DH, :].astype(jnp.float32), (pieces[0:1] + pieces[1:2]) + pieces[2:3]


def merged(parts):
    best = functools.reduce(jnp.maximum, [level for _, level in parts])
    numerator, denominator = 0.0, 0.0
    for result, level in parts:
        share = jnp.exp2(level - best)
        numerator = numerator + result * share
        denominator = denominator + share
    return numerator / denominator, best + jnp.log2(denominator)


def run(tasks, states):
    def scores_at(i):
        _, rows, keys, _ = tasks[i]
        return scores_of(rows[...], keys[...])

    ahead = scores_at(0)
    for i, (owner, _, _, values) in enumerate(tasks):
        scores = ahead
        if i + 1 < len(tasks):
            ahead = scores_at(i + 1)
        states[owner] = add_block(*states[owner], scores, values[...])
    return states


def empty():
    return (
        jnp.full((LANES, DH), FLOOR, jnp.float32),
        jnp.zeros((LANES, 2 * DH), jnp.float32),
    )


def own_kernel(q, qkv, bias, kv, top_out, total_out, k, values):
    split((kv,), k, values)
    rows = stacked(q)
    scores = scores_of(rows, qkv[:ROWS, :]) + jnp.concatenate([bias[...]] * GROUP, axis=0)
    block = scores_of(rows, k[...])
    top, total = add_block(
        *empty(),
        scores,
        jnp.concatenate([qkv[ROWS:, :], jnp.ones((ROWS, DH), jnp.bfloat16)], axis=1),
    )
    top_out[...], total_out[...] = add_block(top, total, block, values[...])


def near_kernel(q0, q1, q2, q, kv, kv_c, top_out, total_out, rows, k0, v0, k1, v1):
    split((kv,), k0, v0)
    split((kv_c,), k1, v1)
    for i, ref in enumerate((q0, q1, q2, q)):
        rows[i] = stacked(ref)
    tasks = [(i, rows.at[i], k, v) for k, v in ((k0, v0), (k1, v1)) for i in range(3)]
    for i, (top, total) in enumerate(run(tasks, [empty() for _ in range(3)])):
        top_out[i], total_out[i] = top, total


def others_kernel(rows, top_in, total_in, *refs):
    *parts, top_out, total_out, k, values = refs
    split(parts, k, values)
    states = [(top_in[i], total_in[i]) for i in range(3)]
    states = run([(i, rows.at[i], k, values) for i in range(3)], states)
    for i, (top, total) in enumerate(states):
        top_out[i], total_out[i] = top, total


def own_kernel_2(rows, top, total, kv, half, other_half, top_out, total_out, k0, v0, k1, v1):
    split((kv,), k0, v0)
    split((half, other_half), k1, v1)
    tasks = [(0, rows.at[3], k0, v0), (0, rows.at[3], k1, v1)]
    top_out[...], total_out[...] = run(tasks, [(top[...], total[...])])[0]


def last_kernel(rows, top, total, half, other_half, *refs, owners):
    *outs, k, values = refs
    split((half, other_half), k, values)
    tasks = [(i, rows.at[owner], k, values) for i, owner in enumerate(owners)]
    states = run(tasks, [(top[owner], total[owner]) for owner in owners])
    for state, out in zip(states, outs):
        out[...] = packed(*finish(*state))


def own_last_kernel(rows, top, total, half, other_half, r2, result_ref, level_ref, k, values):
    split((half, other_half), k, values)
    states = run([(0, rows.at[3], k, values)], [(top[...], total[...])])
    result, level = merged([finish(*states[0]), unpacked(r2)])
    result_ref[...] = result
    level_ref[...] = jnp.broadcast_to(level, (8, LANES))


def merge_kernel(live, result, level, r0, r1, att):
    parts = [(result[...], level[:1])] + [unpacked(r) for r in (r0, r1)]
    whole, _ = merged(parts)
    slot = lax.broadcasted_iota(jnp.int32, (1, LANES), 1) % ROWS
    rows = jnp.where(slot < live[0], whole, 0.0).T.astype(jnp.bfloat16)
    for head in range(GROUP):
        att[:, head * DH : (head + 1) * DH] = rows[head * ROWS : (head + 1) * ROWS, :]


def project_kernel(index, a0, a1, a2, a3, a4, a5, a6, a7, wa, wb, out, rows):
    for i, ref in enumerate((a0, a1, a2, a3, a4, a5, a6, a7)):
        rows[i * ROWS : (i + 1) * ROWS, :] = ref[...]
    width = wa.shape[1]
    xh, z = index[0] // (Z * CORE), (index[0] // CORE) % Z
    slots = [((xh + dx) % XH) * Z + (z + Z - dz) % Z for dx in range(XH) for dz in (0,) + FAR]
    for side, w in enumerate((wa, wb)):
        terms = jnp.dot(rows[...], w[...], preferred_element_type=jnp.float32).astype(jnp.bfloat16)
        for i in range(8):
            out[slots[i], :, side * width : (side + 1) * width] = terms[i * ROWS : (i + 1) * ROWS, :]


def sum_kernel(terms, mine, other, *, width):
    acc = terms[0].astype(jnp.float32)
    for i in range(1, terms.shape[0]):
        acc = acc + terms[i].astype(jnp.float32)
    acc = acc.astype(jnp.bfloat16)
    mine[...] = acc[:, :width]
    other[...] = acc[:, width:]


def call(kernel, outs, scratch=(), flops=0, **kwargs):
    return pl.pallas_call(
        kernel,
        out_shape=tuple(jax.ShapeDtypeStruct(s, d) for s, d in outs),
        scratch_shapes=list(scratch),
        compiler_params=pltpu.CompilerParams(vmem_limit_bytes=VMEM_LIMIT),
        cost_estimate=(
            pl.CostEstimate(flops=flops, bytes_accessed=0, transcendentals=0) if flops else None
        ),
        **kwargs,
    )


def shards(
    queries,
    question_keys,
    question_values,
    question_ids,
    live_rows,
    prefix_keys,
    prefix_values,
    out_weight,
):
    f32, bf16 = jnp.float32, jnp.bfloat16
    index = lax.axis_index("blk")
    core = index % CORE
    positions = prefix_keys.shape[0]
    vmem = pl.BlockSpec(memory_space=pltpu.VMEM)
    smem = pl.BlockSpec(memory_space=pltpu.SMEM)
    block_flops = 8 * LANES * positions * DH
    part = ((DH + EXTRA, LANES), bf16)

    own_state = [((LANES, DH), f32), ((LANES, 2 * DH), f32)]
    state = [((3, LANES, DH), f32), ((3, LANES, 2 * DH), f32)]

    early = positions * 7 // 16
    late = positions - early
    kv, *halves = call(
        join_kernel, [((2 * size, DH), bf16) for size in (positions, early, late)]
    )(prefix_keys, prefix_values)
    x0, x1 = [moved(half, xh=1) for half in halves]
    kv_c = moved(kv, c=1)
    q_z = [moved(queries, z=z) for z in FAR]
    row = jnp.arange(ROWS, dtype=jnp.int32)
    allowed = (question_ids[:, None] == question_ids[None, :]) & (row[None, :] <= row[:, None])
    bias = jnp.where(allowed, 0.0, FLOOR).astype(f32)
    def scratch(*sizes):
        return [pltpu.VMEM((size, width), bf16) for size in sizes for width in (DH, 2 * DH)]

    own_top, own_total = call(own_kernel, own_state, scratch(positions))(
        queries, jnp.concatenate([question_keys, question_values]), bias, after(kv, q_z[0])
    )
    x0 = after(x0, own_top, *q_z)
    xc0 = moved(x0, c=1)
    top, total, rows = call(
        near_kernel, state + [((4, LANES, DH), bf16)], scratch(positions, positions), flops=1
    )(*q_z, queries, kv, kv_c)
    top, total = call(others_kernel, state, scratch(2 * early), flops=1)(rows, top, total, x0, xc0)

    x1, weight, top = lax.optimization_barrier((x1, out_weight, top))
    xc1 = moved(x1, c=1)
    weight_c = moved(weight, c=1)
    own_top, own_total = call(
        own_kernel_2, own_state, scratch(positions, 2 * early), flops=2 * block_flops
    )(after(rows, x1), own_top, own_total, kv_c, x0, xc0)
    top = after(top, own_top)
    (p_far,) = call(functools.partial(last_kernel, owners=(2,)), [part], scratch(2 * late), flops=1)(
        rows, top, total, x1, xc1
    )
    p_next = call(
        functools.partial(last_kernel, owners=(0, 1)), [part] * 2, scratch(2 * late), flops=4 * block_flops
    )(rows, after(top, p_far), total, x1, xc1)
    back = [moved(p, z=-z) for p, z in zip((*p_next, p_far), FAR)]
    result, level = call(
        own_last_kernel, [((DH, LANES), f32), ((8, LANES), f32)], scratch(2 * late), flops=1
    )(after(rows, *p_next), own_top, own_total, x1, xc1, back[2])
    (att,) = call(
        merge_kernel, [((ROWS, GROUP * DH), bf16)], in_specs=[smem] + [vmem] * 4
    )(live_rows, result, level, *back[:2])

    held = [att] + [moved(att, z=z) for z in FAR]
    held = held + [moved(rows, xh=1) for rows in held]
    width = out_weight.shape[1]
    (terms,) = call(
        project_kernel,
        [((8, ROWS, CORE * width), bf16)],
        [pltpu.VMEM((8 * ROWS, GROUP * DH), bf16)],
        in_specs=[smem] + [vmem] * 10,
    )(index.reshape(1), *held, out_weight, weight_c)
    gathered = lax.all_to_all(terms, "head", 0, 0, tiled=True)
    mine, other = call(
        functools.partial(sum_kernel, width=width),
        [((ROWS, width), bf16), ((ROWS, width), bf16)],
    )(gathered)
    theirs = moved(other, c=1)
    return jnp.where(
        core == 0,
        jnp.concatenate([mine, theirs], axis=0),
        jnp.concatenate([theirs, mine], axis=0),
    )


def solution(mesh):
    return jax.shard_map(
        shards,
        mesh=mesh,
        in_specs=(
            P("blk", "head"),
            P("blk", "head"),
            P("blk", "head"),
            P("blk"),
            P("blk"),
            P("blk", "head"),
            P("blk", "head"),
            P("head", "blk"),
        ),
        out_specs=P("head", "blk"),
        check_vma=False,
    )
```

```python
import functools

import jax
import jax.numpy as jnp
from jax import lax
from jax.experimental import pallas as pl
from jax.experimental.pallas import tpu as pltpu
from jax.sharding import PartitionSpec as P

DH = 128
GROUP = 8
ROWS = 64
LANES = GROUP * ROWS
EXTRA = 16
SCALE = DH**-0.5 * 1.4426950408889634
FLOOR = -1e30
XH, Z, CORE = 2, 4, 2
VMEM_LIMIT = 30 << 20
FAR = (1, 3, 2)


def moved(array, xh=0, z=0, c=0):
    pairs = []
    for i in range(XH * Z * CORE):
        a, b, d = i // (Z * CORE), (i // CORE) % Z, i % CORE
        to = (((a + xh) % XH) * Z + (b + z) % Z) * CORE + (d + c) % CORE
        pairs.append((i, to))
    return lax.ppermute(array, "blk", pairs)


def after(array, *others):
    return lax.optimization_barrier((array, *others))[0]


def scores_of(queries, keys):
    return lax.dot_general(
        queries, keys, (((1,), (1,)), ((), ())), preferred_element_type=jnp.float32
    )


def wide(column, width):
    return jnp.concatenate([column] * (width // column.shape[1]), axis=1)


def add_block(top, total, scores, values):
    best = jnp.maximum(top, jnp.max(scores, axis=1, keepdims=True) * SCALE)
    keys = scores.shape[1]
    at = wide(best, keys) if keys >= DH else best[:, :keys]
    weights = jnp.exp2(scores * SCALE - at).astype(jnp.bfloat16)
    part = jnp.dot(weights, values, preferred_element_type=jnp.float32)
    return best, total * wide(jnp.exp2(top - best), 2 * DH) + part


def stacked(ref):
    return jnp.concatenate([ref[:, h * DH : (h + 1) * DH] for h in range(GROUP)], axis=0)


def join_kernel(k, v, whole, first, second):
    size = k.shape[0]
    at = 0
    for kv in (whole, first, second):
        count = kv.shape[0] // 2
        kv[:count, :] = k[at : at + count, :]
        kv[count:, :] = v[at : at + count, :]
        at = (at + count) % size


def split(parts, keys, values):
    at = 0
    for kv in parts:
        size = kv.shape[0] // 2
        keys[at : at + size, :] = kv[:size, :]
        values[at : at + size, :DH] = kv[size:, :]
        at += size
    values[:, DH:] = jnp.ones((at, DH), values.dtype)


def finish(top, total):
    denominator = total[:, DH:]
    result = (total[:, :DH] / denominator).T
    level = (top + jnp.log2(denominator)).T[:1]
    return result, level


def packed(result, level):
    high = level.astype(jnp.bfloat16).astype(jnp.float32)
    mid = (level - high).astype(jnp.bfloat16).astype(jnp.float32)
    low = level - high - mid
    row = lax.broadcasted_iota(jnp.int32, (EXTRA, LANES), 0)
    pieces = jnp.where(row == 0, high, jnp.where(row == 1, mid, low))
    return jnp.concatenate([result, pieces], axis=0).astype(jnp.bfloat16)


def unpacked(block):
    pieces = block[DH:, :].astype(jnp.float32)
    return block[:DH, :].astype(jnp.float32), (pieces[0:1] + pieces[1:2]) + pieces[2:3]


def merged(parts):
    best = functools.reduce(jnp.maximum, [level for _, level in parts])
    numerator, denominator = 0.0, 0.0
    for result, level in parts:
        share = jnp.exp2(level - best)
        numerator = numerator + result * share
        denominator = denominator + share
    return numerator / denominator, best + jnp.log2(denominator)


def run(tasks, states):
    def scores_at(i):
        _, rows, keys, _ = tasks[i]
        return scores_of(rows[...], keys[...])

    ahead = scores_at(0)
    for i, (owner, _, _, values) in enumerate(tasks):
        scores = ahead
        if i + 1 < len(tasks):
            ahead = scores_at(i + 1)
        states[owner] = add_block(*states[owner], scores, values[...])
    return states


def empty():
    return (
        jnp.full((LANES, DH), FLOOR, jnp.float32),
        jnp.zeros((LANES, 2 * DH), jnp.float32),
    )


def own_kernel(q, qkv, bias, kv, top_out, total_out, k, values):
    split((kv,), k, values)
    rows = stacked(q)
    scores = scores_of(rows, qkv[:ROWS, :]) + jnp.concatenate([bias[...]] * GROUP, axis=0)
    block = scores_of(rows, k[...])
    top, total = add_block(
        *empty(),
        scores,
        jnp.concatenate([qkv[ROWS:, :], jnp.ones((ROWS, DH), jnp.bfloat16)], axis=1),
    )
    top_out[...], total_out[...] = add_block(top, total, block, values[...])


def near_kernel(q0, q1, q2, q, kv, kv_c, top_out, total_out, rows, k0, v0, k1, v1):
    split((kv,), k0, v0)
    split((kv_c,), k1, v1)
    for i, ref in enumerate((q0, q1, q2, q)):
        rows[i] = stacked(ref)
    tasks = [(i, rows.at[i], k, v) for k, v in ((k0, v0), (k1, v1)) for i in range(3)]
    for i, (top, total) in enumerate(run(tasks, [empty() for _ in range(3)])):
        top_out[i], total_out[i] = top, total


def others_kernel(rows, top_in, total_in, *refs):
    *parts, top_out, total_out, k, values = refs
    split(parts, k, values)
    states = [(top_in[i], total_in[i]) for i in range(3)]
    states = run([(i, rows.at[i], k, values) for i in range(3)], states)
    for i, (top, total) in enumerate(states):
        top_out[i], total_out[i] = top, total


def own_more_kernel(rows, top, total, *refs):
    *parts, top_out, total_out, k, values = refs
    split(parts, k, values)
    states = run([(0, rows.at[3], k, values)], [(top[...], total[...])])
    top_out[...], total_out[...] = states[0]


def last_kernel(rows, top, total, half, other_half, *refs, owners):
    *outs, k, values = refs
    split((half, other_half), k, values)
    tasks = [(i, rows.at[owner], k, values) for i, owner in enumerate(owners)]
    states = run(tasks, [(top[owner], total[owner]) for owner in owners])
    for state, out in zip(states, outs):
        out[...] = packed(*finish(*state))


def own_last_kernel(rows, top, total, half, other_half, r2, result_ref, level_ref, k, values):
    split((half, other_half), k, values)
    states = run([(0, rows.at[3], k, values)], [(top[...], total[...])])
    result, level = merged([finish(*states[0]), unpacked(r2)])
    result_ref[...] = result
    level_ref[...] = jnp.broadcast_to(level, (8, LANES))


def merge_kernel(live, result, level, r0, r1, att):
    parts = [(result[...], level[:1])] + [unpacked(r) for r in (r0, r1)]
    whole, _ = merged(parts)
    slot = lax.broadcasted_iota(jnp.int32, (1, LANES), 1) % ROWS
    rows = jnp.where(slot < live[0], whole, 0.0).T.astype(jnp.bfloat16)
    for head in range(GROUP):
        att[:, head * DH : (head + 1) * DH] = rows[head * ROWS : (head + 1) * ROWS, :]


def project_kernel(index, a0, a1, a2, a3, a4, a5, a6, a7, wa, wb, out, rows):
    for i, ref in enumerate((a0, a1, a2, a3, a4, a5, a6, a7)):
        rows[i * ROWS : (i + 1) * ROWS, :] = ref[...]
    width = wa.shape[1]
    xh, z = index[0] // (Z * CORE), (index[0] // CORE) % Z
    slots = [((xh + dx) % XH) * Z + (z + Z - dz) % Z for dx in range(XH) for dz in (0,) + FAR]
    for side, w in enumerate((wa, wb)):
        terms = jnp.dot(rows[...], w[...], preferred_element_type=jnp.float32).astype(jnp.bfloat16)
        for i in range(8):
            out[slots[i], :, side * width : (side + 1) * width] = terms[i * ROWS : (i + 1) * ROWS, :]


def sum_kernel(terms, mine, other, *, width):
    acc = terms[0].astype(jnp.float32)
    for i in range(1, terms.shape[0]):
        acc = acc + terms[i].astype(jnp.float32)
    acc = acc.astype(jnp.bfloat16)
    mine[...] = acc[:, :width]
    other[...] = acc[:, width:]


def call(kernel, outs, scratch=(), flops=0, **kwargs):
    return pl.pallas_call(
        kernel,
        out_shape=tuple(jax.ShapeDtypeStruct(s, d) for s, d in outs),
        scratch_shapes=list(scratch),
        compiler_params=pltpu.CompilerParams(vmem_limit_bytes=VMEM_LIMIT),
        cost_estimate=(
            pl.CostEstimate(flops=flops, bytes_accessed=0, transcendentals=0) if flops else None
        ),
        **kwargs,
    )


def shards(
    queries,
    question_keys,
    question_values,
    question_ids,
    live_rows,
    prefix_keys,
    prefix_values,
    out_weight,
):
    f32, bf16 = jnp.float32, jnp.bfloat16
    index = lax.axis_index("blk")
    core = index % CORE
    positions = prefix_keys.shape[0]
    vmem = pl.BlockSpec(memory_space=pltpu.VMEM)
    smem = pl.BlockSpec(memory_space=pltpu.SMEM)
    block_flops = 8 * LANES * positions * DH
    part = ((DH + EXTRA, LANES), bf16)

    own_state = [((LANES, DH), f32), ((LANES, 2 * DH), f32)]
    state = [((3, LANES, DH), f32), ((3, LANES, 2 * DH), f32)]

    early = positions * 7 // 16
    late = positions - early
    kv, *halves = call(
        join_kernel, [((2 * size, DH), bf16) for size in (positions, early, late)]
    )(prefix_keys, prefix_values)
    x0, x1 = [moved(half, xh=1) for half in halves]
    kv_c = moved(kv, c=1)
    q_z = [moved(queries, z=z) for z in FAR]
    row = jnp.arange(ROWS, dtype=jnp.int32)
    allowed = (question_ids[:, None] == question_ids[None, :]) & (row[None, :] <= row[:, None])
    bias = jnp.where(allowed, 0.0, FLOOR).astype(f32)
    def scratch(*sizes):
        return [pltpu.VMEM((size, width), bf16) for size in sizes for width in (DH, 2 * DH)]

    own_top, own_total = call(own_kernel, own_state, scratch(positions))(
        queries, jnp.concatenate([question_keys, question_values]), bias, after(kv, q_z[0])
    )
    top, total, rows = call(
        near_kernel, state + [((4, LANES, DH), bf16)], scratch(positions, positions), flops=1
    )(*q_z, queries, after(kv, own_top), kv_c)
    x0, top = lax.optimization_barrier((x0, top))
    xc0 = moved(x0, c=1)
    own_top, own_total = call(own_more_kernel, own_state, scratch(positions), flops=block_flops)(
        after(rows, x0), own_top, own_total, kv_c
    )
    top, total = call(others_kernel, state, scratch(2 * early), flops=1)(
        rows, after(top, own_top), total, x0, xc0
    )

    x1, weight, top = lax.optimization_barrier((x1, out_weight, top))
    xc1 = moved(x1, c=1)
    weight_c = moved(weight, c=1)
    own_top, own_total = call(own_more_kernel, own_state, scratch(2 * early), flops=2 * block_flops)(
        after(rows, x1), own_top, own_total, x0, xc0
    )
    top = after(top, own_top)
    (p_far,) = call(functools.partial(last_kernel, owners=(2,)), [part], scratch(2 * late), flops=1)(
        rows, top, total, x1, xc1
    )
    p_next = call(
        functools.partial(last_kernel, owners=(0, 1)), [part] * 2, scratch(2 * late), flops=4 * block_flops
    )(rows, after(top, p_far), total, x1, xc1)
    back = [moved(p, z=-z) for p, z in zip((*p_next, p_far), FAR)]
    result, level = call(
        own_last_kernel, [((DH, LANES), f32), ((8, LANES), f32)], scratch(2 * late), flops=1
    )(after(rows, *p_next), own_top, own_total, x1, xc1, back[2])
    (att,) = call(
        merge_kernel, [((ROWS, GROUP * DH), bf16)], in_specs=[smem] + [vmem] * 4
    )(live_rows, result, level, *back[:2])

    att_x = moved(att, xh=1)
    held = [att] + [moved(att, z=z) for z in FAR] + [att_x] + [moved(att_x, z=z) for z in FAR]
    width = out_weight.shape[1]
    (terms,) = call(
        project_kernel,
        [((8, ROWS, CORE * width), bf16)],
        [pltpu.VMEM((8 * ROWS, GROUP * DH), bf16)],
        in_specs=[smem] + [vmem] * 10,
    )(index.reshape(1), *held, out_weight, weight_c)
    gathered = lax.all_to_all(terms, "head", 0, 0, tiled=True)
    mine, other = call(
        functools.partial(sum_kernel, width=width),
        [((ROWS, width), bf16), ((ROWS, width), bf16)],
    )(gathered)
    theirs = moved(other, c=1)
    return jnp.where(
        core == 0,
        jnp.concatenate([mine, theirs], axis=0),
        jnp.concatenate([theirs, mine], axis=0),
    )


def solution(mesh):
    return jax.shard_map(
        shards,
        mesh=mesh,
        in_specs=(
            P("blk", "head"),
            P("blk", "head"),
            P("blk", "head"),
            P("blk"),
            P("blk"),
            P("blk", "head"),
            P("blk", "head"),
            P("head", "blk"),
        ),
        out_specs=P("head", "blk"),
        check_vma=False,
    )
```

```python
import functools

import jax
import jax.numpy as jnp
from jax import lax
from jax.experimental import pallas as pl
from jax.experimental.pallas import tpu as pltpu
from jax.sharding import PartitionSpec as P

DH = 128
GROUP = 8
ROWS = 64
LANES = GROUP * ROWS
EXTRA = 16
SCALE = DH**-0.5 * 1.4426950408889634
FLOOR = -1e30
XH, Z, CORE = 2, 4, 2
VMEM_LIMIT = 30 << 20
FAR = (1, 3, 2)


def moved(array, xh=0, z=0, c=0):
    pairs = []
    for i in range(XH * Z * CORE):
        a, b, d = i // (Z * CORE), (i // CORE) % Z, i % CORE
        to = (((a + xh) % XH) * Z + (b + z) % Z) * CORE + (d + c) % CORE
        pairs.append((i, to))
    return lax.ppermute(array, "blk", pairs)


def after(array, *others):
    return lax.optimization_barrier((array, *others))[0]


def scores_of(queries, keys):
    return lax.dot_general(
        queries, keys, (((1,), (1,)), ((), ())), preferred_element_type=jnp.float32
    )


def wide(column, width):
    return jnp.concatenate([column] * (width // column.shape[1]), axis=1)


def add_block(top, total, scores, values):
    best = jnp.maximum(top, jnp.max(scores, axis=1, keepdims=True) * SCALE)
    keys = scores.shape[1]
    at = wide(best, keys) if keys >= DH else best[:, :keys]
    weights = jnp.exp2(scores * SCALE - at).astype(jnp.bfloat16)
    part = jnp.dot(weights, values, preferred_element_type=jnp.float32)
    return best, total * wide(jnp.exp2(top - best), 2 * DH) + part


def stacked(ref):
    return jnp.concatenate([ref[:, h * DH : (h + 1) * DH] for h in range(GROUP)], axis=0)


def join_kernel(k, v, whole, first, second):
    size = k.shape[0]
    at = 0
    for kv in (whole, first, second):
        count = kv.shape[0] // 2
        kv[:count, :] = k[at : at + count, :]
        kv[count:, :] = v[at : at + count, :]
        at = (at + count) % size


def split(parts, keys, values):
    at = 0
    for kv in parts:
        size = kv.shape[0] // 2
        keys[at : at + size, :] = kv[:size, :]
        values[at : at + size, :DH] = kv[size:, :]
        at += size
    values[:, DH:] = jnp.ones((at, DH), values.dtype)


def finish(top, total):
    denominator = total[:, DH:]
    result = (total[:, :DH] / denominator).T
    level = (top + jnp.log2(denominator)).T[:1]
    return result, level


def packed(result, level):
    high = level.astype(jnp.bfloat16).astype(jnp.float32)
    mid = (level - high).astype(jnp.bfloat16).astype(jnp.float32)
    low = level - high - mid
    row = lax.broadcasted_iota(jnp.int32, (EXTRA, LANES), 0)
    pieces = jnp.where(row == 0, high, jnp.where(row == 1, mid, low))
    return jnp.concatenate([result, pieces], axis=0).astype(jnp.bfloat16)


def unpacked(block):
    pieces = block[DH:, :].astype(jnp.float32)
    return block[:DH, :].astype(jnp.float32), (pieces[0:1] + pieces[1:2]) + pieces[2:3]


def merged(parts):
    best = functools.reduce(jnp.maximum, [level for _, level in parts])
    numerator, denominator = 0.0, 0.0
    for result, level in parts:
        share = jnp.exp2(level - best)
        numerator = numerator + result * share
        denominator = denominator + share
    return numerator / denominator, best + jnp.log2(denominator)


def run(tasks, states):
    def scores_at(i):
        _, rows, keys, _ = tasks[i]
        return scores_of(rows[...], keys[...])

    ahead = scores_at(0)
    for i, (owner, _, _, values) in enumerate(tasks):
        scores = ahead
        if i + 1 < len(tasks):
            ahead = scores_at(i + 1)
        states[owner] = add_block(*states[owner], scores, values[...])
    return states


def empty():
    return (
        jnp.full((LANES, DH), FLOOR, jnp.float32),
        jnp.zeros((LANES, 2 * DH), jnp.float32),
    )


def own_kernel(q, qkv, bias, kv, top_out, total_out, k, v):
    split((kv,), k, v)
    rows = stacked(q)
    scores = scores_of(rows, qkv[:ROWS, :]) + jnp.concatenate([bias[...]] * GROUP, axis=0)
    block = scores_of(rows, k[...])
    top, total = add_block(
        *empty(),
        scores,
        jnp.concatenate([qkv[ROWS:, :], jnp.ones((ROWS, DH), jnp.bfloat16)], axis=1),
    )
    top_out[...], total_out[...] = add_block(top, total, block, v[...])


def near_kernel(q0, q1, q2, q, k0, v0, kv_c, top_out, total_out, rows, k1, v1):
    split((kv_c,), k1, v1)
    for i, ref in enumerate((q0, q1, q2, q)):
        rows[i] = stacked(ref)
    tasks = [(i, rows.at[i], k, v) for k, v in ((k0, v0), (k1, v1)) for i in range(3)]
    for i, (top, total) in enumerate(run(tasks, [empty() for _ in range(3)])):
        top_out[i], total_out[i] = top, total


def others_kernel(rows, top_in, total_in, part, other_part, top_out, total_out, k, v):
    split((part, other_part), k, v)
    states = [(top_in[i], total_in[i]) for i in range(3)]
    states = run([(i, rows.at[i], k, v) for i in range(3)], states)
    for i, (top, total) in enumerate(states):
        top_out[i], total_out[i] = top, total


def own_more_kernel(rows, top, total, k, v, top_out, total_out):
    states = run([(0, rows.at[3], k, v)], [(top[...], total[...])])
    top_out[...], total_out[...] = states[0]


def far_kernel(rows, top, total, part, other_part, out, k, v):
    split((part, other_part), k, v)
    states = run([(0, rows.at[2], k, v)], [(top[2], total[2])])
    out[...] = packed(*finish(*states[0]))


def next_kernel(rows, top, total, k, v, *outs):
    states = [(top[i], total[i]) for i in range(2)]
    states = run([(i, rows.at[i], k, v) for i in range(2)], states)
    for state, out in zip(states, outs):
        out[...] = packed(*finish(*state))


def own_last_kernel(rows, top, total, k, v, r2, result_ref, level_ref):
    states = run([(0, rows.at[3], k, v)], [(top[...], total[...])])
    result, level = merged([finish(*states[0]), unpacked(r2)])
    result_ref[...] = result
    level_ref[...] = jnp.broadcast_to(level, (8, LANES))


def merge_kernel(live, result, level, r0, r1, att):
    parts = [(result[...], level[:1])] + [unpacked(r) for r in (r0, r1)]
    whole, _ = merged(parts)
    slot = lax.broadcasted_iota(jnp.int32, (1, LANES), 1) % ROWS
    rows = jnp.where(slot < live[0], whole, 0.0).T.astype(jnp.bfloat16)
    for head in range(GROUP):
        att[:, head * DH : (head + 1) * DH] = rows[head * ROWS : (head + 1) * ROWS, :]


def project_kernel(index, a0, a1, a2, a3, a4, a5, a6, a7, wa, wb, out, rows):
    for i, ref in enumerate((a0, a1, a2, a3, a4, a5, a6, a7)):
        rows[i * ROWS : (i + 1) * ROWS, :] = ref[...]
    width = wa.shape[1]
    xh, z = index[0] // (Z * CORE), (index[0] // CORE) % Z
    slots = [((xh + dx) % XH) * Z + (z + Z - dz) % Z for dx in range(XH) for dz in (0, 2, 1, 3)]
    for side, w in enumerate((wa, wb)):
        terms = jnp.dot(rows[...], w[...], preferred_element_type=jnp.float32).astype(jnp.bfloat16)
        for i in range(8):
            out[slots[i], :, side * width : (side + 1) * width] = terms[i * ROWS : (i + 1) * ROWS, :]


def sum_kernel(terms, mine, other, *, width):
    acc = terms[0].astype(jnp.float32)
    for i in range(1, terms.shape[0]):
        acc = acc + terms[i].astype(jnp.float32)
    acc = acc.astype(jnp.bfloat16)
    mine[...] = acc[:, :width]
    other[...] = acc[:, width:]


def place_kernel(core, mine, theirs, out):
    out[pl.ds(pl.multiple_of(core[0] * ROWS, ROWS), ROWS), :] = mine[...]
    out[pl.ds(pl.multiple_of((1 - core[0]) * ROWS, ROWS), ROWS), :] = theirs[...]


def call(kernel, outs, scratch=(), flops=0, **kwargs):
    return pl.pallas_call(
        kernel,
        out_shape=tuple(jax.ShapeDtypeStruct(s, d) for s, d in outs),
        scratch_shapes=list(scratch),
        compiler_params=pltpu.CompilerParams(vmem_limit_bytes=VMEM_LIMIT),
        cost_estimate=(
            pl.CostEstimate(flops=flops, bytes_accessed=0, transcendentals=0) if flops else None
        ),
        **kwargs,
    )


def shards(
    queries,
    question_keys,
    question_values,
    question_ids,
    live_rows,
    prefix_keys,
    prefix_values,
    out_weight,
):
    f32, bf16 = jnp.float32, jnp.bfloat16
    index = lax.axis_index("blk")
    core = index % CORE
    positions = prefix_keys.shape[0]
    vmem = pl.BlockSpec(memory_space=pltpu.VMEM)
    smem = pl.BlockSpec(memory_space=pltpu.SMEM)
    block_flops = 8 * LANES * positions * DH
    part = ((DH + EXTRA, LANES), bf16)

    own_state = [((LANES, DH), f32), ((LANES, 2 * DH), f32)]
    state = [((3, LANES, DH), f32), ((3, LANES, 2 * DH), f32)]

    early = positions * 7 // 16
    late = positions - early
    kv, *halves = call(
        join_kernel, [((2 * size, DH), bf16) for size in (positions, early, late)]
    )(prefix_keys, prefix_values)
    x0, x1 = [moved(half, xh=1) for half in halves]
    kv_c = moved(kv, c=1)
    q_z = [moved(queries, z=z) for z in FAR]
    row = jnp.arange(ROWS, dtype=jnp.int32)
    allowed = (question_ids[:, None] == question_ids[None, :]) & (row[None, :] <= row[:, None])
    bias = jnp.where(allowed, 0.0, FLOOR).astype(f32)
    def layout(size):
        return [((size, DH), bf16), ((size, 2 * DH), bf16)]

    own_top, own_total, *block = call(own_kernel, own_state + layout(positions))(
        queries, jnp.concatenate([question_keys, question_values]), bias, after(kv, q_z[0])
    )
    top, total, rows, *block = call(
        near_kernel, state + [((4, LANES, DH), bf16)] + layout(positions), flops=1
    )(*q_z, queries, *block, kv_c)
    x0, top = lax.optimization_barrier((x0, top))
    xc0 = moved(x0, c=1)
    own_top, own_total = call(own_more_kernel, own_state, flops=block_flops)(
        after(rows, x0), own_top, own_total, *block
    )
    top, total, *block = call(others_kernel, state + layout(2 * early), flops=1)(
        rows, after(top, own_top), total, x0, xc0
    )

    x1, weight, top = lax.optimization_barrier((x1, out_weight, top))
    xc1 = moved(x1, c=1)
    weight_c = moved(weight, c=1)
    own_top, own_total = call(own_more_kernel, own_state, flops=2 * block_flops)(
        after(rows, x1), own_top, own_total, *block
    )
    p_far, *block = call(far_kernel, [part] + layout(2 * late), flops=1)(
        rows, after(top, own_top), total, x1, xc1
    )
    p_next = call(next_kernel, [part] * 2, flops=4 * block_flops)(
        rows, after(top, p_far), total, *block
    )
    back = [moved(p, z=-z) for p, z in zip((*p_next, p_far), FAR)]
    result, level = call(own_last_kernel, [((DH, LANES), f32), ((8, LANES), f32)], flops=1)(
        after(rows, *p_next), own_top, own_total, *block, back[2]
    )
    (att,) = call(
        merge_kernel, [((ROWS, GROUP * DH), bf16)], in_specs=[smem] + [vmem] * 4
    )(live_rows, result, level, *back[:2])

    att_x = moved(att, xh=1)
    steps = (2, 1, 3)
    held = [att] + [moved(att, z=z) for z in steps] + [att_x] + [moved(att_x, z=z) for z in steps]
    width = out_weight.shape[1]
    (terms,) = call(
        project_kernel,
        [((8, ROWS, CORE * width), bf16)],
        [pltpu.VMEM((8 * ROWS, GROUP * DH), bf16)],
        in_specs=[smem] + [vmem] * 10,
    )(index.reshape(1), *held, out_weight, weight_c)
    gathered = lax.all_to_all(terms, "head", 0, 0, tiled=True)
    mine, other = call(
        functools.partial(sum_kernel, width=width),
        [((ROWS, width), bf16), ((ROWS, width), bf16)],
    )(gathered)
    theirs = moved(other, c=1)
    (projected,) = call(
        place_kernel, [((CORE * ROWS, width), bf16)], in_specs=[smem, vmem, vmem]
    )(core.reshape(1), mine, theirs)
    return projected


def solution(mesh):
    return jax.shard_map(
        shards,
        mesh=mesh,
        in_specs=(
            P("blk", "head"),
            P("blk", "head"),
            P("blk", "head"),
            P("blk"),
            P("blk"),
            P("blk", "head"),
            P("blk", "head"),
            P("head", "blk"),
        ),
        out_specs=P("head", "blk"),
        check_vma=False,
    )
```

```python
import functools

import jax
import jax.numpy as jnp
from jax import lax
from jax.experimental import pallas as pl
from jax.experimental.pallas import tpu as pltpu
from jax.sharding import PartitionSpec as P

DH = 128
GROUP = 8
ROWS = 64
LANES = GROUP * ROWS
EXTRA = 16
SCALE = DH**-0.5 * 1.4426950408889634
FLOOR = -1e30
XH, Z, CORE = 2, 4, 2
VMEM_LIMIT = 30 << 20
FAR = (1, 3, 2)


def moved(array, xh=0, z=0, c=0):
    pairs = []
    for i in range(XH * Z * CORE):
        a, b, d = i // (Z * CORE), (i // CORE) % Z, i % CORE
        to = (((a + xh) % XH) * Z + (b + z) % Z) * CORE + (d + c) % CORE
        pairs.append((i, to))
    return lax.ppermute(array, "blk", pairs)


def after(array, *others):
    return lax.optimization_barrier((array, *others))[0]


def scores_of(queries, keys):
    return lax.dot_general(
        queries, keys, (((1,), (1,)), ((), ())), preferred_element_type=jnp.float32
    )


def wide(column, width):
    return jnp.concatenate([column] * (width // column.shape[1]), axis=1)


def add_block(top, total, scores, values):
    best = jnp.maximum(top, jnp.max(scores, axis=1, keepdims=True) * SCALE)
    keys = scores.shape[1]
    at = wide(best, keys) if keys >= DH else best[:, :keys]
    weights = jnp.exp2(scores * SCALE - at).astype(jnp.bfloat16)
    part = jnp.dot(weights, values, preferred_element_type=jnp.float32)
    return best, total * wide(jnp.exp2(top - best), 2 * DH) + part


def stacked(ref):
    return jnp.concatenate([ref[:, h * DH : (h + 1) * DH] for h in range(GROUP)], axis=0)


def join_kernel(k, v, whole, first, second):
    size = k.shape[0]
    at = 0
    for kv in (whole, first, second):
        count = kv.shape[0] // 2
        kv[:count, :] = k[at : at + count, :]
        kv[count:, :] = v[at : at + count, :]
        at = (at + count) % size


def split(parts, keys, values):
    at = 0
    for kv in parts:
        size = kv.shape[0] // 2
        keys[at : at + size, :] = kv[:size, :]
        values[at : at + size, :DH] = kv[size:, :]
        at += size
    values[:, DH:] = jnp.ones((at, DH), values.dtype)


def finish(top, total):
    denominator = total[:, DH:]
    result = (total[:, :DH] / denominator).T
    level = (top + jnp.log2(denominator)).T[:1]
    return result, level


def packed(result, level):
    high = level.astype(jnp.bfloat16).astype(jnp.float32)
    mid = (level - high).astype(jnp.bfloat16).astype(jnp.float32)
    low = level - high - mid
    row = lax.broadcasted_iota(jnp.int32, (EXTRA, LANES), 0)
    pieces = jnp.where(row == 0, high, jnp.where(row == 1, mid, low))
    return jnp.concatenate([result, pieces], axis=0).astype(jnp.bfloat16)


def unpacked(block):
    pieces = block[DH:, :].astype(jnp.float32)
    return block[:DH, :].astype(jnp.float32), (pieces[0:1] + pieces[1:2]) + pieces[2:3]


def merged(parts):
    best = functools.reduce(jnp.maximum, [level for _, level in parts])
    numerator, denominator = 0.0, 0.0
    for result, level in parts:
        share = jnp.exp2(level - best)
        numerator = numerator + result * share
        denominator = denominator + share
    return numerator / denominator, best + jnp.log2(denominator)


def run(tasks, states):
    def scores_at(i):
        _, rows, keys, _ = tasks[i]
        return scores_of(rows[...], keys[...])

    ahead = scores_at(0)
    for i, (owner, _, _, values) in enumerate(tasks):
        scores = ahead
        if i + 1 < len(tasks):
            ahead = scores_at(i + 1)
        states[owner] = add_block(*states[owner], scores, values[...])
    return states


def empty():
    return (
        jnp.full((LANES, DH), FLOOR, jnp.float32),
        jnp.zeros((LANES, 2 * DH), jnp.float32),
    )


def own_kernel(q, qkv, bias, kv, top_out, total_out, k, v):
    split((kv,), k, v)
    rows = stacked(q)
    scores = scores_of(rows, qkv[:ROWS, :]) + jnp.concatenate([bias[...]] * GROUP, axis=0)
    block = scores_of(rows, k[...])
    top, total = add_block(
        *empty(),
        scores,
        jnp.concatenate([qkv[ROWS:, :], jnp.ones((ROWS, DH), jnp.bfloat16)], axis=1),
    )
    top_out[...], total_out[...] = add_block(top, total, block, v[...])


def near_kernel(q0, q1, q2, q, k0, v0, kv_c, top_out, total_out, rows, k1, v1):
    split((kv_c,), k1, v1)
    for i, ref in enumerate((q0, q1, q2, q)):
        rows[i] = stacked(ref)
    tasks = [(i, rows.at[i], k, v) for k, v in ((k0, v0), (k1, v1)) for i in range(3)]
    for i, (top, total) in enumerate(run(tasks, [empty() for _ in range(3)])):
        top_out[i], total_out[i] = top, total


def others_kernel(rows, top_in, total_in, part, other_part, top_out, total_out, k, v):
    split((part, other_part), k, v)
    states = [(top_in[i], total_in[i]) for i in range(3)]
    states = run([(i, rows.at[i], k, v) for i in range(3)], states)
    for i, (top, total) in enumerate(states):
        top_out[i], total_out[i] = top, total


def own_more_kernel(rows, top, total, k, v, top_out, total_out):
    states = run([(0, rows.at[3], k, v)], [(top[...], total[...])])
    top_out[...], total_out[...] = states[0]


def far_kernel(rows, top, total, part, other_part, out, k, v):
    split((part, other_part), k, v)
    states = run([(0, rows.at[2], k, v)], [(top[2], total[2])])
    out[...] = packed(*finish(*states[0]))


def next_kernel(rows, top, total, k, v, *outs):
    states = [(top[i], total[i]) for i in range(2)]
    states = run([(i, rows.at[i], k, v) for i in range(2)], states)
    for state, out in zip(states, outs):
        out[...] = packed(*finish(*state))


def own_last_kernel(rows, top, total, k, v, r2, result_ref, level_ref):
    states = run([(0, rows.at[3], k, v)], [(top[...], total[...])])
    result, level = merged([finish(*states[0]), unpacked(r2)])
    result_ref[...] = result
    level_ref[...] = jnp.broadcast_to(level, (8, LANES))


def merge_kernel(live, result, level, r0, r1, att):
    parts = [(result[...], level[:1])] + [unpacked(r) for r in (r0, r1)]
    whole, _ = merged(parts)
    slot = lax.broadcasted_iota(jnp.int32, (1, LANES), 1) % ROWS
    rows = jnp.where(slot < live[0], whole, 0.0).T.astype(jnp.bfloat16)
    for head in range(GROUP):
        att[:, head * DH : (head + 1) * DH] = rows[head * ROWS : (head + 1) * ROWS, :]


def project_kernel(index, a0, a1, a2, a3, a4, a5, a6, a7, wa, wb, out, rows):
    for i, ref in enumerate((a0, a1, a2, a3, a4, a5, a6, a7)):
        rows[i * ROWS : (i + 1) * ROWS, :] = ref[...]
    width = wa.shape[1]
    xh, z = index[0] // (Z * CORE), (index[0] // CORE) % Z
    slots = [((xh + dx) % XH) * Z + (z + Z - dz) % Z for dx in range(XH) for dz in (0, 2, 1, 3)]
    for side, w in enumerate((wa, wb)):
        terms = jnp.dot(rows[...], w[...], preferred_element_type=jnp.float32).astype(jnp.bfloat16)
        for i in range(8):
            out[slots[i], :, side * width : (side + 1) * width] = terms[i * ROWS : (i + 1) * ROWS, :]


def sum_kernel(terms, mine, other, *, width):
    acc = terms[0].astype(jnp.float32)
    for i in range(1, terms.shape[0]):
        acc = acc + terms[i].astype(jnp.float32)
    acc = acc.astype(jnp.bfloat16)
    mine[...] = acc[:, :width]
    other[...] = acc[:, width:]


def place_kernel(core, mine, theirs, out):
    out[pl.ds(pl.multiple_of(core[0] * ROWS, ROWS), ROWS), :] = mine[...]
    out[pl.ds(pl.multiple_of((1 - core[0]) * ROWS, ROWS), ROWS), :] = theirs[...]


def call(kernel, outs, scratch=(), flops=0, **kwargs):
    return pl.pallas_call(
        kernel,
        out_shape=tuple(jax.ShapeDtypeStruct(s, d) for s, d in outs),
        scratch_shapes=list(scratch),
        compiler_params=pltpu.CompilerParams(vmem_limit_bytes=VMEM_LIMIT),
        cost_estimate=(
            pl.CostEstimate(flops=flops, bytes_accessed=0, transcendentals=0) if flops else None
        ),
        **kwargs,
    )


def shards(
    queries,
    question_keys,
    question_values,
    question_ids,
    live_rows,
    prefix_keys,
    prefix_values,
    out_weight,
):
    f32, bf16 = jnp.float32, jnp.bfloat16
    index = lax.axis_index("blk")
    core = index % CORE
    positions = prefix_keys.shape[0]
    vmem = pl.BlockSpec(memory_space=pltpu.VMEM)
    smem = pl.BlockSpec(memory_space=pltpu.SMEM)
    block_flops = 8 * LANES * positions * DH
    part = ((DH + EXTRA, LANES), bf16)

    own_state = [((LANES, DH), f32), ((LANES, 2 * DH), f32)]
    state = [((3, LANES, DH), f32), ((3, LANES, 2 * DH), f32)]

    early = positions * 7 // 16
    late = positions - early
    kv, *halves = call(
        join_kernel, [((2 * size, DH), bf16) for size in (positions, early, late)]
    )(prefix_keys, prefix_values)
    x0, x1 = [moved(half, xh=1) for half in halves]
    kv_c = moved(kv, c=1)
    q_z = [moved(queries, z=z) for z in FAR]
    row = jnp.arange(ROWS, dtype=jnp.int32)
    allowed = (question_ids[:, None] == question_ids[None, :]) & (row[None, :] <= row[:, None])
    bias = jnp.where(allowed, 0.0, FLOOR).astype(f32)
    def layout(size):
        return [((size, DH), bf16), ((size, 2 * DH), bf16)]

    own_top, own_total, *block = call(own_kernel, own_state + layout(positions))(
        queries, jnp.concatenate([question_keys, question_values]), bias, after(kv, q_z[0])
    )
    top, total, rows, *block = call(
        near_kernel, state + [((4, LANES, DH), bf16)] + layout(positions), flops=1
    )(*q_z, queries, *block, kv_c)
    x0, top = lax.optimization_barrier((x0, top))
    xc0 = moved(x0, c=1)
    own_top, own_total = call(own_more_kernel, own_state, flops=block_flops)(
        after(rows, x0), own_top, own_total, *block
    )
    top, total, *block = call(others_kernel, state + layout(2 * early), flops=1)(
        rows, after(top, own_top), total, x0, xc0
    )

    x1, weight, top = lax.optimization_barrier((x1, out_weight, top))
    xc1 = moved(x1, c=1)
    weight_c = moved(weight, c=1)
    own_top, own_total = call(own_more_kernel, own_state, flops=2 * block_flops)(
        after(rows, x1), own_top, own_total, *block
    )
    p_far, *block = call(far_kernel, [part] + layout(2 * late), flops=1)(
        rows, after(top, own_top), total, x1, xc1
    )
    p_next = call(next_kernel, [part] * 2, flops=4 * block_flops)(
        rows, after(top, p_far), total, *block
    )
    back = [moved(p, z=-z) for p, z in zip((*p_next, p_far), FAR)]
    result, level = call(own_last_kernel, [((DH, LANES), f32), ((8, LANES), f32)], flops=1)(
        after(rows, *p_next), own_top, own_total, *block, back[2]
    )
    (att,) = call(
        merge_kernel, [((ROWS, GROUP * DH), bf16)], in_specs=[smem] + [vmem] * 4
    )(live_rows, result, level, *back[:2])

    att_x = moved(att, xh=1)
    held = [att] + [moved(att, z=z) for z in (2, 1, 3)]
    held += [att_x, moved(held[1], xh=1)] + [moved(att_x, z=z) for z in (1, 3)]
    width = out_weight.shape[1]
    (terms,) = call(
        project_kernel,
        [((8, ROWS, CORE * width), bf16)],
        [pltpu.VMEM((8 * ROWS, GROUP * DH), bf16)],
        in_specs=[smem] + [vmem] * 10,
    )(index.reshape(1), *held, out_weight, weight_c)
    gathered = lax.all_to_all(terms, "head", 0, 0, tiled=True)
    mine, other = call(
        functools.partial(sum_kernel, width=width),
        [((ROWS, width), bf16), ((ROWS, width), bf16)],
    )(gathered)
    theirs = moved(other, c=1)
    (projected,) = call(
        place_kernel, [((CORE * ROWS, width), bf16)], in_specs=[smem, vmem, vmem]
    )(core.reshape(1), mine, theirs)
    return projected


def solution(mesh):
    return jax.shard_map(
        shards,
        mesh=mesh,
        in_specs=(
            P("blk", "head"),
            P("blk", "head"),
            P("blk", "head"),
            P("blk"),
            P("blk"),
            P("blk", "head"),
            P("blk", "head"),
            P("head", "blk"),
        ),
        out_specs=P("head", "blk"),
        check_vma=False,
    )
```

```python
import functools

import jax
import jax.numpy as jnp
from jax import lax
from jax.experimental import pallas as pl
from jax.experimental.pallas import tpu as pltpu
from jax.sharding import PartitionSpec as P

DH = 128
GROUP = 8
ROWS = 64
LANES = GROUP * ROWS
EXTRA = 16
SCALE = DH**-0.5 * 1.4426950408889634
FLOOR = -1e30
XH, Z, CORE = 2, 4, 2
VMEM_LIMIT = 30 << 20
FAR = (1, 3, 2)


def moved(array, xh=0, z=0, c=0):
    pairs = []
    for i in range(XH * Z * CORE):
        a, b, d = i // (Z * CORE), (i // CORE) % Z, i % CORE
        to = (((a + xh) % XH) * Z + (b + z) % Z) * CORE + (d + c) % CORE
        pairs.append((i, to))
    return lax.ppermute(array, "blk", pairs)


def after(array, *others):
    return lax.optimization_barrier((array, *others))[0]


def scores_of(queries, keys):
    return lax.dot_general(
        queries, keys, (((1,), (1,)), ((), ())), preferred_element_type=jnp.float32
    )


def wide(column, width):
    return jnp.concatenate([column] * (width // column.shape[1]), axis=1)


def add_block(top, total, scores, values):
    best = jnp.maximum(top, jnp.max(scores, axis=1, keepdims=True) * SCALE)
    keys = scores.shape[1]
    at = wide(best, keys) if keys >= DH else best[:, :keys]
    weights = jnp.exp2(scores * SCALE - at).astype(jnp.bfloat16)
    part = jnp.dot(weights, values, preferred_element_type=jnp.float32)
    return best, total * wide(jnp.exp2(top - best), 2 * DH) + part


def stacked(ref):
    return jnp.concatenate([ref[:, h * DH : (h + 1) * DH] for h in range(GROUP)], axis=0)


def join_kernel(k, v, whole, first, second):
    size = k.shape[0]
    at = 0
    for kv in (whole, first, second):
        count = kv.shape[0] // 2
        kv[:count, :] = k[at : at + count, :]
        kv[count:, :] = v[at : at + count, :]
        at = (at + count) % size


def split(parts, keys, values):
    at = 0
    for kv in parts:
        size = kv.shape[0] // 2
        keys[at : at + size, :] = kv[:size, :]
        values[at : at + size, :DH] = kv[size:, :]
        at += size
    values[:, DH:] = jnp.ones((at, DH), values.dtype)


def finish(top, total):
    denominator = total[:, DH:]
    result = (total[:, :DH] / denominator).T
    level = (top + jnp.log2(denominator)).T[:1]
    return result, level


def packed(result, level):
    high = level.astype(jnp.bfloat16).astype(jnp.float32)
    mid = (level - high).astype(jnp.bfloat16).astype(jnp.float32)
    low = level - high - mid
    row = lax.broadcasted_iota(jnp.int32, (EXTRA, LANES), 0)
    pieces = jnp.where(row == 0, high, jnp.where(row == 1, mid, low))
    return jnp.concatenate([result, pieces], axis=0).astype(jnp.bfloat16)


def unpacked(block):
    pieces = block[DH:, :].astype(jnp.float32)
    return block[:DH, :].astype(jnp.float32), (pieces[0:1] + pieces[1:2]) + pieces[2:3]


def merged(parts):
    best = functools.reduce(jnp.maximum, [level for _, level in parts])
    numerator, denominator = 0.0, 0.0
    for result, level in parts:
        share = jnp.exp2(level - best)
        numerator = numerator + result * share
        denominator = denominator + share
    return numerator / denominator, best + jnp.log2(denominator)


def run(tasks, states):
    def scores_at(i):
        _, rows, keys, _ = tasks[i]
        return scores_of(rows[...], keys[...])

    ahead = scores_at(0)
    for i, (owner, _, _, values) in enumerate(tasks):
        scores = ahead
        if i + 1 < len(tasks):
            ahead = scores_at(i + 1)
        states[owner] = add_block(*states[owner], scores, values[...])
    return states


def empty():
    return (
        jnp.full((LANES, DH), FLOOR, jnp.float32),
        jnp.zeros((LANES, 2 * DH), jnp.float32),
    )


def near_kernel(
    q0, q1, q2, q, qkv, bias, kv, kv_c,
    top_out, total_out, own_top, own_total, rows, k1, v1, k0, v0,
):
    split((kv,), k0, v0)
    split((kv_c,), k1, v1)
    for i, ref in enumerate((q0, q1, q2, q)):
        rows[i] = stacked(ref)
    scores = scores_of(rows[3], qkv[:ROWS, :]) + jnp.concatenate([bias[...]] * GROUP, axis=0)
    own = add_block(
        *empty(),
        scores,
        jnp.concatenate([qkv[ROWS:, :], jnp.ones((ROWS, DH), jnp.bfloat16)], axis=1),
    )
    tasks = [(i, rows.at[i], k0, v0) for i in range(4)] + [(i, rows.at[i], k1, v1) for i in range(3)]
    states = run(tasks, [empty() for _ in range(3)] + [own])
    for i in range(3):
        top_out[i], total_out[i] = states[i]
    own_top[...], own_total[...] = states[3]


def others_kernel(rows, top_in, total_in, part, other_part, top_out, total_out, k, v):
    split((part, other_part), k, v)
    states = [(top_in[i], total_in[i]) for i in range(3)]
    states = run([(i, rows.at[i], k, v) for i in range(3)], states)
    for i, (top, total) in enumerate(states):
        top_out[i], total_out[i] = top, total


def own_more_kernel(rows, top, total, k, v, top_out, total_out):
    states = run([(0, rows.at[3], k, v)], [(top[...], total[...])])
    top_out[...], total_out[...] = states[0]


def far_kernel(rows, top, total, part, other_part, out, k, v):
    split((part, other_part), k, v)
    states = run([(0, rows.at[2], k, v)], [(top[2], total[2])])
    out[...] = packed(*finish(*states[0]))


def next_kernel(rows, top, total, k, v, *outs):
    states = [(top[i], total[i]) for i in range(2)]
    states = run([(i, rows.at[i], k, v) for i in range(2)], states)
    for state, out in zip(states, outs):
        out[...] = packed(*finish(*state))


def own_last_kernel(rows, top, total, k, v, r2, result_ref, level_ref):
    states = run([(0, rows.at[3], k, v)], [(top[...], total[...])])
    result, level = merged([finish(*states[0]), unpacked(r2)])
    result_ref[...] = result
    level_ref[...] = jnp.broadcast_to(level, (8, LANES))


def merge_kernel(live, result, level, r0, r1, att):
    parts = [(result[...], level[:1])] + [unpacked(r) for r in (r0, r1)]
    whole, _ = merged(parts)
    slot = lax.broadcasted_iota(jnp.int32, (1, LANES), 1) % ROWS
    rows = jnp.where(slot < live[0], whole, 0.0).T.astype(jnp.bfloat16)
    for head in range(GROUP):
        att[:, head * DH : (head + 1) * DH] = rows[head * ROWS : (head + 1) * ROWS, :]


def project_kernel(index, a0, a1, a2, a3, a4, a5, a6, a7, wa, wb, out, rows):
    for i, ref in enumerate((a0, a1, a2, a3, a4, a5, a6, a7)):
        rows[i * ROWS : (i + 1) * ROWS, :] = ref[...]
    width = wa.shape[1]
    xh, z = index[0] // (Z * CORE), (index[0] // CORE) % Z
    slots = [((xh + dx) % XH) * Z + (z + Z - dz) % Z for dx in range(XH) for dz in (0, 2, 1, 3)]
    for side, w in enumerate((wa, wb)):
        terms = jnp.dot(rows[...], w[...], preferred_element_type=jnp.float32).astype(jnp.bfloat16)
        for i in range(8):
            out[slots[i], :, side * width : (side + 1) * width] = terms[i * ROWS : (i + 1) * ROWS, :]


def sum_kernel(terms, mine, other, *, width):
    acc = terms[0].astype(jnp.float32)
    for i in range(1, terms.shape[0]):
        acc = acc + terms[i].astype(jnp.float32)
    acc = acc.astype(jnp.bfloat16)
    mine[...] = acc[:, :width]
    other[...] = acc[:, width:]


def place_kernel(core, mine, theirs, out):
    out[pl.ds(pl.multiple_of(core[0] * ROWS, ROWS), ROWS), :] = mine[...]
    out[pl.ds(pl.multiple_of((1 - core[0]) * ROWS, ROWS), ROWS), :] = theirs[...]


def call(kernel, outs, scratch=(), flops=0, **kwargs):
    return pl.pallas_call(
        kernel,
        out_shape=tuple(jax.ShapeDtypeStruct(s, d) for s, d in outs),
        scratch_shapes=list(scratch),
        compiler_params=pltpu.CompilerParams(vmem_limit_bytes=VMEM_LIMIT),
        cost_estimate=(
            pl.CostEstimate(flops=flops, bytes_accessed=0, transcendentals=0) if flops else None
        ),
        **kwargs,
    )


def shards(
    queries,
    question_keys,
    question_values,
    question_ids,
    live_rows,
    prefix_keys,
    prefix_values,
    out_weight,
):
    f32, bf16 = jnp.float32, jnp.bfloat16
    index = lax.axis_index("blk")
    core = index % CORE
    positions = prefix_keys.shape[0]
    vmem = pl.BlockSpec(memory_space=pltpu.VMEM)
    smem = pl.BlockSpec(memory_space=pltpu.SMEM)
    block_flops = 8 * LANES * positions * DH
    part = ((DH + EXTRA, LANES), bf16)

    own_state = [((LANES, DH), f32), ((LANES, 2 * DH), f32)]
    state = [((3, LANES, DH), f32), ((3, LANES, 2 * DH), f32)]

    early = positions * 7 // 16
    late = positions - early
    kv, *halves = call(
        join_kernel, [((2 * size, DH), bf16) for size in (positions, early, late)]
    )(prefix_keys, prefix_values)
    x0, x1 = [moved(half, xh=1) for half in halves]
    kv_c = moved(kv, c=1)
    q_z = [moved(queries, z=z) for z in FAR]
    row = jnp.arange(ROWS, dtype=jnp.int32)
    allowed = (question_ids[:, None] == question_ids[None, :]) & (row[None, :] <= row[:, None])
    bias = jnp.where(allowed, 0.0, FLOOR).astype(f32)
    def layout(size):
        return [((size, DH), bf16), ((size, 2 * DH), bf16)]

    top, total, own_top, own_total, rows, *block = call(
        near_kernel,
        state + own_state + [((4, LANES, DH), bf16)] + layout(positions),
        [pltpu.VMEM((positions, DH), bf16), pltpu.VMEM((positions, 2 * DH), bf16)],
        flops=1,
    )(*q_z, queries, jnp.concatenate([question_keys, question_values]), bias, kv, kv_c)
    x0, top = lax.optimization_barrier((x0, top))
    xc0 = moved(x0, c=1)
    own_top, own_total = call(own_more_kernel, own_state, flops=block_flops)(
        after(rows, x0), own_top, own_total, *block
    )
    top, total, *block = call(others_kernel, state + layout(2 * early), flops=1)(
        rows, after(top, own_top), total, x0, xc0
    )

    x1, weight, top = lax.optimization_barrier((x1, out_weight, top))
    xc1 = moved(x1, c=1)
    weight_c = moved(weight, c=1)
    own_top, own_total = call(own_more_kernel, own_state, flops=2 * block_flops)(
        after(rows, x1), own_top, own_total, *block
    )
    p_far, *block = call(far_kernel, [part] + layout(2 * late), flops=1)(
        rows, after(top, own_top), total, x1, xc1
    )
    p_next = call(next_kernel, [part] * 2, flops=4 * block_flops)(
        rows, after(top, p_far), total, *block
    )
    back = [moved(p, z=-z) for p, z in zip((*p_next, p_far), FAR)]
    result, level = call(own_last_kernel, [((DH, LANES), f32), ((8, LANES), f32)], flops=1)(
        after(rows, *p_next), own_top, own_total, *block, back[2]
    )
    (att,) = call(
        merge_kernel, [((ROWS, GROUP * DH), bf16)], in_specs=[smem] + [vmem] * 4
    )(live_rows, result, level, *back[:2])

    att_x = moved(att, xh=1)
    held = [att] + [moved(att, z=z) for z in (2, 1, 3)]
    held += [att_x, moved(held[1], xh=1)] + [moved(att_x, z=z) for z in (1, 3)]
    width = out_weight.shape[1]
    (terms,) = call(
        project_kernel,
        [((8, ROWS, CORE * width), bf16)],
        [pltpu.VMEM((8 * ROWS, GROUP * DH), bf16)],
        in_specs=[smem] + [vmem] * 10,
    )(index.reshape(1), *held, out_weight, weight_c)
    gathered = lax.all_to_all(terms, "head", 0, 0, tiled=True)
    mine, other = call(
        functools.partial(sum_kernel, width=width),
        [((ROWS, width), bf16), ((ROWS, width), bf16)],
    )(gathered)
    theirs = moved(other, c=1)
    (projected,) = call(
        place_kernel, [((CORE * ROWS, width), bf16)], in_specs=[smem, vmem, vmem]
    )(core.reshape(1), mine, theirs)
    return projected


def solution(mesh):
    return jax.shard_map(
        shards,
        mesh=mesh,
        in_specs=(
            P("blk", "head"),
            P("blk", "head"),
            P("blk", "head"),
            P("blk"),
            P("blk"),
            P("blk", "head"),
            P("blk", "head"),
            P("head", "blk"),
        ),
        out_specs=P("head", "blk"),
        check_vma=False,
    )
```

```python
import functools

import jax
import jax.numpy as jnp
from jax import lax
from jax.experimental import pallas as pl
from jax.experimental.pallas import tpu as pltpu
from jax.sharding import PartitionSpec as P

DH = 128
GROUP = 8
ROWS = 64
LANES = GROUP * ROWS
EXTRA = 16
SCALE = DH**-0.5 * 1.4426950408889634
FLOOR = -1e30
XH, Z, CORE = 2, 4, 2
VMEM_LIMIT = 30 << 20
FAR = (1, 3, 2)


def moved(array, xh=0, z=0, c=0):
    pairs = []
    for i in range(XH * Z * CORE):
        a, b, d = i // (Z * CORE), (i // CORE) % Z, i % CORE
        to = (((a + xh) % XH) * Z + (b + z) % Z) * CORE + (d + c) % CORE
        pairs.append((i, to))
    return lax.ppermute(array, "blk", pairs)


def after(array, *others):
    return lax.optimization_barrier((array, *others))[0]


def scores_of(queries, keys):
    return lax.dot_general(
        queries, keys, (((1,), (1,)), ((), ())), preferred_element_type=jnp.float32
    )


def wide(column, width):
    return jnp.concatenate([column] * (width // column.shape[1]), axis=1)


def add_block(top, total, scores, values):
    best = jnp.maximum(top, jnp.max(scores, axis=1, keepdims=True) * SCALE)
    keys = scores.shape[1]
    at = wide(best, keys) if keys >= DH else best[:, :keys]
    weights = jnp.exp2(scores * SCALE - at).astype(jnp.bfloat16)
    part = jnp.dot(weights, values, preferred_element_type=jnp.float32)
    return best, total * wide(jnp.exp2(top - best), 2 * DH) + part


def stacked(ref):
    return jnp.concatenate([ref[:, h * DH : (h + 1) * DH] for h in range(GROUP)], axis=0)


def join_kernel(k, v, whole, first, second):
    size = k.shape[0]
    at = 0
    for kv in (whole, first, second):
        count = kv.shape[0] // 2
        kv[:count, :] = k[at : at + count, :]
        kv[count:, :] = v[at : at + count, :]
        at = (at + count) % size


def split(parts, keys, values):
    at = 0
    for kv in parts:
        size = kv.shape[0] // 2
        keys[at : at + size, :] = kv[:size, :]
        values[at : at + size, :DH] = kv[size:, :]
        at += size
    values[:, DH:] = jnp.ones((at, DH), values.dtype)


def finish(top, total):
    denominator = total[:, DH:]
    result = (total[:, :DH] / denominator).T
    level = (top + jnp.log2(denominator)).T[:1]
    return result, level


def packed(result, level):
    high = level.astype(jnp.bfloat16).astype(jnp.float32)
    mid = (level - high).astype(jnp.bfloat16).astype(jnp.float32)
    low = level - high - mid
    row = lax.broadcasted_iota(jnp.int32, (EXTRA, LANES), 0)
    pieces = jnp.where(row == 0, high, jnp.where(row == 1, mid, low))
    return jnp.concatenate([result, pieces], axis=0).astype(jnp.bfloat16)


def unpacked(block):
    pieces = block[DH:, :].astype(jnp.float32)
    return block[:DH, :].astype(jnp.float32), (pieces[0:1] + pieces[1:2]) + pieces[2:3]


def merged(parts):
    best = functools.reduce(jnp.maximum, [level for _, level in parts])
    numerator, denominator = 0.0, 0.0
    for result, level in parts:
        share = jnp.exp2(level - best)
        numerator = numerator + result * share
        denominator = denominator + share
    return numerator / denominator, best + jnp.log2(denominator)


def run(tasks, states):
    def scores_at(i):
        _, rows, keys, _ = tasks[i]
        return scores_of(rows[...], keys[...])

    ahead = scores_at(0)
    for i, (owner, _, _, values) in enumerate(tasks):
        scores = ahead
        if i + 1 < len(tasks):
            ahead = scores_at(i + 1)
        states[owner] = add_block(*states[owner], scores, values[...])
    return states


def empty():
    return (
        jnp.full((LANES, DH), FLOOR, jnp.float32),
        jnp.zeros((LANES, 2 * DH), jnp.float32),
    )


def own_kernel(q, qkv, bias, kv, top_out, total_out, k, v):
    split((kv,), k, v)
    rows = stacked(q)
    scores = scores_of(rows, qkv[:ROWS, :]) + jnp.concatenate([bias[...]] * GROUP, axis=0)
    block = scores_of(rows, k[...])
    top, total = add_block(
        *empty(),
        scores,
        jnp.concatenate([qkv[ROWS:, :], jnp.ones((ROWS, DH), jnp.bfloat16)], axis=1),
    )
    top_out[...], total_out[...] = add_block(top, total, block, v[...])


def near_kernel(q0, q1, q2, q, k0, v0, kv_c, top_out, total_out, rows, k1, v1):
    split((kv_c,), k1, v1)
    for i, ref in enumerate((q0, q1, q2, q)):
        rows[i] = stacked(ref)
    tasks = [(i, rows.at[i], k, v) for k, v in ((k0, v0), (k1, v1)) for i in range(3)]
    for i, (top, total) in enumerate(run(tasks, [empty() for _ in range(3)])):
        top_out[i], total_out[i] = top, total


def others_kernel(rows, top_in, total_in, part, other_part, top_out, total_out, k, v):
    split((part, other_part), k, v)
    states = [(top_in[i], total_in[i]) for i in range(3)]
    states = run([(i, rows.at[i], k, v) for i in range(3)], states)
    for i, (top, total) in enumerate(states):
        top_out[i], total_out[i] = top, total


def own_more_kernel(rows, top, total, k, v, top_out, total_out):
    states = run([(0, rows.at[3], k, v)], [(top[...], total[...])])
    top_out[...], total_out[...] = states[0]


def far_kernel(rows, top, total, part, other_part, out, k, v):
    split((part, other_part), k, v)
    states = run([(0, rows.at[2], k, v)], [(top[2], total[2])])
    out[...] = packed(*finish(*states[0]))


def next_kernel(rows, top, total, k, v, *outs):
    states = [(top[i], total[i]) for i in range(2)]
    states = run([(i, rows.at[i], k, v) for i in range(2)], states)
    for state, out in zip(states, outs):
        out[...] = packed(*finish(*state))


def own_last_kernel(rows, top, total, k, v, r2, result_ref, level_ref):
    states = run([(0, rows.at[3], k, v)], [(top[...], total[...])])
    result, level = merged([finish(*states[0]), unpacked(r2)])
    result_ref[...] = result
    level_ref[...] = jnp.broadcast_to(level, (8, LANES))


def merge_kernel(live, result, level, r0, r1, att):
    parts = [(result[...], level[:1])] + [unpacked(r) for r in (r0, r1)]
    whole, _ = merged(parts)
    slot = lax.broadcasted_iota(jnp.int32, (1, LANES), 1) % ROWS
    rows = jnp.where(slot < live[0], whole, 0.0).T.astype(jnp.bfloat16)
    for head in range(GROUP):
        att[:, head * DH : (head + 1) * DH] = rows[head * ROWS : (head + 1) * ROWS, :]


def project_kernel(index, a0, a1, a2, a3, a4, a5, a6, a7, wa, wb, out, rows):
    for i, ref in enumerate((a0, a1, a2, a3, a4, a5, a6, a7)):
        rows[i * ROWS : (i + 1) * ROWS, :] = ref[...]
    width = wa.shape[1]
    xh, z = index[0] // (Z * CORE), (index[0] // CORE) % Z
    slots = [((xh + dx) % XH) * Z + (z + Z - dz) % Z for dx in range(XH) for dz in (0, 2, 1, 3)]
    for side, w in enumerate((wa, wb)):
        terms = jnp.dot(rows[...], w[...], preferred_element_type=jnp.float32).astype(jnp.bfloat16)
        for i in range(8):
            out[slots[i], :, side * width : (side + 1) * width] = terms[i * ROWS : (i + 1) * ROWS, :]


def sum_kernel(terms, mine, other, *, width):
    acc = terms[0].astype(jnp.float32)
    for i in range(1, terms.shape[0]):
        acc = acc + terms[i].astype(jnp.float32)
    acc = acc.astype(jnp.bfloat16)
    mine[...] = acc[:, :width]
    other[...] = acc[:, width:]


def place_kernel(core, mine, theirs, out):
    out[pl.ds(pl.multiple_of(core[0] * ROWS, ROWS), ROWS), :] = mine[...]
    out[pl.ds(pl.multiple_of((1 - core[0]) * ROWS, ROWS), ROWS), :] = theirs[...]


def call(kernel, outs, scratch=(), flops=0, **kwargs):
    return pl.pallas_call(
        kernel,
        out_shape=tuple(jax.ShapeDtypeStruct(s, d) for s, d in outs),
        scratch_shapes=list(scratch),
        compiler_params=pltpu.CompilerParams(vmem_limit_bytes=VMEM_LIMIT),
        cost_estimate=(
            pl.CostEstimate(flops=flops, bytes_accessed=0, transcendentals=0) if flops else None
        ),
        **kwargs,
    )


def shards(
    queries,
    question_keys,
    question_values,
    question_ids,
    live_rows,
    prefix_keys,
    prefix_values,
    out_weight,
):
    f32, bf16 = jnp.float32, jnp.bfloat16
    index = lax.axis_index("blk")
    core = index % CORE
    positions = prefix_keys.shape[0]
    vmem = pl.BlockSpec(memory_space=pltpu.VMEM)
    smem = pl.BlockSpec(memory_space=pltpu.SMEM)
    block_flops = 8 * LANES * positions * DH
    part = ((DH + EXTRA, LANES), bf16)

    own_state = [((LANES, DH), f32), ((LANES, 2 * DH), f32)]
    state = [((3, LANES, DH), f32), ((3, LANES, 2 * DH), f32)]

    early = positions * 7 // 16
    late = positions - early
    kv, *halves = call(
        join_kernel, [((2 * size, DH), bf16) for size in (positions, early, late)]
    )(prefix_keys, prefix_values)
    x0, x1 = [moved(half, xh=1) for half in halves]
    kv_c = moved(kv, c=1)
    q_z = [moved(queries, z=z) for z in FAR]
    row = jnp.arange(ROWS, dtype=jnp.int32)
    allowed = (question_ids[:, None] == question_ids[None, :]) & (row[None, :] <= row[:, None])
    bias = jnp.where(allowed, 0.0, FLOOR).astype(f32)
    def layout(size):
        return [((size, DH), bf16), ((size, 2 * DH), bf16)]

    own_top, own_total, *block = call(own_kernel, own_state + layout(positions))(
        queries, jnp.concatenate([question_keys, question_values]), bias, after(kv, q_z[0])
    )
    top, total, rows, *block = call(
        near_kernel, state + [((4, LANES, DH), bf16)] + layout(positions), flops=1
    )(*q_z, queries, *block, kv_c)
    x0, top = lax.optimization_barrier((x0, top))
    xc0 = moved(x0, c=1)
    own_top, own_total = call(own_more_kernel, own_state, flops=block_flops)(
        after(rows, x0), own_top, own_total, *block
    )
    top, total, *block = call(others_kernel, state + layout(2 * early), flops=1)(
        rows, after(top, own_top), total, x0, xc0
    )

    x1, weight, top = lax.optimization_barrier((x1, out_weight, top))
    xc1 = moved(x1, c=1)
    weight_c = moved(weight, c=1)
    own_top, own_total = call(own_more_kernel, own_state, flops=2 * block_flops)(
        after(rows, x1), own_top, own_total, *block
    )
    p_far, *block = call(far_kernel, [part] + layout(2 * late), flops=1)(
        rows, after(top, own_top), total, x1, xc1
    )
    p_next = call(next_kernel, [part] * 2, flops=4 * block_flops)(
        rows, after(top, p_far), total, *block
    )
    back = [moved(p, z=-z) for p, z in zip((*p_next, p_far), FAR)]
    result, level = call(own_last_kernel, [((DH, LANES), f32), ((8, LANES), f32)], flops=1)(
        after(rows, *p_next), own_top, own_total, *block, back[2]
    )
    (att,) = call(
        merge_kernel, [((ROWS, GROUP * DH), bf16)], in_specs=[smem] + [vmem] * 4
    )(live_rows, result, level, *back[:2])

    att_x = moved(att, xh=1)
    held = [att] + [moved(att, z=z) for z in (2, 1, 3)]
    held += [att_x, moved(held[1], xh=1), moved(att_x, z=1), moved(held[3], xh=1)]
    width = out_weight.shape[1]
    (terms,) = call(
        project_kernel,
        [((8, ROWS, CORE * width), bf16)],
        [pltpu.VMEM((8 * ROWS, GROUP * DH), bf16)],
        in_specs=[smem] + [vmem] * 10,
    )(index.reshape(1), *held, out_weight, weight_c)
    gathered = lax.all_to_all(terms, "head", 0, 0, tiled=True)
    mine, other = call(
        functools.partial(sum_kernel, width=width),
        [((ROWS, width), bf16), ((ROWS, width), bf16)],
    )(gathered)
    theirs = moved(other, c=1)
    (projected,) = call(
        place_kernel, [((CORE * ROWS, width), bf16)], in_specs=[smem, vmem, vmem]
    )(core.reshape(1), mine, theirs)
    return projected


def solution(mesh):
    return jax.shard_map(
        shards,
        mesh=mesh,
        in_specs=(
            P("blk", "head"),
            P("blk", "head"),
            P("blk", "head"),
            P("blk"),
            P("blk"),
            P("blk", "head"),
            P("blk", "head"),
            P("head", "blk"),
        ),
        out_specs=P("head", "blk"),
        check_vma=False,
    )
```
